32 devices in a mesh: dp: 16 (over z, y, core), tensor: 2 (over x).
Axes of the slice: x: 2, y: 2, z: 4, core: 2. Of those that a mesh axis runs over, the one named last changes fastest.
Arguments:
- tokens: bfloat16 [4096, 1024], P('dp'), may hold values from -24 to 24
- segments: int32 [16, 256], P('dp'), may hold values from 0 to 3, never falling along the last dimension, each value on 1 to 128 neighbouring positions
- positions: int32 [16, 256], P('dp'), may hold values from 0 to 1023
- attn_gain: float32 [1024], replicated, may hold values from 0.5 to 1.5
- w_query: bfloat16 [1024, 2048], P(None, 'tensor'), may hold values from -0.1875 to 0.1875
- key_weight: bfloat16 [1024, 1024], P(None, 'tensor'), may hold values from -0.1875 to 0.1875
- value_weight: bfloat16 [1024, 1024], P(None, 'tensor'), may hold values from -0.1875 to 0.1875
- query_gain: float32 [128], replicated, may hold values from 0.5 to 1.5
- key_gain: float32 [128], replicated, may hold values from 0.5 to 1.5
- w_out: bfloat16 [2048, 1024], P('tensor'), may hold values from -0.75 to 0.75
- ffn_gain: float32 [1024], replicated, may hold values from 0.5 to 1.5
- w_gate: bfloat16 [1024, 3072], P(None, 'tensor'), may hold values from -0.1875 to 0.1875
- w_up: bfloat16 [1024, 3072], P(None, 'tensor'), may hold values from -0.1875 to 0.1875
- w_down: bfloat16 [3072, 1024], P('tensor'), may hold values from -0.109375 to 0.109375
- cotangent: bfloat16 [4096, 1024], P('dp'), may hold values from -6 to 6
Outputs:
- mixed: bfloat16 [4096, 1024], P('dp')
- tokens_grad: bfloat16 [4096, 1024], P('dp')
- attn_gain_grad: float32 [1024], replicated
- w_query_grad: float32 [1024, 2048], P(None, 'tensor')
- w_key_grad: float32 [1024, 1024], P(None, 'tensor')
- w_value_grad: float32 [1024, 1024], P(None, 'tensor')
- query_gain_grad: float32 [128], replicated
- key_gain_grad: float32 [128], replicated
- w_out_grad: float32 [2048, 1024], P('tensor')
- ffn_gain_grad: float32 [1024], replicated
- w_gate_grad: float32 [1024, 3072], P(None, 'tensor')
- w_up_grad: float32 [1024, 3072], P(None, 'tensor')
- w_down_grad: float32 [3072, 1024], P('tensor')
The draws below stay inside these ranges and needn't reach their ends.
Inputs may be any that keep to these rules, and one draw needn't show every extreme that they name: `segments`: within each packed sequence segment numbers never fall; each document has 1 to 128 tokens and one has exactly that many.
All inputs are finite; a program needn't handle non-finite values.
Results may differ from the reference program's by a relative error of at most 0.013.
Values sent between devices are 32-bit elements; how exact they have to be, the bound alone decides.
A program may use at most 192 MiB of HBM per device.

```python
import math
import jax
import jax.numpy as jnp
import numpy as np
from jax import lax

MODEL_WIDTH = 1024
QUERY_HEAD_COUNT = 16
KEY_VALUE_HEADS = 8
HEAD_SIZE = 128
FF = 3072
TOK_DEV = 256
SEQS = 16
TOKENS = 4096


def draw_tokens(key, part):
    key = jax.random.fold_in(key, 11)
    first_key, second_key, third_key = jax.random.split(key, 3)
    base_rows = jnp.clip(jax.random.normal(first_key, (TOKENS, MODEL_WIDTH), jnp.float32), -4.0, 4.0)
    row_scale = jnp.exp(jax.random.uniform(second_key, (TOKENS, 1), jnp.float32, math.log(0.5), math.log(2.0)))
    column_scale = jnp.exp(jax.random.uniform(third_key, (1, MODEL_WIDTH), jnp.float32, math.log(0.3), math.log(3.0)))
    return (base_rows * row_scale * column_scale).astype(jnp.bfloat16)


def with_ends(values, stream_key, low, largest):
    extent = values.shape
    index_at = [jax.random.randint(jax.random.fold_in(stream_key, axis), (), 0, extent[axis]) for axis in range(len(extent))]
    values = values.at[tuple(index_at)].set(low)
    longest = extent.index(max(extent))
    index_at[longest] = (index_at[longest] + 1) % extent[longest]
    return values.at[tuple(index_at)].set(largest)


def steps_of(own_key, shape, cuts, smallest, high):
    gain = 1.0
    for position, shards_of in cuts:
        steps = jax.random.uniform(jax.random.fold_in(jax.random.fold_in(own_key, 6), position), (shards_of,), jnp.float32, smallest / len(cuts), high / len(cuts))
        gain = gain * jnp.repeat(jnp.exp(steps), shape[position] // shards_of).reshape((-1,) + (1,) * (len(shape) - 1 - position))
    return gain


def length_profile(number_of, total, most, lean):
    weights = [(1 << 20) // math.isqrt(standing ** lean) + 1 for standing in range(2, number_of + 1)]
    surplus, given = total - most - (number_of - 1), [1] * (number_of - 1)
    while surplus > 0:
        candidates = [i for i in range(number_of - 1) if given[i] < most]
        pool, left = sum([weights[i] for i in candidates]), surplus
        for i in candidates:
            addition = min(most - given[i], max(1, left * weights[i] // pool), surplus)
            given[i] = given[i] + addition
            surplus = surplus - addition
    return np.array([most] + given)


def uneven(key, number_of, total, limit, skew):
    if number_of == 2:
        one = jax.random.randint(key, (), max(1, total - limit), min(limit, total - 1) + 1)
        return jnp.stack([one, total - one])
    tallies = jnp.asarray(length_profile(number_of, total, limit, skew), jnp.int32)
    pairs = (number_of - 1) // 2
    source_of, receiver = tallies[1:1 + 2 * pairs:2], tallies[2:2 + 2 * pairs:2]
    slack = jnp.minimum(source_of - 1, limit - receiver)
    shifted = jax.random.randint(jax.random.fold_in(key, 1), (pairs,), 0, 1 << 20) % (slack + 1)
    tallies = tallies.at[1:1 + 2 * pairs:2].set(source_of - shifted).at[2:2 + 2 * pairs:2].set(receiver + shifted)
    return tallies[jax.random.permutation(jax.random.fold_in(key, 2), number_of)]


def noise(stream_key, extent, deviation, reach, shards=(), kind=jnp.bfloat16):
    array = deviation * jax.random.normal(stream_key, extent, jnp.float32)
    if shards:
        array = array * steps_of(stream_key, extent, shards, -0.22, 0.18)
    return jnp.clip(array, -reach, reach).astype(kind)


def setup_inputs(seed: int = 0) -> dict:
    seeds = jax.random.split(jax.random.key(seed), 16)
    return {
        "tokens": draw_tokens(jax.random.fold_in(seeds[15], 71), 0),
        "segments": jax.vmap(lambda own: jnp.searchsorted(jnp.cumsum(uneven(own, 4, TOK_DEV, TOK_DEV // 2, 0)), jnp.arange(TOK_DEV), side="right"))(jax.random.split(seeds[1], SEQS)).reshape((SEQS, TOK_DEV)).astype(jnp.int32),
        "positions": with_ends(jax.random.randint(seeds[2], (SEQS, TOK_DEV), 0, 1024), jax.random.fold_in(seeds[2], 1), 0, 1023).astype(jnp.int32),
        "attn_gain": jnp.clip(1.0 + 0.1 * jax.random.normal(seeds[3], (MODEL_WIDTH,), jnp.float32), 0.5, 1.5),
        "w_query": noise(seeds[4], (MODEL_WIDTH, QUERY_HEAD_COUNT * HEAD_SIZE), MODEL_WIDTH ** -0.5, 0.1875, ((1, 2),)),
        "key_weight": noise(seeds[5], (MODEL_WIDTH, KEY_VALUE_HEADS * HEAD_SIZE), MODEL_WIDTH ** -0.5, 0.1875, ((1, 2),)),
        "value_weight": noise(seeds[6], (MODEL_WIDTH, KEY_VALUE_HEADS * HEAD_SIZE), MODEL_WIDTH ** -0.5, 0.1875, ((1, 2),)),
        "query_gain": jnp.clip(1.0 + 0.1 * jax.random.normal(seeds[7], (HEAD_SIZE,), jnp.float32), 0.5, 1.5),
        "key_gain": jnp.clip(1.0 + 0.1 * jax.random.normal(seeds[8], (HEAD_SIZE,), jnp.float32), 0.5, 1.5),
        "w_out": noise(seeds[9], (QUERY_HEAD_COUNT * HEAD_SIZE, MODEL_WIDTH), (QUERY_HEAD_COUNT * HEAD_SIZE // 32) ** -0.5, 0.75, ((0, 2),)),
        "ffn_gain": jnp.clip(1.0 + 0.1 * jax.random.normal(seeds[10], (MODEL_WIDTH,), jnp.float32), 0.5, 1.5),
        "w_gate": noise(seeds[11], (MODEL_WIDTH, FF), MODEL_WIDTH ** -0.5, 0.1875, ((1, 2),)),
        "w_up": noise(seeds[12], (MODEL_WIDTH, FF), MODEL_WIDTH ** -0.5, 0.1875, ((1, 2),)),
        "w_down": noise(seeds[13], (FF, MODEL_WIDTH), FF ** -0.5, 0.109375, ((0, 2),)),
        "cotangent": noise(seeds[14], (TOKENS, MODEL_WIDTH), 1.0, 6.0, ((0, 16),)),
    }


EPS = 1e-06
THETA = 1000000.0

@jax.custom_vjp
def lower_precision(v):
    return lax.optimization_barrier(v.astype(jnp.bfloat16)).astype(jnp.float32)

@jax.custom_vjp
def lower_precision_backward(v):
    return v

def low_keep(v):
    return (lower_precision(v), None)

def low_pass(kept, grad):
    return (grad,)

def back_keep(v):
    return (v, None)

def back_low(kept, grad):
    return (lower_precision(grad),)
lower_precision.defvjp(low_keep, low_pass)
lower_precision_backward.defvjp(back_keep, back_low)

def dense_matmul(leading, trailing):
    return jnp.matmul(leading, trailing, precision=lax.Precision.HIGHEST)

def rms_norm(values, scale_gain):
    return values * lax.rsqrt(lax.optimization_barrier(jnp.mean(values * values, axis=-1, keepdims=True)) + EPS) * scale_gain

def rotate(values, places):
    head_width = values.shape[-1]
    half_width = head_width // 2
    inverse = THETA ** (-(jnp.arange(half_width, dtype=jnp.float32) * 2.0 / head_width))
    angles = places.astype(jnp.float32)[..., None] * inverse
    cosine = jnp.concatenate([jnp.cos(angles), jnp.cos(angles)], axis=-1)[..., None, :]
    sine_table = jnp.concatenate([jnp.sin(angles), jnp.sin(angles)], axis=-1)[..., None, :]
    turned = jnp.concatenate([-values[..., half_width:], values[..., :half_width]], axis=-1)
    return values * cosine + turned * sine_table

def layer(params, inputs, segment_rows, places):
    attn_gain, w_query, key_weight, value_weight, query_gain, key_gain, w_out, ffn_gain, w_gate, w_up, w_down = params
    batch_rows_count, sequence_length = (inputs.shape[0], inputs.shape[1])
    attention_input = lower_precision(rms_norm(inputs, attn_gain))
    query_lin = lower_precision_backward(dense_matmul(attention_input, w_query)).reshape(batch_rows_count, sequence_length, QUERY_HEAD_COUNT, HEAD_SIZE)
    queries = lower_precision(rotate(rms_norm(query_lin, query_gain), places))
    key_linear = lower_precision_backward(dense_matmul(attention_input, key_weight)).reshape(batch_rows_count, sequence_length, KEY_VALUE_HEADS, HEAD_SIZE)
    key_row_block = lower_precision(rotate(rms_norm(key_linear, key_gain), places))
    value_row_block = lower_precision(lower_precision_backward(dense_matmul(attention_input, value_weight))).reshape(batch_rows_count, sequence_length, KEY_VALUE_HEADS, HEAD_SIZE)
    key_row_block = jnp.repeat(key_row_block, QUERY_HEAD_COUNT // KEY_VALUE_HEADS, axis=2)
    value_row_block = jnp.repeat(value_row_block, QUERY_HEAD_COUNT // KEY_VALUE_HEADS, axis=2)
    score_rows = jnp.einsum('bqhd,bkhd->bhqk', queries, key_row_block, precision=lax.Precision.HIGHEST) * (1.0 / math.sqrt(HEAD_SIZE))
    score_rows = lower_precision_backward(score_rows)
    order_rows = jnp.arange(sequence_length)
    allowed = (segment_rows[:, :, None] == segment_rows[:, None, :]) & (order_rows[:, None] >= order_rows[None, :])[None]
    score_rows = jnp.where(allowed[:, None], score_rows, -1e+30)
    weights = lower_precision(jax.nn.softmax(score_rows, axis=-1))
    context = jnp.einsum('bhqk,bkhd->bqhd', weights, value_row_block, precision=lax.Precision.HIGHEST)
    context = lower_precision(lower_precision_backward(context.reshape(batch_rows_count, sequence_length, QUERY_HEAD_COUNT * HEAD_SIZE)))
    middle = inputs + lower_precision_backward(dense_matmul(context, w_out))
    ffn_in = lower_precision(rms_norm(middle, ffn_gain))
    gate_lin = lower_precision_backward(dense_matmul(ffn_in, w_gate))
    up_lin = lower_precision_backward(dense_matmul(ffn_in, w_up))
    hidden = lower_precision(jax.nn.silu(gate_lin) * up_lin)
    return middle + lower_precision_backward(dense_matmul(hidden, w_down))

def reference(tokens, segments, positions, attn_gain, w_query, key_weight, value_weight, query_gain, key_gain, w_out, ffn_gain, w_gate, w_up, w_down, cotangent):
    params = (attn_gain.astype(jnp.float32), w_query.astype(jnp.float32), key_weight.astype(jnp.float32), value_weight.astype(jnp.float32), query_gain.astype(jnp.float32), key_gain.astype(jnp.float32), w_out.astype(jnp.float32), ffn_gain.astype(jnp.float32), w_gate.astype(jnp.float32), w_up.astype(jnp.float32), w_down.astype(jnp.float32))
    group_size = math.gcd(SEQS, max(1, 4096 // TOK_DEV))
    count_groups = SEQS // group_size
    inputs = tokens.astype(jnp.float32).reshape(count_groups, group_size, TOK_DEV, MODEL_WIDTH)
    grads_in = cotangent.astype(jnp.float32).reshape(count_groups, group_size, TOK_DEV, MODEL_WIDTH)
    segment_rows = segments.reshape(count_groups, group_size, TOK_DEV)
    place_rows = positions.reshape(count_groups, group_size, TOK_DEV)

    def run_group(totals, pieces):
        group_inputs, group_segments, group_places, group_cot = pieces
        result, pullback = jax.vjp(lambda weights_all, rows_in: layer(weights_all, rows_in, group_segments, group_places), params, group_inputs)
        param_grads, input_grad = pullback(group_cot)
        totals = jax.tree.map(lambda left_sum, right_sum: left_sum + right_sum, totals, param_grads)
        return (totals, (result, input_grad))
    start = jax.tree.map(jnp.zeros_like, params)
    totals, (results, input_grads) = lax.scan(run_group, start, (inputs, segment_rows, place_rows, grads_in))
    return (results.reshape(TOKENS, MODEL_WIDTH).astype(jnp.bfloat16), input_grads.reshape(TOKENS, MODEL_WIDTH).astype(jnp.bfloat16), totals[0], totals[1], totals[2], totals[3], totals[4], totals[5], totals[6], totals[7], totals[8], totals[9], totals[10])
```

```python
import functools
import math

import jax
import jax.numpy as jnp
from jax import lax
from jax.experimental import pallas as pl
from jax.experimental.pallas import tpu as pltpu
from jax.sharding import PartitionSpec as P

EPS = 1e-06
THETA = 1000000.0
F32 = jnp.float32
BF16 = jnp.bfloat16
VMEM_BYTES = 56 * 2**20
GROUP = 16


def norm_factor(values):
    return lax.rsqrt(jnp.mean(values * values, axis=-1, keepdims=True) + EPS)


def norm_grad(grad_out, unit_rows, factor, scale_gain):
    scaled = grad_out * scale_gain
    return factor * (scaled - unit_rows * jnp.mean(scaled * unit_rows, axis=-1, keepdims=True))


def rows_dot(leading, trailing):
    return jnp.dot(leading, trailing, preferred_element_type=F32)


def across_rows(leading, trailing):
    return lax.dot_general(
        leading, trailing, (((0,), (0,)), ((), ())), preferred_element_type=F32
    )


def against_rows(leading, trailing):
    return lax.dot_general(
        leading, trailing, (((1,), (1,)), ((), ())), preferred_element_type=F32
    )


def call(kernel, outs, *arrays, flops=0, **more):
    traffic = sum(a.size * a.dtype.itemsize for a in arrays)
    traffic += sum(math.prod(o.shape) * o.dtype.itemsize for o in outs)
    return pl.pallas_call(
        kernel,
        out_shape=outs,
        compiler_params=pltpu.CompilerParams(vmem_limit_bytes=VMEM_BYTES),
        cost_estimate=pl.CostEstimate(flops=int(flops), bytes_accessed=traffic, transcendentals=0),
        **more,
    )(*arrays)


def shaped(rows, columns, kind=F32):
    return jax.ShapeDtypeStruct((rows, columns), kind)


def attention_forward_kernel(
    scale, tokens, mask, cosine, sine, gain, wq, wk, wv, qgain, kgain, wo,
    part, attn_in, q_lin, k_lin, q_out, k_out, v_out, probs, context,
):
    width = qgain.shape[1]
    resid = tokens[...].astype(F32)
    normed = (resid * norm_factor(resid) * gain[...]).astype(BF16)
    attn_in[...] = normed.astype(F32)
    q_lin[...] = rows_dot(normed, wq[...])
    k_lin[...] = rows_dot(normed, wk[...])
    v_out[...] = rows_dot(normed, wv[...]).astype(BF16)

    def turned(lin, head_gain):
        normed_head = lin * norm_factor(lin) * head_gain[...]
        swapped = pltpu.roll(normed_head, width // 2, 1)
        return (normed_head * cosine[...] + swapped * sine[...]).astype(BF16)

    kv_heads = wk.shape[1] // width
    group = wq.shape[1] // wk.shape[1]
    for kv in range(kv_heads):
        kv_cols = slice(kv * width, (kv + 1) * width)
        keys = turned(k_lin[:, kv_cols], kgain)
        k_out[:, kv_cols] = keys
        values = v_out[:, kv_cols]
        for member in range(group):
            head = kv * group + member
            cols = slice(head * width, (head + 1) * width)
            queries = turned(q_lin[:, cols], qgain)
            q_out[:, cols] = queries
            scores = jnp.where(mask[...] > 0, against_rows(queries, keys) * scale, -1e30)
            raised = jnp.exp(scores - jnp.max(scores, axis=-1, keepdims=True))
            prob = raised / jnp.sum(raised, axis=-1, keepdims=True)
            probs[head] = prob
            context[:, cols] = rows_dot(prob.astype(BF16), values).astype(BF16).astype(F32)
    part[...] = rows_dot(context[...].astype(BF16), wo[...])


def ffn_kernel(
    tokens, part, theirs, gain, cot, wg, wu, wd,
    middle, ffn_in, grad_part, out_part, low_in,
):
    @pl.when(pl.program_id(0) == 0)
    def _():
        value = tokens[...].astype(F32) + (part[...] + theirs[...])
        middle[...] = value
        low = (value * norm_factor(value) * gain[...]).astype(BF16)
        low_in[...] = low
        ffn_in[...] = low.astype(F32)
        grad_part[...] = jnp.zeros_like(grad_part)
        out_part[...] = jnp.zeros_like(out_part)

    hidden, gate_grad, up_grad = ffn_middle(low_in[...], cot[...], wg[...], wu[...], wd[...])
    grad_part[...] += against_rows(gate_grad, wg[...]) + against_rows(up_grad, wu[...])
    out_part[...] += rows_dot(hidden, wd[...])


def ffn_middle(low_in, cot, wg, wu, wd):
    gate = rows_dot(low_in, wg)
    up = rows_dot(low_in, wu)
    sig = jax.nn.sigmoid(gate)
    silu = gate * sig
    hidden = (silu * up).astype(BF16)
    hidden_grad = against_rows(cot, wd)
    up_grad = (hidden_grad * silu).astype(BF16)
    gate_grad = (hidden_grad * up * sig * (1.0 + gate * (1.0 - sig))).astype(BF16)
    return hidden, gate_grad, up_grad


def ffn_norm_back_kernel(grad_part, theirs, middle, gain, cot, middle_grad, branch, gain_grad):
    grad = grad_part[...] + theirs[...]
    value = middle[...]
    factor = norm_factor(value)
    unit = value * factor
    total = cot[...].astype(F32) + norm_grad(grad, unit, factor, gain[...])
    middle_grad[...] = total
    branch[...] = total.astype(BF16).astype(F32)
    gain_grad[...] = jnp.sum(grad * unit, axis=0, keepdims=True)


def attention_backward_kernel(
    scale, branch, wo, q_lin, k_lin, q_in, k_in, v_in, probs, cosine, sine, qgain, kgain, wq, wk, wv,
    low, part, qgain_grad, kgain_grad, context_grad,
):
    width = qgain.shape[1]
    q_cols, k_cols = wq.shape[1], wk.shape[1]
    context_grad[...] = against_rows(branch[...].astype(BF16), wo[...]).astype(BF16)

    def back(grad, lin, head_gain):
        turned = grad * cosine[...] - pltpu.roll(grad, width // 2, 1) * sine[...]
        factor = norm_factor(lin)
        unit = lin * factor
        return (
            norm_grad(turned, unit, factor, head_gain[...]).astype(BF16),
            jnp.sum(turned * unit, axis=0, keepdims=True),
        )

    kv_heads = k_cols // width
    group = q_cols // k_cols
    q_total = jnp.zeros((1, width), F32)
    k_total = jnp.zeros((1, width), F32)
    for kv in range(kv_heads):
        kv_cols = slice(kv * width, (kv + 1) * width)
        keys, values = k_in[:, kv_cols], v_in[:, kv_cols]
        keys_grad = values_grad = 0.0
        for member in range(group):
            head = kv * group + member
            cols = slice(head * width, (head + 1) * width)
            grad = context_grad[:, cols]
            prob = probs[head]
            prob_grad = against_rows(grad, values)
            values_grad += across_rows(prob.astype(BF16), grad)
            inner = jnp.sum(prob * prob_grad, axis=-1, keepdims=True)
            score_grad = (prob * (prob_grad - inner)).astype(BF16)
            queries_grad = rows_dot(score_grad, keys) * scale
            keys_grad += across_rows(score_grad, q_in[:, cols])
            head_low, head_total = back(queries_grad, q_lin[:, cols], qgain)
            low[:, cols] = head_low.astype(F32)
            q_total += head_total
        head_low, head_total = back(keys_grad * scale, k_lin[:, kv_cols], kgain)
        k_total += head_total
        low[:, slice(q_cols + kv * width, q_cols + (kv + 1) * width)] = head_low.astype(F32)
        low[:, slice(q_cols + k_cols + kv * width, q_cols + k_cols + (kv + 1) * width)] = (
            values_grad.astype(BF16).astype(F32)
        )
    qgain_grad[...] = q_total
    kgain_grad[...] = k_total
    part[...] = (
        against_rows(low[:, :q_cols].astype(BF16), wq[...])
        + against_rows(low[:, q_cols : q_cols + k_cols].astype(BF16), wk[...])
        + against_rows(low[:, q_cols + k_cols :].astype(BF16), wv[...])
    )


def token_grad_kernel(part, theirs, tokens, gain, middle_grad, tokens_grad, gain_grad):
    grad = part[...] + theirs[...]
    value = tokens[...].astype(F32)
    factor = norm_factor(value)
    unit = value * factor
    tokens_grad[...] = (middle_grad[...] + norm_grad(grad, unit, factor, gain[...])).astype(BF16)
    gain_grad[...] = jnp.sum(grad * unit, axis=0, keepdims=True)


def pair_grad_kernel(left, left_theirs, right, right_theirs, out, left_low, right_low):
    rows = left.shape[0]
    left_low[:rows] = left[...].astype(BF16)
    left_low[rows:] = left_theirs[...].astype(BF16)
    right_low[:rows] = right[...].astype(BF16)
    right_low[rows:] = right_theirs[...].astype(BF16)
    out[...] = across_rows(left_low[...], right_low[...])


def pair_grad(left, left_theirs, right, right_theirs):
    rows, inner, columns = left.shape[0], left.shape[1], right.shape[1]
    (out,) = call(
        pair_grad_kernel,
        [shaped(inner, columns)],
        left, left_theirs, right, right_theirs,
        flops=4 * rows * inner * columns,
        scratch_shapes=[pltpu.VMEM((2 * rows, inner), BF16), pltpu.VMEM((2 * rows, columns), BF16)],
    )
    return out


def ffn_grad_kernel(blocks, first, core, *refs):
    del core
    ffn_blocks, cot_blocks = refs[:blocks], refs[blocks : 2 * blocks]
    rest = refs[2 * blocks :]
    wg, wu, wd = rest[:3]
    rest = rest[3:]
    if not first:
        old, rest = rest[:3], rest[3:]
    gate_sum, up_sum, down_sum, ffn_low, ffn_turned, cot_low = rest

    @pl.when(pl.program_id(0) == 0)
    def _():
        at = 0
        for ffn_block, cot_block in zip(ffn_blocks, cot_blocks):
            rows = ffn_block.shape[0]
            low = ffn_block[...].astype(BF16)
            ffn_low[at : at + rows] = low
            ffn_turned[:, at : at + rows] = low.T
            cot_low[at : at + rows] = cot_block[...].astype(BF16)
            at += rows

    hidden, gate_grad, up_grad = ffn_middle(ffn_low[...], cot_low[...], wg[...], wu[...], wd[...])
    down = across_rows(hidden, cot_low[...])
    gate = rows_dot(ffn_turned[...], gate_grad)
    up = rows_dot(ffn_turned[...], up_grad)
    if first:
        gate_sum[...], up_sum[...], down_sum[...] = gate, up, down
    else:
        gate_sum[...] = old[0][...] + gate
        up_sum[...] = old[1][...] + up
        down_sum[...] = old[2][...] + down


def ffn_grads(core, ffn_blocks, cot_blocks, wg, wu, wd, sums, chunk=256):
    blocks = len(ffn_blocks)
    rows = sum(b.shape[0] for b in ffn_blocks)
    width, units = wg.shape[0], wg.shape[1] // 2
    chunk = math.gcd(chunk, units)
    steps = units // chunk
    whole = [pl.BlockSpec(b.shape, lambda j, c: (0, 0), pipeline_mode=pl.Buffered(1)) for b in (*ffn_blocks, *cot_blocks)]
    columns = pl.BlockSpec((width, chunk), lambda j, c: (0, c[0] * steps + j))
    down_rows = pl.BlockSpec((chunk, width), lambda j, c: (c[0] * steps + j, 0))
    sum_columns = pl.BlockSpec((width, chunk), lambda j, c: (0, j))
    sum_rows = pl.BlockSpec((chunk, width), lambda j, c: (j, 0))
    sum_specs = [sum_columns, sum_columns, sum_rows]
    first = sums is None
    arrays = [*ffn_blocks, *cot_blocks, wg, wu, wd, *(sums or ())]
    aliases = {} if first else {1 + 2 * blocks + 3 + i: i for i in range(3)}
    return call(
        functools.partial(ffn_grad_kernel, blocks, first),
        [shaped(width, units), shaped(width, units), shaped(units, width)],
        core.reshape(1), *arrays,
        flops=12 * rows * width * units,
        grid_spec=pltpu.PrefetchScalarGridSpec(
            num_scalar_prefetch=1,
            grid=(steps,),
            in_specs=whole + [columns, columns, down_rows] + ([] if first else sum_specs),
            out_specs=sum_specs,
            scratch_shapes=[
                pltpu.VMEM((rows, width), BF16),
                pltpu.VMEM((width, rows), BF16),
                pltpu.VMEM((rows, width), BF16),
            ],
        ),
        input_output_aliases=aliases,
    )


class Ring:
    def __init__(self, dp_size):
        self.dp_size = dp_size
        self.group = math.gcd(GROUP, dp_size)
        n = self.chips = self.group // 2
        self.half = n // 2
        length = n // 2
        order = [2 * step for step in range(length)]
        order += [2 * step + 1 for step in reversed(range(length))]
        self.place = [order.index(chip) for chip in range(n)]
        self.forward = [
            (base + order[i] * 2 + c, base + order[(i + 1) % n] * 2 + c)
            for base in range(0, dp_size, self.group)
            for i in range(n)
            for c in range(2)
        ]
        self.backward = [(b, a) for a, b in self.forward]
        self.sibling = [(d, d ^ 1) for d in range(dp_size)]

    def position(self):
        chip = lax.axis_index("dp") % self.group // 2
        return jnp.asarray(self.place, jnp.int32)[chip]

    def over_groups(self, values):
        step = self.group
        while step < self.dp_size:
            values = values + send(values, [(d, d ^ step) for d in range(self.dp_size)])
            step *= 2
        return values


def send(values, pairs):
    return lax.ppermute(values, "dp", pairs)


def across(values):
    return lax.ppermute(values, "tensor", [(0, 1), (1, 0)])


def gather_blocks(ring, block):
    up, down = block, block
    rounds = [[block]]
    for _ in range(ring.half - 1):
        up, down = send(up, ring.forward), send(down, ring.backward)
        rounds.append([up, down])
    middle = block.shape[0] // 2
    rounds[0] += [send(up[:middle], ring.forward), send(down[middle:], ring.backward)]
    return rounds[1:] + rounds[:1]


def piece_of(values, index, count):
    rows = values.shape[0] // count
    return lax.dynamic_slice_in_dim(values, index * rows, rows, 0)


def sum_scatter(ring, values, position):
    n, half = ring.chips, ring.half
    rows = values.shape[0] // n
    middle = rows // 2
    far = piece_of(values, (position + half) % n, n)
    up = send(far[:middle], ring.forward)
    down = send(far[middle:], ring.backward)
    for step in range(half - 1, 0, -1):
        ahead = piece_of(values, (position + step) % n, n)
        behind = piece_of(values, (position - step + n) % n, n)
        if step == half - 1:
            ahead = jnp.concatenate([ahead[:middle] + up, ahead[middle:]], 0)
            behind = jnp.concatenate([behind[:middle], behind[middle:] + down], 0)
        else:
            ahead, behind = ahead + up, behind + down
        up, down = send(ahead, ring.forward), send(behind, ring.backward)
    return piece_of(values, position, n) + up + down


def gather_rows(ring, piece, position, whole, base):
    n, half = ring.chips, ring.half
    rows = piece.shape[0]
    middle = rows // 2

    def put(whole, values, index, skip=0):
        return lax.dynamic_update_slice_in_dim(whole, values, base + index * rows + skip, 0)

    whole = put(whole, piece, position)
    up, down = piece, piece
    for step in range(1, half):
        up, down = send(up, ring.forward), send(down, ring.backward)
        whole = put(whole, up, (position - step + n) % n)
        whole = put(whole, down, (position + step) % n)
    up, down = send(up[:middle], ring.forward), send(down[middle:], ring.backward)
    far = (position + half) % n
    whole = put(whole, up, far)
    return put(whole, down, far, middle)


def half_columns(values, index):
    width = values.shape[1] // 2
    return lax.dynamic_slice_in_dim(values, index * width, width, 1)


def rotary_tables(places, head_width):
    inverse = THETA ** (-(jnp.arange(head_width // 2, dtype=F32) * 2.0 / head_width))
    angles = places.astype(F32)[:, None] * inverse[None, :]
    cosine, sine = jnp.cos(angles), jnp.sin(angles)
    return jnp.concatenate([cosine, cosine], -1), jnp.concatenate([-sine, sine], -1)


def per_device(
    ring,
    tokens,
    segments,
    positions,
    attn_gain,
    w_query,
    key_weight,
    value_weight,
    query_gain,
    key_gain,
    w_out,
    ffn_gain,
    w_gate,
    w_up,
    w_down,
    cotangent,
):
    rows, width = tokens.shape
    head_width = query_gain.shape[0]
    q_cols, k_cols = w_query.shape[1], key_weight.shape[1]
    heads = q_cols // head_width
    units = w_gate.shape[1]
    scale = 1.0 / math.sqrt(head_width)
    core = lax.axis_index("dp") % 2
    other = 1 - core
    position = ring.position()
    attn_gain, ffn_gain = attn_gain[None], ffn_gain[None]
    query_gain, key_gain = query_gain[None], key_gain[None]

    cot_rounds = gather_blocks(ring, cotangent.astype(F32))

    segment_row = segments[0]
    order_rows = jnp.arange(rows)
    mask = (
        (segment_row[:, None] == segment_row[None, :])
        & (order_rows[:, None] >= order_rows[None, :])
    ).astype(F32)
    cosine, sine = rotary_tables(positions[0], head_width)

    attn_part, attn_in, q_lin, k_lin, queries, keys, values, probs, context = call(
        functools.partial(attention_forward_kernel, scale),
        [
            shaped(rows, width),
            shaped(rows, width),
            shaped(rows, q_cols),
            shaped(rows, k_cols),
            shaped(rows, q_cols, BF16),
            shaped(rows, k_cols, BF16),
            shaped(rows, k_cols, BF16),
            jax.ShapeDtypeStruct((heads, rows, rows), F32),
            shaped(rows, q_cols),
        ],
        tokens, mask, cosine, sine, attn_gain, w_query, key_weight, value_weight,
        query_gain, key_gain, w_out,
        flops=2 * rows * width * (2 * q_cols + 2 * k_cols) + 4 * rows * rows * q_cols,
    )
    attn_theirs = across(attn_part)

    chunk = math.gcd(256, units)
    same = pl.BlockSpec((rows, width), lambda j: (0, 0))
    one_row = pl.BlockSpec((1, width), lambda j: (0, 0))
    columns = pl.BlockSpec((width, chunk), lambda j: (0, j))
    down_rows = pl.BlockSpec((chunk, width), lambda j: (j, 0))
    middle, ffn_in, ffn_in_part, ffn_part = call(
        ffn_kernel,
        [shaped(rows, width)] * 4,
        tokens, attn_part, attn_theirs, ffn_gain, cotangent, w_gate, w_up, w_down,
        flops=12 * rows * width * units,
        grid=(units // chunk,),
        in_specs=[same, same, same, one_row, same, columns, columns, down_rows],
        out_specs=[same] * 4,
        scratch_shapes=[pltpu.VMEM((rows, width), BF16)],
    )
    ffn_in_theirs = across(ffn_in_part)
    ffn_rounds = gather_blocks(ring, ffn_in)

    middle_grad, branch, ffn_gain_grad = call(
        ffn_norm_back_kernel,
        [shaped(rows, width), shaped(rows, width), shaped(1, width)],
        ffn_in_part, ffn_in_theirs, middle, ffn_gain, cotangent,
    )

    context_theirs = send(half_columns(context, other), ring.sibling)
    attn_in_theirs = send(half_columns(attn_in, other), ring.sibling)
    w_out_half = pair_grad(
        half_columns(context, core), context_theirs, branch, send(branch, ring.sibling)
    )
    out_piece = sum_scatter(ring, w_out_half, position)

    low, attn_in_part, query_gain_grad, key_gain_grad = call(
        functools.partial(attention_backward_kernel, scale),
        [
            shaped(rows, q_cols + 2 * k_cols),
            shaped(rows, width),
            shaped(1, head_width),
            shaped(1, head_width),
        ],
        branch, w_out, q_lin, k_lin, queries, keys, values, probs, cosine, sine,
        query_gain, key_gain, w_query, key_weight, value_weight,
        flops=2 * rows * width * (2 * q_cols + 2 * k_cols) + 8 * rows * rows * q_cols,
        scratch_shapes=[pltpu.VMEM((rows, q_cols), BF16)],
    )
    attn_in_grad_theirs = across(attn_in_part)
    qkv_half = pair_grad(
        half_columns(attn_in, core), attn_in_theirs, low, send(low, ring.sibling)
    )
    qkv_piece = sum_scatter(ring, qkv_half, position)

    tokens_grad, attn_gain_grad = call(
        token_grad_kernel,
        [shaped(rows, width, BF16), shaped(1, width)],
        attn_in_part, attn_in_grad_theirs, tokens, attn_gain, middle_grad,
    )
    ffn_part, _ = lax.optimization_barrier((ffn_part, attn_in_grad_theirs))
    mixed = (middle + (ffn_part + across(ffn_part))).astype(BF16)

    sums = None
    for ffn_blocks, cot_blocks in zip(ffn_rounds, cot_rounds):
        ffn_blocks = ffn_blocks + [send(b, ring.sibling) for b in ffn_blocks]
        cot_blocks = cot_blocks + [send(b, ring.sibling) for b in cot_blocks]
        sums = ffn_grads(core, ffn_blocks, cot_blocks, w_gate, w_up, w_down, sums)
    gate_half, up_half, down_half = [ring.over_groups(s) for s in sums]

    def join(mine, axis):
        theirs = send(mine, ring.sibling)
        return jnp.where(
            core == 0,
            jnp.concatenate([mine, theirs], axis),
            jnp.concatenate([theirs, mine], axis),
        )

    w_down_grad = join(down_half, 0)
    w_gate_grad = join(gate_half, 1)
    w_up_grad = join(up_half, 1)

    def spread(piece):
        piece = ring.over_groups(piece)
        count = piece.shape[0] * ring.chips
        half = gather_rows(ring, piece, position, jnp.zeros((count, piece.shape[1]), F32), 0)
        return join(half, 0)

    w_out_grad = spread(out_piece)
    qkv_grad = spread(qkv_piece)
    w_query_grad = qkv_grad[:, :q_cols]
    w_key_grad = qkv_grad[:, q_cols : q_cols + k_cols]
    w_value_grad = qkv_grad[:, q_cols + k_cols :]

    small = jnp.concatenate([query_gain_grad[0], key_gain_grad[0]])
    small = small + across(small)
    gains = lax.psum(jnp.concatenate([attn_gain_grad[0], ffn_gain_grad[0], small]), "dp")
    attn_gain_grad, ffn_gain_grad = gains[:width], gains[width : 2 * width]
    query_gain_grad = gains[2 * width : 2 * width + head_width]
    key_gain_grad = gains[2 * width + head_width :]
    return (
        mixed,
        tokens_grad,
        attn_gain_grad,
        w_query_grad,
        w_key_grad,
        w_value_grad,
        query_gain_grad,
        key_gain_grad,
        w_out_grad,
        ffn_gain_grad,
        w_gate_grad,
        w_up_grad,
        w_down_grad,
    )


def solution(mesh):
    ring = Ring(mesh.shape["dp"])

    def layer(*arrays):
        return per_device(ring, *arrays)

    return jax.shard_map(
        layer,
        mesh=mesh,
        in_specs=(
            P("dp", None),
            P("dp", None),
            P("dp", None),
            P(),
            P(None, "tensor"),
            P(None, "tensor"),
            P(None, "tensor"),
            P(),
            P(),
            P("tensor", None),
            P(),
            P(None, "tensor"),
            P(None, "tensor"),
            P("tensor", None),
            P("dp", None),
        ),
        out_specs=(
            P("dp", None),
            P("dp", None),
            P(),
            P(None, "tensor"),
            P(None, "tensor"),
            P(None, "tensor"),
            P(),
            P(),
            P("tensor", None),
            P(),
            P(None, "tensor"),
            P(None, "tensor"),
            P("tensor", None),
        ),
        check_vma=False,
    )
```

```python
import functools
import math

import jax
import jax.numpy as jnp
from jax import lax
from jax.experimental import pallas as pl
from jax.experimental.pallas import tpu as pltpu
from jax.sharding import PartitionSpec as P

EPS = 1e-06
THETA = 1000000.0
F32 = jnp.float32
BF16 = jnp.bfloat16
MESH = pl.DeviceIdType.MESH
VMEM_BYTES = 62 * 2**20
GROUP = 16
COT, FFN = 0, 1


def norm_factor(values):
    return lax.rsqrt(jnp.mean(values * values, axis=-1, keepdims=True) + EPS)


def norm_grad(grad_out, unit_rows, factor, scale_gain):
    scaled = grad_out * scale_gain
    return factor * (scaled - unit_rows * jnp.mean(scaled * unit_rows, axis=-1, keepdims=True))


def rows_dot(leading, trailing):
    return jnp.dot(leading, trailing, preferred_element_type=F32)


def across_rows(leading, trailing):
    return lax.dot_general(
        leading, trailing, (((0,), (0,)), ((), ())), preferred_element_type=F32
    )


def against_rows(leading, trailing):
    return lax.dot_general(
        leading, trailing, (((1,), (1,)), ((), ())), preferred_element_type=F32
    )


def ffn_middle(low_in, cot, wg, wu, wd):
    gate = rows_dot(low_in, wg)
    up = rows_dot(low_in, wu)
    sig = jax.nn.sigmoid(gate)
    silu = gate * sig
    hidden = (silu * up).astype(BF16)
    hidden_grad = against_rows(cot, wd)
    up_grad = (hidden_grad * silu).astype(BF16)
    gate_grad = (hidden_grad * up * sig * (1.0 + gate * (1.0 - sig))).astype(BF16)
    return hidden, gate_grad, up_grad


def shaped(*shape, kind=F32):
    return jax.ShapeDtypeStruct(shape, kind)


class Sizes:
    def __init__(self, dp_size, tokens, w_query, key_weight, query_gain, w_gate):
        self.rows, self.width = tokens
        self.head_width = query_gain[0]
        self.q_cols, self.k_cols = w_query[1], key_weight[1]
        self.heads, self.kv_heads = self.q_cols // self.head_width, self.k_cols // self.head_width
        self.units = w_gate[1]
        self.all_cols = self.q_cols + 2 * self.k_cols
        self.scale = 1.0 / math.sqrt(self.head_width)
        self.group = math.gcd(GROUP, dp_size)
        self.chips = self.group // 2
        self.half = self.chips // 2
        self.share = self.width // 4
        self.grad_rows = self.width // 2
        self.grad_cols = self.width + self.all_cols
        self.piece = self.grad_rows // self.chips
        self.streams = 2


def layer_kernel(
    sz,
    tokens, cot, mask, cosine, sine, attn_gain, query_gain, key_gain, ffn_gain,
    w_query, key_weight, value_weight, w_out, w_gate, w_up, w_down,
    mixed, tokens_grad, gains,
    attn_grads, gate_grads, up_grads, down_grads, mine, theirs,
    own, part, part_theirs, middle, middle_grad,
    ctx_send, ctx_recv, attn_send, attn_recv, branch, branch_recv, low, low_recv,
    grads, sum_up, sum_down, gain_send, gain_recv, gain_slots, attn_low,
    send_sems, recv_sems, local_sems,
):
    rows, width, head_width = sz.rows, sz.width, sz.head_width
    q_cols, k_cols, units = sz.q_cols, sz.k_cols, sz.units
    n, half, share, piece = sz.chips, sz.half, sz.share, sz.piece
    half_units = units // 2
    mid = rows // 2

    device = lax.axis_index("dp")
    base = device // sz.group * sz.group
    core = device % 2
    chip = device % sz.group // 2
    line = chip % 2
    place = chip // 2 + line * (2 * half - 1 - 2 * (chip // 2))
    side = lax.axis_index("tensor")

    def device_at(position):
        position = position % n
        second = position // half
        return base + (2 * (position + second * (2 * half - 1 - 2 * position)) + second) * 2 + core

    forward = {"dp": device_at(place + 1)}
    backward = {"dp": device_at(place + n - 1)}
    sibling = {"dp": base + chip * 2 + 1 - core}
    across = {"tensor": 1 - side}

    barrier = pltpu.get_barrier_semaphore()
    for neighbour in (forward, backward, sibling, across):
        pl.semaphore_signal(barrier, inc=1, device_id=neighbour, device_id_type=MESH)
    pl.semaphore_wait(barrier, 4)

    book = {}

    def remote(name, src, dst, target):
        book[name] = (len(book), src, dst, target)

    def made(name):
        index, src, dst, target = book[name]
        return pltpu.make_async_remote_copy(
            src_ref=src, dst_ref=dst, send_sem=send_sems.at[index], recv_sem=recv_sems.at[index],
            device_id=target, device_id_type=MESH,
        )

    def start(*names):
        for name in names:
            made(name).start()

    def arrived(*names):
        for name in names:
            made(name).wait_recv()

    def cols(first, count):
        return pl.ds(pl.multiple_of(first, 128), count)

    def piece_rows(index, first=0, count=piece, base_row=0):
        return pl.ds(pl.multiple_of(base_row + index % n * piece + first, 8), count)

    window = cols(side * share, width - share)
    shared = cols(side * (width - share), share)
    slots = 2 * half
    up_slot = lambda h: 2 * h - 1
    down_slot = lambda h: 2 * h
    last = slots - 1
    for a in (COT, FFN):
        for h in range(1, half):
            src = own.at[a] if h == 1 else mine.at[a, up_slot(h - 1)]
            remote(("up", a, h), src.at[:, window], mine.at[a, up_slot(h), :, window], forward)
            src = own.at[a] if h == 1 else mine.at[a, down_slot(h - 1)]
            remote(("down", a, h), src.at[:, window], mine.at[a, down_slot(h), :, window], backward)
        remote(
            ("up", a, half), mine.at[a, up_slot(half - 1), pl.ds(0, mid), window],
            mine.at[a, last, pl.ds(0, mid), window], forward,
        )
        remote(
            ("down", a, half), mine.at[a, down_slot(half - 1), pl.ds(mid, mid), window],
            mine.at[a, last, pl.ds(mid, mid), window], backward,
        )
        for s in range(1, slots):
            remote(("x", a, s), mine.at[a, s, :, shared], mine.at[a, s, :, shared], across)
        for s in range(slots):
            remote(("core", a, s), own.at[a] if s == 0 else mine.at[a, s], theirs.at[a, s], sibling)
    for k in range(4):
        remote(("part", k), part.at[k % 3], part_theirs.at[k], across)
    remote("ctx", ctx_send, ctx_recv, sibling)
    remote("attn", attn_send, attn_recv, sibling)
    remote("branch", branch, branch_recv, sibling)
    remote("low", low, low_recv, sibling)
    stream_cols = sz.grad_cols // sz.streams
    small = piece // 2
    for s in range(sz.streams):
        c = pl.ds(s * stream_cols, stream_cols)
        for h in range(1, half + 1):
            size, skip = (small, small) if h == 1 else (piece, 0)
            remote(
                ("su", s, h), grads.at[piece_rows(place + half + 1 - h, 0, size), c],
                sum_up.at[h - 1, pl.ds(0, size), c], forward,
            )
            remote(
                ("sd", s, h), grads.at[piece_rows(place + n - half - 1 + h, skip, size), c],
                sum_down.at[h - 1, pl.ds(0, size), c], backward,
            )
        for h in range(1, half + 1):
            size, skip = (small, small) if h == half else (piece, 0)
            base_row = core * sz.grad_rows
            up_rows = piece_rows(place + n - h + 1, 0, size, base_row)
            down_rows = piece_rows(place + h - 1, skip, size, base_row)
            own_piece = grads.at[piece_rows(place), c]
            remote(
                ("gu", s, h), own_piece if h == 1 else attn_grads.at[up_rows, c],
                attn_grads.at[up_rows, c], forward,
            )
            remote(
                ("gd", s, h), own_piece if h == 1 else attn_grads.at[down_rows, c],
                attn_grads.at[down_rows, c], backward,
            )
            got_up = attn_grads.at[piece_rows(place + n - h, 0, size, base_row), c]
            got_down = attn_grads.at[piece_rows(place + h, skip, size, base_row), c]
            remote(("cu", s, h), got_up, got_up, sibling)
            remote(("cd", s, h), got_down, got_down, sibling)
        own_rows = piece_rows(place, 0, piece, core * sz.grad_rows)
        remote(("cu", s, 0), grads.at[piece_rows(place), c], attn_grads.at[own_rows, c], sibling)
    remote("gains", gain_send, gain_recv, sibling)
    for h in range(1, half + 1):
        slot = gain_slots.at[(place + n - h + 1) % n]
        remote(("vu", h), slot, slot, forward)
        if h < half:
            slot = gain_slots.at[(place + h - 1) % n]
            remote(("vd", h), slot, slot, backward)

    def ring_step(a, h):
        arrived(("up", a, h), ("down", a, h))
        if h < half:
            start(("up", a, h + 1), ("down", a, h + 1))

    def x_start(a, s):
        start(("x", a, s))

    def x_done(a, s):
        arrived(("x", a, s))
        start(("core", a, s))

    def head_norm(lin, gain):
        return lin * norm_factor(lin) * gain[...]

    def turned(lin, gain):
        normed = head_norm(lin, gain)
        swapped = pltpu.roll(normed, head_width // 2, 1)
        return (normed * cosine[...] + swapped * sine[...]).astype(BF16)

    def turned_back(grad, lin, gain):
        back = grad * cosine[...] - pltpu.roll(grad, head_width // 2, 1) * sine[...]
        factor = norm_factor(lin)
        unit = lin * factor
        return (
            norm_grad(back, unit, factor, gain[...]).astype(BF16),
            jnp.sum(back * unit, axis=0, keepdims=True),
        )

    group = q_cols // k_cols
    other_half = lambda count: cols((1 - core) * count, count)
    own_half = lambda count: cols(core * count, count)

    def first_phase(
        wq, wk, wv, wo, wg, wu, wd, q_lin, k_lin, q_low, k_low, v_low, probs, context, ffn_low, hidden,
        context_grad,
    ):
        loads = [
            pltpu.make_async_copy(src, dst, local_sems.at[i])
            for i, (src, dst) in enumerate(
                zip(
                    (w_query, key_weight, value_weight, w_out, w_gate, w_up, w_down),
                    (wq, wk, wv, wo, wg, wu, wd),
                )
            )
        ]
        for load in loads:
            load.start()
        own[COT] = cot[...].astype(F32)
        start(("up", COT, 1), ("down", COT, 1), ("core", COT, 0))

        resid = tokens[...].astype(F32)
        attn_in = (resid * norm_factor(resid) * attn_gain[...]).astype(BF16)
        attn_low[...] = attn_in
        attn_send[...] = attn_low[:, other_half(width // 2)].astype(F32)
        start("attn")
        for load in loads[:3]:
            load.wait()
        q_lin[...] = rows_dot(attn_in, wq[...])
        k_lin[...] = rows_dot(attn_in, wk[...])
        v_low[...] = rows_dot(attn_in, wv[...]).astype(BF16)
        for kv in range(sz.kv_heads):
            kv_at = slice(kv * head_width, (kv + 1) * head_width)
            keys = turned(k_lin[:, kv_at], key_gain)
            k_low[:, kv_at] = keys
            values = v_low[:, kv_at]
            for member in range(group):
                head = kv * group + member
                at = slice(head * head_width, (head + 1) * head_width)
                queries = turned(q_lin[:, at], query_gain)
                q_low[:, at] = queries
                scores = jnp.where(mask[...] > 0, against_rows(queries, keys) * sz.scale, -1e30)
                raised = jnp.exp(scores - jnp.max(scores, axis=-1, keepdims=True))
                prob = raised / jnp.sum(raised, axis=-1, keepdims=True)
                probs[head] = prob
                context[:, at] = rows_dot(prob.astype(BF16), values).astype(BF16)
        loads[3].wait()
        part[0, :rows] = rows_dot(context[...], wo[...])
        part[0, rows:] = jnp.zeros((8, width), F32)
        start(("part", 0))
        ctx_send[...] = context[:, other_half(q_cols // 2)].astype(F32)
        start("ctx")
        for load in loads[4:]:
            load.wait()
        ring_step(COT, 1)

        arrived(("part", 0))
        value = tokens[...].astype(F32) + (part[0, :rows] + part_theirs[0, :rows])
        middle[...] = value
        ffn_low[...] = (value * norm_factor(value) * ffn_gain[...]).astype(BF16)
        own[FFN] = ffn_low[...].astype(F32)
        start(("up", FFN, 1), ("down", FFN, 1), ("core", FFN, 0))
        start(("x", COT, 1), ("x", COT, 2))
        chunks = 3
        size = units // chunks
        for j in range(chunks):
            at = slice(j * size, (j + 1) * size)
            low_hidden, gate_grad, up_grad = ffn_middle(
                ffn_low[...], cot[...], wg[:, at], wu[:, at], wd[at]
            )
            hidden[:, at] = low_hidden
            term = against_rows(gate_grad, wg[:, at]) + against_rows(up_grad, wu[:, at])
            if j == 0:
                part[1, :rows] = term
            else:
                part[1, :rows] += term
        part[1, rows:] = jnp.zeros((8, width), F32)
        start(("part", 1))
        ring_step(COT, 2)
        made(("part", 0)).wait_send()
        part[0, :rows] = rows_dot(hidden[...], wd[...])
        x_done(COT, 1)
        x_done(COT, 2)

        arrived(("part", 1))
        grad = part[1, :rows] + part_theirs[1, :rows]
        value = middle[...]
        factor = norm_factor(value)
        unit = value * factor
        total = cot[...].astype(F32) + norm_grad(grad, unit, factor, ffn_gain[...])
        middle_grad[...] = total
        branch_low = total.astype(BF16)
        branch[...] = branch_low.astype(F32)
        start("branch", ("x", COT, 3), ("x", COT, 4))
        gain_send[1:2, :] = jnp.sum(grad * unit, axis=0, keepdims=True)
        ring_step(FFN, 1)
        start(("x", FFN, 1), ("x", FFN, 2))
        context_grad[...] = against_rows(branch_low, wo[...]).astype(BF16)
        q_total = jnp.zeros((1, head_width), F32)
        k_total = jnp.zeros((1, head_width), F32)
        for kv in range(sz.kv_heads):
            kv_at = slice(kv * head_width, (kv + 1) * head_width)
            keys, values = k_low[:, kv_at], v_low[:, kv_at]
            keys_grad = values_grad = 0.0
            for member in range(group):
                head = kv * group + member
                at = slice(head * head_width, (head + 1) * head_width)
                head_grad = context_grad[:, at]
                prob = probs[head]
                prob_grad = against_rows(head_grad, values)
                values_grad += across_rows(prob.astype(BF16), head_grad)
                inner = jnp.sum(prob * prob_grad, axis=-1, keepdims=True)
                score_grad = (prob * (prob_grad - inner)).astype(BF16)
                queries_grad = rows_dot(score_grad, keys) * sz.scale
                keys_grad += across_rows(score_grad, q_low[:, at])
                head_low, head_total = turned_back(queries_grad, q_lin[:, at], query_gain)
                low[:, at] = head_low.astype(F32)
                q_total += head_total
            head_low, head_total = turned_back(keys_grad * sz.scale, k_lin[:, kv_at], key_gain)
            k_total += head_total
            low[:, q_cols + kv * head_width : q_cols + (kv + 1) * head_width] = head_low.astype(F32)
            at = q_cols + k_cols + kv * head_width
            low[:, at : at + head_width] = values_grad.astype(BF16).astype(F32)
        start("low")
        ring_step(COT, 3)
        arrived("ctx", "branch")
        grads[:, :width] = across_rows(
            context[:, own_half(q_cols // 2)], branch[...].astype(BF16)
        ) + across_rows(ctx_recv[...].astype(BF16), branch_recv[...].astype(BF16))
        arrived("attn", "low")
        grads[:, width:] = across_rows(
            attn_low[:, own_half(width // 2)], low[...].astype(BF16)
        ) + across_rows(attn_recv[...].astype(BF16), low_recv[...].astype(BF16))
        for s in range(sz.streams):
            start(("su", s, 1), ("sd", s, 1))
        part[2, :rows] = (
            against_rows(low[:, :q_cols].astype(BF16), wq[...])
            + against_rows(low[:, q_cols : q_cols + k_cols].astype(BF16), wk[...])
            + against_rows(low[:, q_cols + k_cols :].astype(BF16), wv[...])
        )
        part[2, rows:] = jnp.zeros((8, width), F32)
        part[2, rows : rows + 1, :head_width] = q_total
        part[2, rows : rows + 1, head_width : 2 * head_width] = k_total
        x_done(COT, 3)
        x_done(COT, 4)
        start(("x", COT, 5), ("x", COT, 6))

    pl.run_scoped(
        first_phase,
        pltpu.VMEM(w_query.shape, BF16),
        pltpu.VMEM(key_weight.shape, BF16),
        pltpu.VMEM(value_weight.shape, BF16),
        pltpu.VMEM(w_out.shape, BF16),
        pltpu.VMEM(w_gate.shape, BF16),
        pltpu.VMEM(w_up.shape, BF16),
        pltpu.VMEM(w_down.shape, BF16),
        pltpu.VMEM((rows, q_cols), F32),
        pltpu.VMEM((rows, k_cols), F32),
        pltpu.VMEM((rows, q_cols), BF16),
        pltpu.VMEM((rows, k_cols), BF16),
        pltpu.VMEM((rows, k_cols), BF16),
        pltpu.VMEM((sz.heads, rows, rows), F32),
        pltpu.VMEM((rows, q_cols), BF16),
        pltpu.VMEM((rows, width), BF16),
        pltpu.VMEM((rows, units), BF16),
        pltpu.VMEM((rows, q_cols), BF16),
    )


    def stream(s):
        return pl.ds(s * stream_cols, stream_cols)

    def sum_step(s, h):
        arrived(("su", s, h), ("sd", s, h))
        c = stream(s)
        size, skip = (small, small) if h == 1 else (piece, 0)
        if h < half:
            grads[piece_rows(place + half - h, 0, size), c] += sum_up[h - 1, :size, c]
            grads[piece_rows(place + n - half + h, skip, size), c] += sum_down[h - 1, :size, c]
            start(("su", s, h + 1), ("sd", s, h + 1))
        else:
            grads[piece_rows(place), c] += sum_up[h - 1, :size, c] + sum_down[h - 1, :size, c]
            start(("gu", s, 1), ("gd", s, 1), ("cu", s, 0))
            local_own(s).start()

    def local_own(s):
        c = stream(s)
        return pltpu.make_async_copy(
            grads.at[piece_rows(place), c],
            attn_grads.at[piece_rows(place, 0, piece, core * sz.grad_rows), c],
            local_sems.at[7 + s],
        )

    def gather_step(s, h):
        arrived(("gu", s, h), ("gd", s, h))
        if h < half:
            start(("gu", s, h + 1), ("gd", s, h + 1))
        start(("cu", s, h), ("cd", s, h))

    def finish_tokens():
        arrived(("part", 2))
        grad = part[2, :rows] + part_theirs[2, :rows]
        value = tokens[...].astype(F32)
        factor = norm_factor(value)
        unit = value * factor
        tokens_grad[...] = (
            middle_grad[...] + norm_grad(grad, unit, factor, attn_gain[...])
        ).astype(BF16)
        gain_send[0:1, :] = jnp.sum(grad * unit, axis=0, keepdims=True)
        gain_send[2:, :] = part[2, rows : rows + 6] + part_theirs[2, rows : rows + 6]
        start("gains")

    def finish_mixed():
        arrived(("part", 3))
        mixed[...] = (middle[...] + (part[0, :rows] + part_theirs[3, :rows])).astype(BF16)

    def gain_first():
        arrived("gains")
        gain_slots[place] = gain_send[...] + gain_recv[...]
        start(("vu", 1), ("vd", 1))

    def gain_step(h):
        arrived(("vu", h))
        if h < half:
            arrived(("vd", h))
            start(("vu", h + 1))
            if h + 1 < half:
                start(("vd", h + 1))
        else:
            total = gain_slots[0]
            for chip_at in range(1, n):
                total = total + gain_slots[chip_at]
            gains[...] = total

    def second_phase(wg, wu, wd, gate_sum, up_sum, down_sum, staged, ffn_low, ffn_turned, cot_low):
        weight_loads = [
            pltpu.make_async_copy(src, dst, local_sems.at[i])
            for i, (src, dst) in enumerate(
                (
                    (w_gate.at[:, own_half(half_units)], wg),
                    (w_up.at[:, own_half(half_units)], wu),
                    (w_down.at[pl.ds(pl.multiple_of(core * half_units, 8), half_units)], wd),
                )
            )
        ]
        for load in weight_loads:
            load.start()

        def stage(slot, first):
            copies = []
            for a in (COT, FFN):
                src = own.at[a] if first else mine.at[a, slot]
                copies.append(
                    pltpu.make_async_copy(src, staged.at[a, 0], local_sems.at[9 + 2 * a])
                )
                copies.append(
                    pltpu.make_async_copy(
                        theirs.at[a, slot], staged.at[a, 1], local_sems.at[10 + 2 * a]
                    )
                )
            return copies

        arrived(("core", COT, 0), ("core", FFN, 0))
        for copy in stage(0, True):
            copy.start()
        for load in weight_loads:
            load.wait()
        chunks = 3
        size = half_units // chunks
        events = {}

        def at(tick, *todo):
            events.setdefault(tick, []).extend(todo)

        def later(event, *of):
            return lambda: event(*of)

        far = chunks * slots
        at(1, later(x_done, FFN, 1), later(x_done, FFN, 2))
        at(2, later(ring_step, FFN, 2), later(x_start, FFN, 3), later(x_start, FFN, 4))
        at(3, later(sum_step, 0, 1))
        at(4, later(sum_step, 1, 1))
        at(5, later(ring_step, COT, 4), later(x_done, COT, 5), later(x_done, COT, 6))
        at(6, later(start, ("part", 2)))
        at(7, later(x_done, FFN, 3), later(x_done, FFN, 4))
        at(9, later(sum_step, 0, 2))
        at(11, later(sum_step, 1, 2))
        at(12, later(x_start, COT, 7))
        at(13, later(ring_step, FFN, 3), later(x_start, FFN, 5), later(x_start, FFN, 6))
        at(14, later(x_done, FFN, 5), later(x_done, FFN, 6))
        at(16, later(sum_step, 0, 3))
        at(17, later(ring_step, FFN, 4), later(x_start, FFN, 7), finish_tokens)
        at(18, later(sum_step, 1, 3))
        at(19, later(x_done, COT, 7), later(x_done, FFN, 7), later(start, ("part", 3)))
        at(20, gain_first)
        at(21, later(gain_step, 1), later(sum_step, 0, 4))
        at(22, later(gain_step, 2))
        at(23, later(gain_step, 3), later(sum_step, 1, 4))
        at(far, later(gather_step, 0, 1), later(gain_step, 4), later(gather_step, 1, 1))
        at(far + 1, finish_mixed)
        for h in range(2, half + 1):
            at(far + h, later(gather_step, 0, h), later(gather_step, 1, h))

        def step(i, _):
            slot, j = i // chunks, i % chunks

            @pl.when(j == 0)
            def _():
                for copy in stage(slot, False):
                    copy.wait()
                for lane in range(2):
                    here = pl.ds(lane * rows, rows)
                    low_block = staged[FFN, lane].astype(BF16)
                    ffn_low[here] = low_block
                    ffn_turned[:, lane * rows : (lane + 1) * rows] = low_block.T
                    cot_low[here] = staged[COT, lane].astype(BF16)

            for tick, todo in events.items():
                if tick < chunks * slots:

                    @pl.when(i == tick)
                    def _():
                        for event in todo:
                            event()

            at_units = pl.ds(pl.multiple_of(j * size, 128), size)
            hidden, gate_grad, up_grad = ffn_middle(
                ffn_low[...], cot_low[...], wg[:, at_units], wu[:, at_units], wd[at_units]
            )
            down = across_rows(hidden, cot_low[...])
            gate = rows_dot(ffn_turned[...], gate_grad)
            up = rows_dot(ffn_turned[...], up_grad)

            @pl.when(slot == 0)
            def _():
                gate_sum[:, at_units] = gate
                up_sum[:, at_units] = up
                down_sum[at_units] = down

            @pl.when(slot > 0)
            def _():
                gate_sum[:, at_units] += gate
                up_sum[:, at_units] += up
                down_sum[at_units] += down

            for s in range(1, slots):

                @pl.when(i == chunks * s - 1)
                def _():
                    arrived(("core", COT, s), ("core", FFN, s))
                    for copy in stage(s, False):
                        copy.start()

            return 0

        lax.fori_loop(0, chunks * slots, step, 0)
        outs = [
            (gate_sum, gate_grads.at[:, own_half(half_units)]),
            (up_sum, up_grads.at[:, own_half(half_units)]),
            (down_sum, down_grads.at[pl.ds(pl.multiple_of(core * half_units, 8), half_units)]),
        ]
        for k, (src, dst) in enumerate(outs):
            remote(("out", k), src, dst, sibling)
            start(("out", k))
            pltpu.make_async_copy(src, dst, local_sems.at[k]).start()
        for tick in sorted(t for t in events if t >= chunks * slots):
            for event in events[tick]:
                event()
        for k, (src, dst) in enumerate(outs):
            pltpu.make_async_copy(src, dst, local_sems.at[k]).wait()
            made(("out", k)).wait()

    pl.run_scoped(
        second_phase,
        pltpu.VMEM((width, half_units), BF16),
        pltpu.VMEM((width, half_units), BF16),
        pltpu.VMEM((half_units, width), BF16),
        pltpu.VMEM((width, half_units), F32),
        pltpu.VMEM((width, half_units), F32),
        pltpu.VMEM((half_units, width), F32),
        pltpu.VMEM((2, 2, rows, width), F32),
        pltpu.VMEM((2 * rows, width), BF16),
        pltpu.VMEM((width, 2 * rows), BF16),
        pltpu.VMEM((2 * rows, width), BF16),
    )
    for s in range(sz.streams):
        local_own(s).wait()
        for h in range(half + 1):
            arrived(("cu", s, h))
            if h:
                arrived(("cd", s, h))
    for name in book:
        if name[0] != "out" and name != ("part", 0):
            made(name).wait_send()


def rotary_tables(places, head_width):
    inverse = THETA ** (-(jnp.arange(head_width // 2, dtype=F32) * 2.0 / head_width))
    angles = places.astype(F32)[:, None] * inverse[None, :]
    cosine, sine = jnp.cos(angles), jnp.sin(angles)
    return jnp.concatenate([cosine, cosine], -1), jnp.concatenate([-sine, sine], -1)


def over_groups(sz, dp_size, values):
    step = sz.group
    while step < dp_size:
        values = values + lax.ppermute(values, "dp", [(d, d ^ step) for d in range(dp_size)])
        step *= 2
    return values


def per_device(
    dp_size,
    tokens,
    segments,
    positions,
    attn_gain,
    w_query,
    key_weight,
    value_weight,
    query_gain,
    key_gain,
    w_out,
    ffn_gain,
    w_gate,
    w_up,
    w_down,
    cotangent,
):
    sz = Sizes(dp_size, tokens.shape, w_query.shape, key_weight.shape, query_gain.shape, w_gate.shape)
    rows, width, head_width, half = sz.rows, sz.width, sz.head_width, sz.half
    q_cols, k_cols = sz.q_cols, sz.k_cols
    segment_row = segments[0]
    order_rows = jnp.arange(rows)
    mask = (
        (segment_row[:, None] == segment_row[None, :])
        & (order_rows[:, None] >= order_rows[None, :])
    ).astype(F32)
    cosine, sine = rotary_tables(positions[0], head_width)

    vmem = pl.BlockSpec(memory_space=pltpu.VMEM)
    anywhere = pl.BlockSpec(memory_space=pl.ANY)
    slots = 2 * half
    transfers = 256
    mixed, tokens_grad, gains, attn_grads, gate_grads, up_grads, down_grads, _, _ = pl.pallas_call(
        functools.partial(layer_kernel, sz),
        out_shape=[
            shaped(rows, width, kind=BF16),
            shaped(rows, width, kind=BF16),
            shaped(8, width),
            shaped(width, sz.grad_cols),
            shaped(*w_gate.shape),
            shaped(*w_up.shape),
            shaped(*w_down.shape),
            shaped(2, slots, rows, width),
            shaped(2, slots, rows, width),
        ],
        in_specs=[vmem] * 9 + [anywhere] * 7,
        out_specs=[vmem] * 3 + [anywhere] * 6,
        scratch_shapes=[
            pltpu.VMEM((2, rows, width), F32),
            pltpu.VMEM((3, rows + 8, width), F32),
            pltpu.VMEM((4, rows + 8, width), F32),
            pltpu.VMEM((rows, width), F32),
            pltpu.VMEM((rows, width), F32),
            pltpu.VMEM((rows, q_cols // 2), F32),
            pltpu.VMEM((rows, q_cols // 2), F32),
            pltpu.VMEM((rows, width // 2), F32),
            pltpu.VMEM((rows, width // 2), F32),
            pltpu.VMEM((rows, width), F32),
            pltpu.VMEM((rows, width), F32),
            pltpu.VMEM((rows, sz.all_cols), F32),
            pltpu.VMEM((rows, sz.all_cols), F32),
            pltpu.VMEM((sz.grad_rows, sz.grad_cols), F32),
            pltpu.VMEM((half, sz.piece, sz.grad_cols), F32),
            pltpu.VMEM((half, sz.piece, sz.grad_cols), F32),
            pltpu.VMEM((8, width), F32),
            pltpu.VMEM((8, width), F32),
            pltpu.VMEM((sz.chips, 8, width), F32),
            pltpu.VMEM((rows, width), BF16),
            pltpu.SemaphoreType.DMA((transfers,)),
            pltpu.SemaphoreType.DMA((transfers,)),
            pltpu.SemaphoreType.DMA((16,)),
        ],
        compiler_params=pltpu.CompilerParams(
            collective_id=0, has_side_effects=True, vmem_limit_bytes=VMEM_BYTES
        ),
    )(
        tokens, cotangent, mask, cosine, sine, attn_gain[None], query_gain[None], key_gain[None],
        ffn_gain[None], w_query, key_weight, value_weight, w_out, w_gate, w_up, w_down,
    )
    gains, attn_grads, gate_grads, up_grads, down_grads = [
        over_groups(sz, dp_size, v) for v in (gains, attn_grads, gate_grads, up_grads, down_grads)
    ]
    at_q, at_k, at_v = width, width + q_cols, width + q_cols + k_cols
    return (
        mixed,
        tokens_grad,
        gains[0],
        attn_grads[:, at_q:at_k],
        attn_grads[:, at_k:at_v],
        attn_grads[:, at_v:],
        gains[2, :head_width],
        gains[2, head_width : 2 * head_width],
        attn_grads[:, :width],
        gains[1],
        gate_grads,
        up_grads,
        down_grads,
    )


def solution(mesh):
    def layer(*arrays):
        return per_device(mesh.shape["dp"], *arrays)

    return jax.shard_map(
        layer,
        mesh=mesh,
        in_specs=(
            P("dp", None),
            P("dp", None),
            P("dp", None),
            P(),
            P(None, "tensor"),
            P(None, "tensor"),
            P(None, "tensor"),
            P(),
            P(),
            P("tensor", None),
            P(),
            P(None, "tensor"),
            P(None, "tensor"),
            P("tensor", None),
            P("dp", None),
        ),
        out_specs=(
            P("dp", None),
            P("dp", None),
            P(),
            P(None, "tensor"),
            P(None, "tensor"),
            P(None, "tensor"),
            P(),
            P(),
            P("tensor", None),
            P(),
            P(None, "tensor"),
            P(None, "tensor"),
            P("tensor", None),
        ),
        check_vma=False,
    )
```

```python
import functools
import math

import jax
import jax.numpy as jnp
import numpy as np
from jax import lax
from jax.experimental import pallas as pl
from jax.experimental.pallas import tpu as pltpu
from jax.sharding import PartitionSpec as P

EPS = 1e-06
THETA = 1000000.0
F32 = jnp.float32
BF16 = jnp.bfloat16
MESH = pl.DeviceIdType.MESH
VMEM_BYTES = 50 * 2**20
RESULTS_VMEM_BYTES = 24 * 2**20
GROUP = 16
COT, FFN = 0, 1


PLAN = {
    "A2": [
        ("ring", COT, 1),
        ("start", "x", COT, 1),
    ],
    "A4": [
        ("ring", COT, 2),
    ],
    "A5": [
        ("x_done", COT, 1),
        ("ring", FFN, 1),
    ],
    "A6": [
        ("ring", COT, 3),
        ("start", "x", COT, 2),
        ("start", "x", COT, 3),
    ],
    "A8": [
        ("x_done", COT, 2),
        ("start", "x", COT, 4),
    ],
    (0, 0): [
        ("ring", FFN, 2),
        ("x_done", COT, 3),
        ("start", "x", FFN, 1),
    ],
    (1, 1): [
        ("x_done", COT, 4),
        ("start", "x", FFN, 2),
    ],
    (2, 0): [
        ("ring", COT, 4),
    ],
    (2, 2): [
        ("sum", 0, 1),
        ("sum", 1, 1),
        ("x_done", FFN, 1),
        ("start", "x", COT, 5),
        ("stage", 1),
    ],
    (4, 1): [
        ("ring", FFN, 3),
        ("x_done", FFN, 2),
        ("start", "x", COT, 6),
    ],
    (5, 1): [
        ("stage", 2),
    ],
    (6, 0): [
        ("x_done", COT, 5),
        ("start", "x", FFN, 3),
    ],
    (6, 1): [
        ("sum", 0, 2),
    ],
    (7, 1): [
        ("x_done", COT, 6),
        ("start", "x", FFN, 4),
    ],
    (8, 2): [
        ("sum", 1, 2),
        ("ring", FFN, 4),
        ("x_done", FFN, 3),
        ("start", "x", FFN, 5),
        ("stage", 3),
    ],
    (9, 1): [
        ("sum", 0, 3),
    ],
    (10, 1): [
        ("x_done", FFN, 4),
        ("start", "x", FFN, 6),
    ],
    (11, 1): [
        ("stage", 4),
    ],
    (12, 0): [
        ("sum", 1, 3),
    ],
    (13, 1): [
        ("x_done", FFN, 5),
        ("start", "x", COT, 7),
    ],
    (14, 0): [
        ("sum", 0, 4),
    ],
    (14, 1): [
        ("stage", 5),
    ],
    (16, 0): [
        ("sum", 1, 4),
        ("x_done", FFN, 6),
        ("start", "x", FFN, 7),
    ],
    (17, 0): [
        ("stage", 6),
    ],
    (17, 1): [
        ("x_done", COT, 7),
        ("start", "part", 2),
    ],
    (18, 0): [
        ("gather", 0, 1),
    ],
    (20, 1): [
        ("gather", 1, 1),
    ],
    (20, 2): [
        ("x_done", FFN, 7),
        ("start", "part", 3),
        ("stage", 7),
    ],
    (21, 0): [
        ("gather", 0, 2),
    ],
    (23, 1): [
        ("gather", 1, 2),
    ],
    (24, 0): [
        ("tokens",),
        ("gather", 0, 3),
        ("gather", 1, 3),
        ("gain", 0),
        ("gather", 0, 4),
        ("gather", 1, 4),
        ("gain", 1),
        ("gain", 2),
        ("gain", 3),
        ("mixed",),
        ("gain", 4),
    ],
}


def norm_factor(values):
    return lax.rsqrt(jnp.mean(values * values, axis=-1, keepdims=True) + EPS)


def norm_grad(grad_out, unit_rows, factor, scale_gain):
    scaled = grad_out * scale_gain
    return factor * (scaled - unit_rows * jnp.mean(scaled * unit_rows, axis=-1, keepdims=True))


def rows_dot(leading, trailing):
    return jnp.dot(leading, trailing, preferred_element_type=F32)


def across_rows(leading, trailing):
    return lax.dot_general(
        leading, trailing, (((0,), (0,)), ((), ())), preferred_element_type=F32
    )


def against_rows(leading, trailing):
    return lax.dot_general(
        leading, trailing, (((1,), (1,)), ((), ())), preferred_element_type=F32
    )


def ffn_middle(low_in, cot, wg, wu, wd):
    gate = rows_dot(low_in, wg)
    up = rows_dot(low_in, wu)
    sig = jax.nn.sigmoid(gate)
    silu = gate * sig
    hidden = (silu * up).astype(BF16)
    hidden_grad = against_rows(cot, wd)
    up_grad = (hidden_grad * silu).astype(BF16)
    gate_grad = (hidden_grad * up * sig * (1.0 + gate * (1.0 - sig))).astype(BF16)
    return hidden, gate_grad, up_grad


def shaped(*shape, kind=F32):
    return jax.ShapeDtypeStruct(shape, kind)


class Sizes:
    def __init__(self, dp_size, tokens, w_query, key_weight, query_gain, w_gate):
        self.rows, self.width = tokens
        self.head_width = query_gain[0]
        self.q_cols, self.k_cols = w_query[1], key_weight[1]
        self.heads, self.kv_heads = self.q_cols // self.head_width, self.k_cols // self.head_width
        self.units = w_gate[1]
        self.all_cols = self.q_cols + 2 * self.k_cols
        self.scale = 1.0 / math.sqrt(self.head_width)
        self.group = math.gcd(GROUP, dp_size)
        self.chips = self.group // 2
        self.half = self.chips // 2
        self.share = (self.width // 4, self.width // 2)
        self.grad_rows = self.width // 2
        self.grad_cols = self.width + self.all_cols
        self.piece = self.grad_rows // self.chips
        self.streams = 2


def layer_kernel(
    sz,
    tokens, cot, segments, positions, inverse, attn_gain, query_gain, key_gain, ffn_gain,
    w_query, key_weight, value_weight, w_out, w_gate, w_up, w_down,
    mixed, tokens_grad, gains, attn_grads,
    gate_grads, up_grads, down_grads, mine, theirs,
    own, part, part_theirs, middle, middle_grad,
    ctx_recv, attn_recv, branch_recv, low_recv,
    sum_up, sum_down, gain_send, gain_recv, gain_slots, attn_low,
    send_sems, recv_sems, local_sems,
):
    rows, width, head_width = sz.rows, sz.width, sz.head_width
    q_cols, k_cols, units = sz.q_cols, sz.k_cols, sz.units
    n, half, piece = sz.chips, sz.half, sz.piece
    half_units = units // 2
    mid = rows // 2

    device = lax.axis_index("dp")
    base = device // sz.group * sz.group
    core = device % 2
    chip = device % sz.group // 2
    line = chip % 2
    place = chip // 2 + line * (2 * half - 1 - 2 * (chip // 2))
    side = lax.axis_index("tensor")

    def device_at(position):
        position = position % n
        second = position // half
        return base + (2 * (position + second * (2 * half - 1 - 2 * position)) + second) * 2 + core

    forward = {"dp": device_at(place + 1)}
    backward = {"dp": device_at(place + n - 1)}
    sibling = {"dp": base + chip * 2 + 1 - core}
    across = {"tensor": 1 - side}

    barrier = pltpu.get_barrier_semaphore()
    for neighbour in (forward, backward, sibling, across):
        pl.semaphore_signal(barrier, inc=1, device_id=neighbour, device_id_type=MESH)
    pl.semaphore_wait(barrier, 4)

    book = {}
    waited = set()

    def remote(name, src, dst, target):
        book[name] = (len(book), src, dst, target)

    def made(name):
        index, src, dst, target = book[name]
        return pltpu.make_async_remote_copy(
            src_ref=src, dst_ref=dst, send_sem=send_sems.at[index], recv_sem=recv_sems.at[index],
            device_id=target, device_id_type=MESH,
        )

    def sent(*names):
        for name in names:
            made(name).wait_send()
            waited.add(name)

    def start(*names):
        for name in names:
            made(name).start()

    def arrived(*names):
        for name in names:
            made(name).wait_recv()

    def cols(first, count):
        return pl.ds(pl.multiple_of(first, 128), count)

    def piece_rows(index, first=0, count=piece, base_row=0):
        return pl.ds(pl.multiple_of(base_row + index % n * piece + first, 8), count)

    grad_base = core * sz.grad_rows
    slots = 2 * half
    up_slot = lambda h: 2 * h - 1
    down_slot = lambda h: 2 * h
    last = slots - 1
    for a, share in zip((COT, FFN), sz.share):
        window = cols(side * share, width - share)
        shared = cols(side * (width - share), share)
        for h in range(1, half):
            src = own.at[a] if h == 1 else mine.at[a, up_slot(h - 1)]
            remote(("up", a, h), src.at[:, window], mine.at[a, up_slot(h), :, window], forward)
            src = own.at[a] if h == 1 else mine.at[a, down_slot(h - 1)]
            remote(("down", a, h), src.at[:, window], mine.at[a, down_slot(h), :, window], backward)
        remote(
            ("up", a, half), mine.at[a, up_slot(half - 1), pl.ds(0, mid), window],
            mine.at[a, last, pl.ds(0, mid), window], forward,
        )
        remote(
            ("down", a, half), mine.at[a, down_slot(half - 1), pl.ds(mid, mid), window],
            mine.at[a, last, pl.ds(mid, mid), window], backward,
        )
        for s in range(1, slots):
            remote(("x", a, s), mine.at[a, s, :, shared], mine.at[a, s, :, shared], across)
        for s in range(slots):
            remote(("core", a, s), own.at[a] if s == 0 else mine.at[a, s], theirs.at[a, s], sibling)
    for k in range(4):
        remote(("part", k), part.at[k % 3], part_theirs.at[k], across)
    stream_cols = sz.grad_cols // sz.streams
    small = piece // 2
    for s in range(sz.streams):
        c = pl.ds(s * stream_cols, stream_cols)
        for h in range(1, half + 1):
            size, skip = (small, small) if h == 1 else (piece, 0)
            src = attn_grads.at[piece_rows(place + half, 0, small, grad_base), c]
            remote(
                ("su", s, h), src if h == 1 else sum_up.at[h - 2, :, c],
                sum_up.at[h - 1, pl.ds(0, size), c], forward,
            )
            src = attn_grads.at[piece_rows(place + half, small, small, grad_base), c]
            remote(
                ("sd", s, h), src if h == 1 else sum_down.at[h - 2, :, c],
                sum_down.at[h - 1, pl.ds(skip, size), c], backward,
            )
        for h in range(1, half + 1):
            size, skip = (small, small) if h == half else (piece, 0)
            going_up = attn_grads.at[piece_rows(place + n - h + 1, 0, size, grad_base), c]
            going_down = attn_grads.at[piece_rows(place + h - 1, skip, size, grad_base), c]
            remote(("gu", s, h), going_up, going_up, forward)
            remote(("gd", s, h), going_down, going_down, backward)
            got_up = attn_grads.at[piece_rows(place + n - h, 0, size, grad_base), c]
            got_down = attn_grads.at[piece_rows(place + h, skip, size, grad_base), c]
            remote(("cu", s, h), got_up, got_up, sibling)
            remote(("cd", s, h), got_down, got_down, sibling)
        own_piece = attn_grads.at[piece_rows(place, 0, piece, grad_base), c]
        remote(("cu", s, 0), own_piece, own_piece, sibling)
    remote("gains", gain_send, gain_recv, sibling)
    for h in range(1, half + 1):
        slot = gain_slots.at[(place + n - h + 1) % n]
        remote(("vu", h), slot, slot, forward)
        if h < half:
            slot = gain_slots.at[(place + h - 1) % n]
            remote(("vd", h), slot, slot, backward)

    def ring_step(a, h):
        arrived(("up", a, h), ("down", a, h))
        if h < half:
            start(("up", a, h + 1), ("down", a, h + 1))

    def x_start(a, s):
        start(("x", a, s))

    def x_done(a, s):
        arrived(("x", a, s))
        start(("core", a, s))


    def stream(s):
        return pl.ds(s * stream_cols, stream_cols)

    def sum_step(s, h):
        arrived(("su", s, h), ("sd", s, h))
        c = stream(s)
        up_rows = piece_rows(place + half - h, 0, piece, grad_base)
        down_rows = piece_rows(place + n - half + h, 0, piece, grad_base)
        if h == 1:
            sent(("su", s, 1), ("sd", s, 1))
            up, down = attn_grads[up_rows, c], attn_grads[down_rows, c]
            sum_up[0, :small, c] += up[:small]
            sum_up[0, small:, c] = up[small:]
            sum_down[0, :small, c] = down[:small]
            sum_down[0, small:, c] += down[small:]
        elif h < half:
            sum_up[h - 1, :, c] += attn_grads[up_rows, c]
            sum_down[h - 1, :, c] += attn_grads[down_rows, c]
        if h < half:
            start(("su", s, h + 1), ("sd", s, h + 1))
        else:
            own_rows = piece_rows(place, 0, piece, grad_base)
            attn_grads[own_rows, c] += sum_up[h - 1, :, c] + sum_down[h - 1, :, c]
            start(("gu", s, 1), ("gd", s, 1), ("cu", s, 0))

    def gather_step(s, h):
        arrived(("gu", s, h), ("gd", s, h))
        if h < half:
            start(("gu", s, h + 1), ("gd", s, h + 1))
        start(("cu", s, h), ("cd", s, h))

    def finish_tokens():
        arrived(("part", 2))
        grad = part[2, :rows] + part_theirs[2, :rows]
        value = tokens[...].astype(F32)
        factor = norm_factor(value)
        unit = value * factor
        tokens_grad[...] = (
            middle_grad[...] + norm_grad(grad, unit, factor, attn_gain[...])
        ).astype(BF16)
        gain_send[0:1, :] = jnp.sum(grad * unit, axis=0, keepdims=True)
        gain_send[2:, :] = part[2, rows : rows + 6] + part_theirs[2, rows : rows + 6]
        start("gains")

    def finish_mixed():
        arrived(("part", 3))
        mixed[...] = (middle[...] + (part[0, :rows] + part_theirs[3, :rows])).astype(BF16)

    def gain_first():
        arrived("gains")
        gain_slots[place] = gain_send[...] + gain_recv[...]
        start(("vu", 1), ("vd", 1))

    def gain_step(h):
        arrived(("vu", h))
        if h < half:
            arrived(("vd", h))
            start(("vu", h + 1))
            if h + 1 < half:
                start(("vd", h + 1))
        else:
            total = gain_slots[0]
            for chip_at in range(1, n):
                total = total + gain_slots[chip_at]
            gains[...] = total

    def stage(slot):
        arrived(("core", COT, slot), ("core", FFN, slot))
        for copy in stage_copies(slot, False):
            copy.start()

    scoped = {}

    def stage_copies(slot, first):
        staged = scoped["staged"]
        copies = []
        for a in (COT, FFN):
            src = own.at[a] if first else mine.at[a, slot]
            copies.append(pltpu.make_async_copy(src, staged.at[a, 0], local_sems.at[9 + 2 * a]))
            copies.append(
                pltpu.make_async_copy(theirs.at[a, slot], staged.at[a, 1], local_sems.at[10 + 2 * a])
            )
        return copies

    def gain_event(h):
        if h == 0:
            gain_first()
        else:
            gain_step(h)

    actions = {
        "ring": ring_step,
        "start": lambda *name: start(name),
        "x_done": x_done,
        "sum": sum_step,
        "gather": gather_step,
        "stage": stage,
        "tokens": finish_tokens,
        "gain": gain_event,
        "mixed": finish_mixed,
    }

    def run(when):
        for event in PLAN.get(when, ()):
            actions[event[0]](*event[1:])

    group = q_cols // k_cols
    other_half = lambda count: cols((1 - core) * count, count)
    own_half = lambda count: cols(core * count, count)

    block = k_cols
    q_blocks, unit_blocks = q_cols // block, units // block
    at_k, at_v, at_o = q_blocks, q_blocks + 1, q_blocks + 2

    def first_phase(
        bank, wd, mask, cosine, sine, q_lin, k_lin, q_low, k_low, v_low, probs, context, ffn_low, hidden,
        context_grad, ctx_send, attn_send, branch, low,
    ):
        remote("ctx", ctx_send, ctx_recv, sibling)
        remote("attn", attn_send, attn_recv, sibling)
        remote("branch", branch, branch_recv, sibling)
        remote("low", low, low_recv, sibling)

        def load(src, dst, index):
            copy = pltpu.make_async_copy(src, dst, local_sems.at[index])
            copy.start()
            return copy

        def block_of(weights, index):
            return weights.at[:, pl.ds(index * block, block)]

        def load_attention():
            order = [(w_query, i) for i in range(q_blocks)] + [(key_weight, 0), (value_weight, 0)]
            order += [(w_out, i) for i in range(width // block)]
            return [load(block_of(w, i), bank.at[k], k) for k, (w, i) in enumerate(order)]

        def load_ffn():
            order = [(w, i) for w in (w_gate, w_up) for i in range(unit_blocks)]
            return [load(block_of(w, i), bank.at[k], k) for k, (w, i) in enumerate(order)]

        loads = load_attention()
        down_load = load(w_down, wd, 15)

        def head_norm(lin, gain):
            return lin * norm_factor(lin) * gain[...]

        def turned(lin, gain):
            normed = head_norm(lin, gain)
            swapped = pltpu.roll(normed, head_width // 2, 1)
            return (normed * cosine[...] + swapped * sine[...]).astype(BF16)

        def turned_back(grad, lin, gain):
            back = grad * cosine[...] - pltpu.roll(grad, head_width // 2, 1) * sine[...]
            factor = norm_factor(lin)
            unit = lin * factor
            return (
                norm_grad(back, unit, factor, gain[...]).astype(BF16),
                jnp.sum(back * unit, axis=0, keepdims=True),
            )

        own[COT] = cot[...].astype(F32)
        start(("up", COT, 1), ("down", COT, 1), ("core", COT, 0))

        resid = tokens[...].astype(F32)
        attn_in = (resid * norm_factor(resid) * attn_gain[...]).astype(BF16)
        attn_low[...] = attn_in
        attn_send[...] = attn_low[:, other_half(width // 2)].astype(F32)
        start("attn")

        def down_rows(row):
            return jnp.broadcast_to(row.astype(F32), (head_width, rows)).T

        segment_rows = jnp.concatenate([down_rows(segments[...])] * (rows // head_width), 1)
        same = segment_rows == jnp.broadcast_to(segments[...].astype(F32), (rows, rows))
        row_at = lax.broadcasted_iota(jnp.int32, (rows, rows), 0)
        column_at = lax.broadcasted_iota(jnp.int32, (rows, rows), 1)
        mask[...] = jnp.where(same & (row_at >= column_at), 1.0, 0.0)
        angles = down_rows(positions[...]) * inverse[...]
        lane = lax.broadcasted_iota(jnp.int32, (rows, head_width), 1)
        cosine[...] = jnp.cos(angles)
        sine[...] = jnp.where(lane < head_width // 2, -1.0, 1.0) * jnp.sin(angles)
        for i in range(q_blocks):
            loads[i].wait()
            q_lin[:, i * block : (i + 1) * block] = rows_dot(attn_in, bank[i])
        loads[at_k].wait()
        k_lin[...] = rows_dot(attn_in, bank[at_k])
        loads[at_v].wait()
        v_low[...] = rows_dot(attn_in, bank[at_v]).astype(BF16)
        run("A1")
        for kv in range(sz.kv_heads):
            kv_at = slice(kv * head_width, (kv + 1) * head_width)
            keys = turned(k_lin[:, kv_at], key_gain)
            k_low[:, kv_at] = keys
            values = v_low[:, kv_at]
            for member in range(group):
                head = kv * group + member
                at = slice(head * head_width, (head + 1) * head_width)
                queries = turned(q_lin[:, at], query_gain)
                q_low[:, at] = queries
                scores = jnp.where(mask[...] > 0, against_rows(queries, keys) * sz.scale, -1e30)
                raised = jnp.exp(scores - jnp.max(scores, axis=-1, keepdims=True))
                prob = raised / jnp.sum(raised, axis=-1, keepdims=True)
                probs[head] = prob
                context[:, at] = rows_dot(prob.astype(BF16), values).astype(BF16)
        for i in range(width // block):
            loads[at_o + i].wait()
            part[0, :rows, i * block : (i + 1) * block] = rows_dot(context[...], bank[at_o + i])
        part[0, rows:] = jnp.zeros((8, width), F32)
        start(("part", 0))
        ctx_send[...] = context[:, other_half(q_cols // 2)].astype(F32)
        start("ctx")
        loads = load_ffn()
        run("A2")

        arrived(("part", 0))
        value = tokens[...].astype(F32) + (part[0, :rows] + part_theirs[0, :rows])
        middle[...] = value
        ffn_low[...] = (value * norm_factor(value) * ffn_gain[...]).astype(BF16)
        own[FFN] = ffn_low[...].astype(F32)
        start(("up", FFN, 1), ("down", FFN, 1), ("core", FFN, 0))
        run("A3")
        down_load.wait()
        for i in range(unit_blocks):
            at = slice(i * block, (i + 1) * block)
            loads[i].wait()
            loads[unit_blocks + i].wait()
            wg, wu = bank[i], bank[unit_blocks + i]
            low_hidden, gate_grad, up_grad = ffn_middle(ffn_low[...], cot[...], wg, wu, wd[at])
            hidden[:, at] = low_hidden
            term = against_rows(gate_grad, wg) + against_rows(up_grad, wu)
            if i == 0:
                part[1, :rows] = term
            else:
                part[1, :rows] += term
        part[1, rows:] = jnp.zeros((8, width), F32)
        start(("part", 1))
        loads = load_attention()
        run("A4")
        sent(("part", 0))
        part[0, :rows] = rows_dot(hidden[...], wd[...])
        run("A5")

        arrived(("part", 1))
        grad = part[1, :rows] + part_theirs[1, :rows]
        value = middle[...]
        factor = norm_factor(value)
        unit = value * factor
        total = cot[...].astype(F32) + norm_grad(grad, unit, factor, ffn_gain[...])
        middle_grad[...] = total
        branch_low = total.astype(BF16)
        branch[...] = branch_low.astype(F32)
        start("branch")
        gain_send[1:2, :] = jnp.sum(grad * unit, axis=0, keepdims=True)
        run("A6")
        for load_of in loads:
            load_of.wait()
        context_grad[...] = sum(
            against_rows(branch_low[:, i * block : (i + 1) * block], bank[at_o + i])
            for i in range(width // block)
        ).astype(BF16)
        q_total = jnp.zeros((1, head_width), F32)
        k_total = jnp.zeros((1, head_width), F32)
        for kv in range(sz.kv_heads):
            kv_at = slice(kv * head_width, (kv + 1) * head_width)
            keys, values = k_low[:, kv_at], v_low[:, kv_at]
            keys_grad = values_grad = 0.0
            for member in range(group):
                head = kv * group + member
                at = slice(head * head_width, (head + 1) * head_width)
                head_grad = context_grad[:, at]
                prob = probs[head]
                prob_grad = against_rows(head_grad, values)
                values_grad += across_rows(prob.astype(BF16), head_grad)
                inner = jnp.sum(prob * prob_grad, axis=-1, keepdims=True)
                score_grad = (prob * (prob_grad - inner)).astype(BF16)
                queries_grad = rows_dot(score_grad, keys) * sz.scale
                keys_grad += across_rows(score_grad, q_low[:, at])
                head_low, head_total = turned_back(queries_grad, q_lin[:, at], query_gain)
                low[:, at] = head_low.astype(F32)
                q_total += head_total
            head_low, head_total = turned_back(keys_grad * sz.scale, k_lin[:, kv_at], key_gain)
            k_total += head_total
            low[:, q_cols + kv * head_width : q_cols + (kv + 1) * head_width] = head_low.astype(F32)
            at = q_cols + k_cols + kv * head_width
            low[:, at : at + head_width] = values_grad.astype(BF16).astype(F32)
        start("low")
        run("A7")
        half_rows = pl.ds(pl.multiple_of(grad_base, 8), sz.grad_rows)
        arrived("ctx", "branch")
        attn_grads[half_rows, :width] = across_rows(
            context[:, own_half(q_cols // 2)], branch[...].astype(BF16)
        ) + across_rows(ctx_recv[...].astype(BF16), branch_recv[...].astype(BF16))
        arrived("attn", "low")
        attn_grads[half_rows, width:] = across_rows(
            attn_low[:, own_half(width // 2)], low[...].astype(BF16)
        ) + across_rows(attn_recv[...].astype(BF16), low_recv[...].astype(BF16))
        for s in range(sz.streams):
            start(("su", s, 1), ("sd", s, 1))
        part[2, :rows] = sum(
            against_rows(low[:, i * block : (i + 1) * block].astype(BF16), bank[i])
            for i in range(at_o)
        )
        part[2, rows:] = jnp.zeros((8, width), F32)
        part[2, rows : rows + 1, :head_width] = q_total
        part[2, rows : rows + 1, head_width : 2 * head_width] = k_total
        run("A8")
        sent("ctx", "attn", "branch", "low")

    pl.run_scoped(
        first_phase,
        pltpu.VMEM((max(at_o + width // block, 2 * unit_blocks), width, block), BF16),
        pltpu.VMEM(w_down.shape, BF16),
        pltpu.VMEM((rows, rows), F32),
        pltpu.VMEM((rows, head_width), F32),
        pltpu.VMEM((rows, head_width), F32),
        pltpu.VMEM((rows, q_cols), F32),
        pltpu.VMEM((rows, k_cols), F32),
        pltpu.VMEM((rows, q_cols), BF16),
        pltpu.VMEM((rows, k_cols), BF16),
        pltpu.VMEM((rows, k_cols), BF16),
        pltpu.VMEM((sz.heads, rows, rows), F32),
        pltpu.VMEM((rows, q_cols), BF16),
        pltpu.VMEM((rows, width), BF16),
        pltpu.VMEM((rows, units), BF16),
        pltpu.VMEM((rows, q_cols), BF16),
        pltpu.VMEM((rows, q_cols // 2), F32),
        pltpu.VMEM((rows, width // 2), F32),
        pltpu.VMEM((rows, width), F32),
        pltpu.VMEM((rows, sz.all_cols), F32),
    )

    def second_phase(
        wg, wu, wd, gate_sum, up_sum, down_sum, staged, ffn_low, ffn_turned, cot_low
    ):
        scoped["staged"] = staged
        weight_loads = [
            pltpu.make_async_copy(src, dst, local_sems.at[i])
            for i, (src, dst) in enumerate(
                (
                    (w_gate.at[:, own_half(half_units)], wg),
                    (w_up.at[:, own_half(half_units)], wu),
                    (w_down.at[pl.ds(pl.multiple_of(core * half_units, 8), half_units)], wd),
                )
            )
        ]
        for load in weight_loads:
            load.start()

        arrived(("core", COT, 0), ("core", FFN, 0))
        for copy in stage_copies(0, True):
            copy.start()
        for load in weight_loads:
            load.wait()
        chunks = 3
        size = half_units // chunks
        def step(i, _):
            slot, j = i // chunks, i % chunks

            @pl.when(j == 0)
            def _():
                for copy in stage_copies(slot, False):
                    copy.wait()
                for lane in range(2):
                    here = pl.ds(lane * rows, rows)
                    low_block = staged[FFN, lane].astype(BF16)
                    ffn_low[here] = low_block
                    ffn_turned[:, lane * rows : (lane + 1) * rows] = low_block.T
                    cot_low[here] = staged[COT, lane].astype(BF16)

            def events(part_of_step):
                for when in PLAN:
                    if isinstance(when, tuple) and when[0] < chunks * slots and when[1] == part_of_step:

                        @pl.when(i == when[0])
                        def _():
                            run(when)

            events(0)
            at_units = pl.ds(pl.multiple_of(j * size, 128), size)
            hidden, gate_grad, up_grad = ffn_middle(
                ffn_low[...], cot_low[...], wg[:, at_units], wu[:, at_units], wd[at_units]
            )
            events(1)
            down = across_rows(hidden, cot_low[...])
            gate = rows_dot(ffn_turned[...], gate_grad)
            up = rows_dot(ffn_turned[...], up_grad)

            @pl.when(slot == 0)
            def _():
                gate_sum[:, at_units] = gate
                up_sum[:, at_units] = up
                down_sum[at_units] = down

            @pl.when(slot > 0)
            def _():
                gate_sum[:, at_units] += gate
                up_sum[:, at_units] += up
                down_sum[at_units] += down

            events(2)
            return 0

        lax.fori_loop(0, chunks * slots, step, 0)
        outs = [
            (gate_sum, gate_grads.at[:, own_half(half_units)]),
            (up_sum, up_grads.at[:, own_half(half_units)]),
            (down_sum, down_grads.at[pl.ds(pl.multiple_of(core * half_units, 8), half_units)]),
        ]
        for k, (src, dst) in enumerate(outs):
            remote(("out", k), src, dst, sibling)
            start(("out", k))
            pltpu.make_async_copy(src, dst, local_sems.at[k]).start()
        run((chunks * slots, 0))
        for k, (src, dst) in enumerate(outs):
            pltpu.make_async_copy(src, dst, local_sems.at[k]).wait()
            arrived(("out", k))
            sent(("out", k))

    pl.run_scoped(
        second_phase,
        pltpu.VMEM((width, half_units), BF16),
        pltpu.VMEM((width, half_units), BF16),
        pltpu.VMEM((half_units, width), BF16),
        pltpu.VMEM((width, half_units), F32),
        pltpu.VMEM((width, half_units), F32),
        pltpu.VMEM((half_units, width), F32),
        pltpu.VMEM((2, 2, rows, width), F32),
        pltpu.VMEM((2 * rows, width), BF16),
        pltpu.VMEM((width, 2 * rows), BF16),
        pltpu.VMEM((2 * rows, width), BF16),
    )
    for s in range(sz.streams):
        for h in range(half + 1):
            arrived(("cu", s, h))
            if h:
                arrived(("cd", s, h))
    for name in book:
        if name not in waited:
            made(name).wait_send()


def results_kernel(
    sz,
    mixed, tokens_grad, gains, attn_grads, gate_grads, up_grads, down_grads,
    mixed_out, tokens_out, out_out, query_out, key_out, value_out, gate_out, up_out, down_out,
    attn_gain_out, ffn_gain_out, query_gain_out, key_gain_out,
    gate_held, up_held, down_held, sems,
):
    through = [
        (gate_grads, gate_held, gate_out),
        (up_grads, up_held, up_out),
        (down_grads, down_held, down_out),
    ]
    parts = 2
    pairs = []
    for src, held, dst in through:
        rows = src.shape[0] // parts
        for k in range(parts):
            at = pl.ds(k * rows, rows)
            index = 2 * len(pairs)
            pairs.append(
                (
                    pltpu.make_async_copy(src.at[at], held.at[at], sems.at[index]),
                    pltpu.make_async_copy(held.at[at], dst.at[at], sems.at[index + 1]),
                )
            )
    straight = [(mixed, mixed_out), (tokens_grad, tokens_out)]
    first = 0
    for dst in (out_out, query_out, key_out, value_out):
        straight.append((attn_grads.at[:, pl.ds(first, dst.shape[1])], dst))
        first += dst.shape[1]
    straight = [
        pltpu.make_async_copy(src, dst, sems.at[2 * len(pairs) + k])
        for k, (src, dst) in enumerate(straight)
    ]
    for load, _ in pairs:
        load.start()
    for copy in straight:
        copy.start()
    attn_gain_out[...] = gains[0:1, :]
    ffn_gain_out[...] = gains[1:2, :]
    query_gain_out[...] = gains[2:3, : sz.head_width]
    key_gain_out[...] = gains[2:3, sz.head_width : 2 * sz.head_width]
    for load, store in pairs:
        load.wait()
        store.start()
    for copy in straight:
        copy.wait()
    for _, store in pairs:
        store.wait()


def over_groups(sz, dp_size, values):
    step = sz.group
    while step < dp_size:
        values = values + lax.ppermute(values, "dp", [(d, d ^ step) for d in range(dp_size)])
        step *= 2
    return values


def per_device(
    dp_size,
    tokens,
    segments,
    positions,
    attn_gain,
    w_query,
    key_weight,
    value_weight,
    query_gain,
    key_gain,
    w_out,
    ffn_gain,
    w_gate,
    w_up,
    w_down,
    cotangent,
):
    sz = Sizes(dp_size, tokens.shape, w_query.shape, key_weight.shape, query_gain.shape, w_gate.shape)
    rows, width, head_width, half = sz.rows, sz.width, sz.head_width, sz.half
    q_cols, k_cols = sz.q_cols, sz.k_cols
    lanes = np.arange(head_width) % (head_width // 2)
    inverse = (THETA ** (-2.0 * lanes / head_width)).astype(np.float32)[None]
    vmem = pl.BlockSpec(memory_space=pltpu.VMEM)
    anywhere = pl.BlockSpec(memory_space=pl.ANY)
    slots = 2 * half
    transfers = 256
    mixed, tokens_grad, gains, attn_grads, gate_grads, up_grads, down_grads, _, _ = pl.pallas_call(
        functools.partial(layer_kernel, sz),
        out_shape=[
            pltpu.VMEM((rows, width), BF16),
            pltpu.VMEM((rows, width), BF16),
            pltpu.VMEM((8, width), F32),
            pltpu.VMEM((width, sz.grad_cols), F32),
            shaped(*w_gate.shape),
            shaped(*w_up.shape),
            shaped(*w_down.shape),
            shaped(2, slots, rows, width),
            shaped(2, slots, rows, width),
        ],
        in_specs=[vmem] * 9 + [anywhere] * 7,
        out_specs=[vmem] * 4 + [anywhere] * 5,
        scratch_shapes=[
            pltpu.VMEM((2, rows, width), F32),
            pltpu.VMEM((3, rows + 8, width), F32),
            pltpu.VMEM((4, rows + 8, width), F32),
            pltpu.VMEM((rows, width), F32),
            pltpu.VMEM((rows, width), F32),
            pltpu.VMEM((rows, q_cols // 2), F32),
            pltpu.VMEM((rows, width // 2), F32),
            pltpu.VMEM((rows, width), F32),
            pltpu.VMEM((rows, sz.all_cols), F32),
            pltpu.VMEM((half, sz.piece, sz.grad_cols), F32),
            pltpu.VMEM((half, sz.piece, sz.grad_cols), F32),
            pltpu.VMEM((8, width), F32),
            pltpu.VMEM((8, width), F32),
            pltpu.VMEM((sz.chips, 8, width), F32),
            pltpu.VMEM((rows, width), BF16),
            pltpu.SemaphoreType.DMA((transfers,)),
            pltpu.SemaphoreType.DMA((transfers,)),
            pltpu.SemaphoreType.DMA((16,)),
        ],
        compiler_params=pltpu.CompilerParams(
            collective_id=0, has_side_effects=True, vmem_limit_bytes=VMEM_BYTES
        ),
    )(
        tokens, cotangent, segments, positions, jnp.asarray(inverse), attn_gain[None], query_gain[None], key_gain[None],
        ffn_gain[None], w_query, key_weight, value_weight, w_out, w_gate, w_up, w_down,
    )
    gains, attn_grads, gate_grads, up_grads, down_grads = [
        over_groups(sz, dp_size, v) for v in (gains, attn_grads, gate_grads, up_grads, down_grads)
    ]
    def in_vmem(values):
        return pltpu.with_memory_space_constraint(values, pltpu.VMEM)

    (
        mixed, tokens_grad, w_out_grad, w_query_grad, w_key_grad, w_value_grad,
        w_gate_grad, w_up_grad, w_down_grad,
        attn_gain_grad, ffn_gain_grad, query_gain_grad, key_gain_grad,
    ) = pl.pallas_call(
        functools.partial(results_kernel, sz),
        out_shape=[
            shaped(rows, width, kind=BF16),
            shaped(rows, width, kind=BF16),
            shaped(*w_out.shape),
            shaped(*w_query.shape),
            shaped(*key_weight.shape),
            shaped(*value_weight.shape),
            shaped(*w_gate.shape),
            shaped(*w_up.shape),
            shaped(*w_down.shape),
            shaped(1, width),
            shaped(1, width),
            shaped(1, head_width),
            shaped(1, head_width),
        ],
        in_specs=[anywhere, anywhere, vmem] + [anywhere] * 4,
        out_specs=[anywhere] * 9 + [vmem] * 4,
        scratch_shapes=[
            pltpu.VMEM(w_gate.shape, F32),
            pltpu.VMEM(w_up.shape, F32),
            pltpu.VMEM(w_down.shape, F32),
            pltpu.SemaphoreType.DMA((24,)),
        ],
        compiler_params=pltpu.CompilerParams(vmem_limit_bytes=RESULTS_VMEM_BYTES),
    )(
        in_vmem(mixed), in_vmem(tokens_grad), gains, in_vmem(attn_grads),
        gate_grads, up_grads, down_grads,
    )
    return (
        mixed,
        tokens_grad,
        attn_gain_grad[0],
        w_query_grad,
        w_key_grad,
        w_value_grad,
        query_gain_grad[0],
        key_gain_grad[0],
        w_out_grad,
        ffn_gain_grad[0],
        w_gate_grad,
        w_up_grad,
        w_down_grad,
    )


def solution(mesh):
    def layer(*arrays):
        return per_device(mesh.shape["dp"], *arrays)

    return jax.shard_map(
        layer,
        mesh=mesh,
        in_specs=(
            P("dp", None),
            P("dp", None),
            P("dp", None),
            P(),
            P(None, "tensor"),
            P(None, "tensor"),
            P(None, "tensor"),
            P(),
            P(),
            P("tensor", None),
            P(),
            P(None, "tensor"),
            P(None, "tensor"),
            P("tensor", None),
            P("dp", None),
        ),
        out_specs=(
            P("dp", None),
            P("dp", None),
            P(),
            P(None, "tensor"),
            P(None, "tensor"),
            P(None, "tensor"),
            P(),
            P(),
            P("tensor", None),
            P(),
            P(None, "tensor"),
            P(None, "tensor"),
            P("tensor", None),
        ),
        check_vma=False,
    )
```

```python
import functools
import math

import jax
import jax.numpy as jnp
import numpy as np
from jax import lax
from jax.experimental import pallas as pl
from jax.experimental.pallas import tpu as pltpu
from jax.sharding import PartitionSpec as P

EPS = 1e-06
THETA = 1000000.0
F32 = jnp.float32
BF16 = jnp.bfloat16
MESH = pl.DeviceIdType.MESH
VMEM_BYTES = 32 * 2**20
RESULTS_VMEM_BYTES = 4 * 2**20
GROUP = 16
COT, FFN = 0, 1


PLAN = {
    "A2": [
        ("ring", COT, 1),
        ("start", "x", COT, 1),
    ],
    "A4": [
        ("ring", COT, 2),
    ],
    "A5": [
        ("x_done", COT, 1),
        ("ring", FFN, 1),
    ],
    "A6": [
        ("ring", COT, 3),
        ("start", "x", COT, 2),
        ("start", "x", COT, 3),
    ],
    "A8": [
        ("x_done", COT, 2),
        ("start", "x", COT, 4),
    ],
    (0, 0): [
        ("ring", FFN, 2),
        ("x_done", COT, 3),
        ("start", "x", FFN, 1),
    ],
    (1, 1): [
        ("x_done", COT, 4),
        ("start", "x", FFN, 2),
    ],
    (2, 0): [
        ("ring", COT, 4),
    ],
    (2, 2): [
        ("sum", 0, 1),
        ("sum", 1, 1),
        ("x_done", FFN, 1),
        ("start", "x", COT, 5),
        ("stage", 1),
    ],
    (4, 1): [
        ("ring", FFN, 3),
        ("x_done", FFN, 2),
        ("start", "x", COT, 6),
    ],
    (5, 1): [
        ("stage", 2),
    ],
    (6, 0): [
        ("x_done", COT, 5),
        ("start", "x", FFN, 3),
    ],
    (6, 1): [
        ("sum", 0, 2),
    ],
    (7, 1): [
        ("x_done", COT, 6),
        ("start", "x", FFN, 4),
    ],
    (8, 2): [
        ("sum", 1, 2),
        ("ring", FFN, 4),
        ("x_done", FFN, 3),
        ("start", "x", FFN, 5),
        ("stage", 3),
    ],
    (9, 1): [
        ("sum", 0, 3),
    ],
    (10, 1): [
        ("x_done", FFN, 4),
        ("start", "x", FFN, 6),
    ],
    (11, 1): [
        ("stage", 4),
    ],
    (12, 0): [
        ("sum", 1, 3),
    ],
    (13, 1): [
        ("x_done", FFN, 5),
        ("start", "x", COT, 7),
    ],
    (14, 0): [
        ("sum", 0, 4),
    ],
    (14, 1): [
        ("stage", 5),
    ],
    (16, 0): [
        ("sum", 1, 4),
        ("x_done", FFN, 6),
        ("start", "x", FFN, 7),
    ],
    (17, 0): [
        ("stage", 6),
    ],
    (17, 1): [
        ("x_done", COT, 7),
        ("start", "part", 2),
    ],
    (18, 0): [
        ("gather", 0, 1),
    ],
    (20, 1): [
        ("gather", 1, 1),
    ],
    (20, 2): [
        ("x_done", FFN, 7),
        ("start", "part", 3),
        ("stage", 7),
    ],
    (21, 0): [
        ("gather", 0, 2),
    ],
    (23, 1): [
        ("gather", 1, 2),
    ],
    (24, 0): [
        ("tokens",),
        ("gather", 0, 3),
        ("gather", 1, 3),
        ("gain", 0),
        ("gather", 0, 4),
        ("gather", 1, 4),
        ("gain", 1),
        ("gain", 2),
        ("gain", 3),
        ("mixed",),
        ("gain", 4),
    ],
}


def norm_factor(values):
    return lax.rsqrt(jnp.mean(values * values, axis=-1, keepdims=True) + EPS)


def norm_grad(grad_out, unit_rows, factor, scale_gain):
    scaled = grad_out * scale_gain
    return factor * (scaled - unit_rows * jnp.mean(scaled * unit_rows, axis=-1, keepdims=True))


def rows_dot(leading, trailing):
    return jnp.dot(leading, trailing, preferred_element_type=F32)


def across_rows(leading, trailing):
    return lax.dot_general(
        leading, trailing, (((0,), (0,)), ((), ())), preferred_element_type=F32
    )


def against_rows(leading, trailing):
    return lax.dot_general(
        leading, trailing, (((1,), (1,)), ((), ())), preferred_element_type=F32
    )


def ffn_middle(low_in, cot, wg, wu, wd):
    gate = rows_dot(low_in, wg)
    up = rows_dot(low_in, wu)
    sig = jax.nn.sigmoid(gate)
    silu = gate * sig
    hidden = (silu * up).astype(BF16)
    hidden_grad = against_rows(cot, wd)
    up_grad = (hidden_grad * silu).astype(BF16)
    gate_grad = (hidden_grad * up * sig * (1.0 + gate * (1.0 - sig))).astype(BF16)
    return hidden, gate_grad, up_grad


def shaped(*shape, kind=F32):
    return jax.ShapeDtypeStruct(shape, kind)


class Sizes:
    def __init__(self, dp_size, tokens, w_query, key_weight, query_gain, w_gate):
        self.rows, self.width = tokens
        self.head_width = query_gain[0]
        self.q_cols, self.k_cols = w_query[1], key_weight[1]
        self.heads, self.kv_heads = self.q_cols // self.head_width, self.k_cols // self.head_width
        self.units = w_gate[1]
        self.all_cols = self.q_cols + 2 * self.k_cols
        self.scale = 1.0 / math.sqrt(self.head_width)
        self.group = math.gcd(GROUP, dp_size)
        self.chips = self.group // 2
        self.half = self.chips // 2
        self.share = (self.width // 4, self.width // 2)
        self.grad_rows = self.width // 2
        self.grad_cols = self.width + self.all_cols
        self.piece = self.grad_rows // self.chips
        self.streams = 2


def layer_kernel(
    sz,
    tokens, cot, segments, positions, inverse, attn_gain, query_gain, key_gain, ffn_gain,
    w_query, key_weight, value_weight, w_out, w_gate, w_up, w_down,
    mixed, tokens_grad, gains, attn_grads, gate_grads, up_grads, down_grads,
    mine, theirs,
    part, part_theirs, middle_grad, sum_up, sum_down, gain_send, gain_recv, gain_slots,
    send_sems, recv_sems, local_sems,
):
    rows, width, head_width = sz.rows, sz.width, sz.head_width
    q_cols, k_cols, units = sz.q_cols, sz.k_cols, sz.units
    n, half, piece = sz.chips, sz.half, sz.piece
    half_units = units // 2
    mid = rows // 2

    device = lax.axis_index("dp")
    base = device // sz.group * sz.group
    core = device % 2
    chip = device % sz.group // 2
    line = chip % 2
    place = chip // 2 + line * (2 * half - 1 - 2 * (chip // 2))
    side = lax.axis_index("tensor")

    def device_at(position):
        position = position % n
        second = position // half
        return base + (2 * (position + second * (2 * half - 1 - 2 * position)) + second) * 2 + core

    forward = {"dp": device_at(place + 1)}
    backward = {"dp": device_at(place + n - 1)}
    sibling = {"dp": base + chip * 2 + 1 - core}
    across = {"tensor": 1 - side}

    barrier = pltpu.get_barrier_semaphore()
    for neighbour in (forward, backward, sibling, across):
        pl.semaphore_signal(barrier, inc=1, device_id=neighbour, device_id_type=MESH)
    pl.semaphore_wait(barrier, 4)

    book = {}
    waited = set()

    def remote(name, src, dst, target):
        book[name] = (len(book), src, dst, target)

    def made(name):
        index, src, dst, target = book[name]
        return pltpu.make_async_remote_copy(
            src_ref=src, dst_ref=dst, send_sem=send_sems.at[index], recv_sem=recv_sems.at[index],
            device_id=target, device_id_type=MESH,
        )

    def sent(*names):
        for name in names:
            made(name).wait_send()
            waited.add(name)

    def start(*names):
        for name in names:
            made(name).start()

    def arrived(*names):
        for name in names:
            made(name).wait_recv()

    def cols(first, count):
        return pl.ds(pl.multiple_of(first, 128), count)

    def piece_rows(index, first=0, count=piece, base_row=0):
        return pl.ds(pl.multiple_of(base_row + index % n * piece + first, 8), count)

    grad_base = core * sz.grad_rows
    slots = 2 * half
    up_slot = lambda h: 2 * h - 1
    down_slot = lambda h: 2 * h
    last = slots - 1
    up_place = lambda row, first, count: up_grads.at[pl.ds(row * rows, rows), pl.ds(first, count)]
    down_place = lambda row: down_grads.at[pl.ds(row * rows, rows)]
    half_width = width // 2
    gate_place = lambda row: gate_grads.at[pl.ds(row * rows, rows), pl.ds(units - width, width)]
    own = (gate_place(0), gate_place(1))
    for a, share in zip((COT, FFN), sz.share):
        window = cols(side * share, width - share)
        shared = cols(side * (width - share), share)
        for h in range(1, half):
            src = own[a] if h == 1 else mine.at[a, up_slot(h - 1)]
            remote(("up", a, h), src.at[:, window], mine.at[a, up_slot(h), :, window], forward)
            src = own[a] if h == 1 else mine.at[a, down_slot(h - 1)]
            remote(("down", a, h), src.at[:, window], mine.at[a, down_slot(h), :, window], backward)
        remote(
            ("up", a, half), mine.at[a, up_slot(half - 1), pl.ds(0, mid), window],
            mine.at[a, last, pl.ds(0, mid), window], forward,
        )
        remote(
            ("down", a, half), mine.at[a, down_slot(half - 1), pl.ds(mid, mid), window],
            mine.at[a, last, pl.ds(mid, mid), window], backward,
        )
        for s in range(1, slots):
            remote(("x", a, s), mine.at[a, s, :, shared], mine.at[a, s, :, shared], across)
        for s in range(slots):
            remote(("core", a, s), own[a] if s == 0 else mine.at[a, s], theirs.at[a, s], sibling)
    for k in range(4):
        remote(("part", k), part.at[(0, 1, 1, 0)[k]], part_theirs.at[k % 2], across)
    stream_cols = sz.grad_cols // sz.streams
    small = piece // 2
    for s in range(sz.streams):
        c = pl.ds(s * stream_cols, stream_cols)
        for h in range(1, half + 1):
            size, skip = (small, small) if h == 1 else (piece, 0)
            src = attn_grads.at[piece_rows(place + half, 0, small, grad_base), c]
            remote(
                ("su", s, h), src if h == 1 else sum_up.at[h - 2, :, c],
                sum_up.at[h - 1, pl.ds(0, size), c], forward,
            )
            src = attn_grads.at[piece_rows(place + half, small, small, grad_base), c]
            remote(
                ("sd", s, h), src if h == 1 else sum_down.at[h - 2, :, c],
                sum_down.at[h - 1, pl.ds(skip, size), c], backward,
            )
        for h in range(1, half + 1):
            size, skip = (small, small) if h == half else (piece, 0)
            going_up = attn_grads.at[piece_rows(place + n - h + 1, 0, size, grad_base), c]
            going_down = attn_grads.at[piece_rows(place + h - 1, skip, size, grad_base), c]
            remote(("gu", s, h), going_up, going_up, forward)
            remote(("gd", s, h), going_down, going_down, backward)
            got_up = attn_grads.at[piece_rows(place + n - h, 0, size, grad_base), c]
            got_down = attn_grads.at[piece_rows(place + h, skip, size, grad_base), c]
            remote(("cu", s, h), got_up, got_up, sibling)
            remote(("cd", s, h), got_down, got_down, sibling)
        own_piece = attn_grads.at[piece_rows(place, 0, piece, grad_base), c]
        remote(("cu", s, 0), own_piece, own_piece, sibling)
    remote("gains", gain_send, gain_recv, sibling)
    for h in range(1, half + 1):
        slot = gain_slots.at[(place + n - h + 1) % n]
        remote(("vu", h), slot, slot, forward)
        if h < half:
            slot = gain_slots.at[(place + h - 1) % n]
            remote(("vd", h), slot, slot, backward)

    def ring_step(a, h):
        arrived(("up", a, h), ("down", a, h))
        if h < half:
            start(("up", a, h + 1), ("down", a, h + 1))

    def x_start(a, s):
        start(("x", a, s))

    def x_done(a, s):
        arrived(("x", a, s))
        start(("core", a, s))


    def stream(s):
        return pl.ds(s * stream_cols, stream_cols)

    def sum_step(s, h):
        arrived(("su", s, h), ("sd", s, h))
        c = stream(s)
        up_rows = piece_rows(place + half - h, 0, piece, grad_base)
        down_rows = piece_rows(place + n - half + h, 0, piece, grad_base)
        if h == 1:
            sent(("su", s, 1), ("sd", s, 1))
            up, down = attn_grads[up_rows, c], attn_grads[down_rows, c]
            sum_up[0, :small, c] += up[:small]
            sum_up[0, small:, c] = up[small:]
            sum_down[0, :small, c] = down[:small]
            sum_down[0, small:, c] += down[small:]
        elif h < half:
            sum_up[h - 1, :, c] += attn_grads[up_rows, c]
            sum_down[h - 1, :, c] += attn_grads[down_rows, c]
        if h < half:
            start(("su", s, h + 1), ("sd", s, h + 1))
        else:
            own_rows = piece_rows(place, 0, piece, grad_base)
            attn_grads[own_rows, c] += sum_up[h - 1, :, c] + sum_down[h - 1, :, c]
            start(("gu", s, 1), ("gd", s, 1), ("cu", s, 0))

    def gather_step(s, h):
        arrived(("gu", s, h), ("gd", s, h))
        if h < half:
            start(("gu", s, h + 1), ("gd", s, h + 1))
        start(("cu", s, h), ("cd", s, h))

    def finish_tokens():
        arrived(("part", 2))
        grad = part[1, :rows] + part_theirs[0, :rows]
        value = tokens[...].astype(F32)
        factor = norm_factor(value)
        unit = value * factor
        tokens_grad[...] = (
            middle_grad[...] + norm_grad(grad, unit, factor, attn_gain[...])
        ).astype(BF16)
        gain_send[0:1, :] = jnp.sum(grad * unit, axis=0, keepdims=True)
        gain_send[2:, :] = part[1, rows : rows + 6] + part_theirs[0, rows : rows + 6]
        start("gains")

    def finish_mixed():
        arrived(("part", 3))
        mixed[...] = (part[0, :rows] + part_theirs[1, :rows]).astype(BF16)

    def gain_first():
        arrived("gains")
        gain_slots[place] = gain_send[...] + gain_recv[...]
        start(("vu", 1), ("vd", 1))

    def gain_step(h):
        arrived(("vu", h))
        if h < half:
            arrived(("vd", h))
            start(("vu", h + 1))
            if h + 1 < half:
                start(("vd", h + 1))
        else:
            total = gain_slots[0]
            for chip_at in range(1, n):
                total = total + gain_slots[chip_at]
            gains[...] = total

    def stage(slot):
        arrived(("core", COT, slot), ("core", FFN, slot))
        for copy in stage_copies(slot, False):
            copy.start()

    scoped = {}

    def stage_copies(slot, first):
        staged = scoped["staged"]
        copies = []
        for a in (COT, FFN):
            src = own[a] if first else mine.at[a, slot]
            copies.append(pltpu.make_async_copy(src, staged.at[a, 0], local_sems.at[9 + 2 * a]))
            copies.append(
                pltpu.make_async_copy(theirs.at[a, slot], staged.at[a, 1], local_sems.at[10 + 2 * a])
            )
        return copies

    def gain_event(h):
        if h == 0:
            gain_first()
        else:
            gain_step(h)

    actions = {
        "ring": ring_step,
        "start": lambda *name: start(name),
        "x_done": x_done,
        "sum": sum_step,
        "gather": gather_step,
        "stage": stage,
        "tokens": finish_tokens,
        "gain": gain_event,
        "mixed": finish_mixed,
    }

    def run(when):
        for event in PLAN.get(when, ()):
            actions[event[0]](*event[1:])

    group = q_cols // k_cols
    other_half = lambda count: cols((1 - core) * count, count)
    own_half = lambda count: cols(core * count, count)

    block = k_cols
    q_blocks, unit_blocks = q_cols // block, units // block
    at_k, at_v, at_o = q_blocks, q_blocks + 1, q_blocks + 2

    half_down = down_grads.at[pl.ds(pl.multiple_of(core * half_units, 8), half_units)]
    outs = (gate_grads.at[:, own_half(half_units)], up_grads.at[:, own_half(half_units)], half_down)
    for k, out in enumerate(outs):
        remote(("out", k), out, out, sibling)

    q_lin, k_lin = up_place(0, 0, q_cols), up_place(0, q_cols, k_cols)
    ctx_send, ctx_recv = up_place(1, 0, q_cols // 2), up_place(1, q_cols // 2, q_cols // 2)
    cosine, sine = up_place(1, q_cols, head_width), up_place(1, q_cols + head_width, head_width)
    attn_send, attn_recv = up_place(2, 0, half_width), up_place(2, half_width, half_width)
    mask = up_place(3, 0, rows)
    lows, low_recvs = (down_place(0), down_place(1)), (down_place(2), down_place(3))
    branch, branch_recv = down_place(4), down_place(5)
    deep = width // rows
    middle = gate_place(2)

    def probs_of(head):
        return gate_grads.at[pl.ds(head % deep * rows, rows), pl.ds(head // deep * rows, rows)]

    remote("ctx", ctx_send, ctx_recv, sibling)
    remote("attn", attn_send, attn_recv, sibling)
    remote("branch", branch, branch_recv, sibling)
    for k in range(2):
        remote(("low", k), lows[k], low_recvs[k], sibling)

    def first_phase(bank, wd, q_low, k_low, v_low, context, ffn_low, hidden, context_grad, attn_low):
        def load(src, dst, index):
            copy = pltpu.make_async_copy(src, dst, local_sems.at[index])
            copy.start()
            return copy

        def block_of(weights, index):
            return weights.at[:, pl.ds(index * block, block)]

        def load_attention():
            order = [(w_query, i) for i in range(q_blocks)] + [(key_weight, 0), (value_weight, 0)]
            order += [(w_out, i) for i in range(width // block)]
            return [load(block_of(w, i), bank.at[k], k) for k, (w, i) in enumerate(order)]

        def load_ffn():
            order = [(w, i) for w in (w_gate, w_up) for i in range(unit_blocks)]
            return [load(block_of(w, i), bank.at[k], k) for k, (w, i) in enumerate(order)]

        loads = load_attention()
        down_load = load(w_down, wd, 15)

        def head_norm(lin, gain):
            return lin * norm_factor(lin) * gain[...]

        def turned(lin, gain):
            normed = head_norm(lin, gain)
            swapped = pltpu.roll(normed, head_width // 2, 1)
            return (normed * cosine[...] + swapped * sine[...]).astype(BF16)

        def turned_back(grad, lin, gain):
            back = grad * cosine[...] - pltpu.roll(grad, head_width // 2, 1) * sine[...]
            factor = norm_factor(lin)
            unit = lin * factor
            return (
                norm_grad(back, unit, factor, gain[...]).astype(BF16),
                jnp.sum(back * unit, axis=0, keepdims=True),
            )

        own[COT][...] = cot[...].astype(F32)
        start(("up", COT, 1), ("down", COT, 1), ("core", COT, 0))

        resid = tokens[...].astype(F32)
        attn_in = (resid * norm_factor(resid) * attn_gain[...]).astype(BF16)
        attn_low[...] = attn_in
        attn_send[...] = attn_low[:, other_half(width // 2)].astype(F32)
        start("attn")

        def down_rows(row):
            return jnp.broadcast_to(row.astype(F32), (head_width, rows)).T

        segment_rows = jnp.concatenate([down_rows(segments[...])] * (rows // head_width), 1)
        same = segment_rows == jnp.broadcast_to(segments[...].astype(F32), (rows, rows))
        row_at = lax.broadcasted_iota(jnp.int32, (rows, rows), 0)
        column_at = lax.broadcasted_iota(jnp.int32, (rows, rows), 1)
        mask[...] = jnp.where(same & (row_at >= column_at), 1.0, 0.0)
        angles = down_rows(positions[...]) * inverse[...]
        lane = lax.broadcasted_iota(jnp.int32, (rows, head_width), 1)
        cosine[...] = jnp.cos(angles)
        sine[...] = jnp.where(lane < head_width // 2, -1.0, 1.0) * jnp.sin(angles)
        for i in range(q_blocks):
            loads[i].wait()
            q_lin[:, i * block : (i + 1) * block] = rows_dot(attn_in, bank[i])
        loads[at_k].wait()
        k_lin[...] = rows_dot(attn_in, bank[at_k])
        loads[at_v].wait()
        v_low[...] = rows_dot(attn_in, bank[at_v]).astype(BF16)
        run("A1")
        for kv in range(sz.kv_heads):
            kv_at = slice(kv * head_width, (kv + 1) * head_width)
            keys = turned(k_lin[:, kv_at], key_gain)
            k_low[:, kv_at] = keys
            values = v_low[:, kv_at]
            for member in range(group):
                head = kv * group + member
                at = slice(head * head_width, (head + 1) * head_width)
                queries = turned(q_lin[:, at], query_gain)
                q_low[:, at] = queries
                scores = jnp.where(mask[...] > 0, against_rows(queries, keys) * sz.scale, -1e30)
                raised = jnp.exp(scores - jnp.max(scores, axis=-1, keepdims=True))
                prob = raised / jnp.sum(raised, axis=-1, keepdims=True)
                probs_of(head)[...] = prob
                context[:, at] = rows_dot(prob.astype(BF16), values).astype(BF16)
        for i in range(width // block):
            loads[at_o + i].wait()
            part[0, :rows, i * block : (i + 1) * block] = rows_dot(context[...], bank[at_o + i])
        part[0, rows:] = jnp.zeros((8, width), F32)
        start(("part", 0))
        ctx_send[...] = context[:, other_half(q_cols // 2)].astype(F32)
        start("ctx")
        loads = load_ffn()
        run("A2")

        arrived(("part", 0))
        value = tokens[...].astype(F32) + (part[0, :rows] + part_theirs[0, :rows])
        middle[...] = value
        ffn_low[...] = (value * norm_factor(value) * ffn_gain[...]).astype(BF16)
        own[FFN][...] = ffn_low[...].astype(F32)
        start(("up", FFN, 1), ("down", FFN, 1), ("core", FFN, 0))
        run("A3")
        down_load.wait()
        for i in range(unit_blocks):
            at = slice(i * block, (i + 1) * block)
            loads[i].wait()
            loads[unit_blocks + i].wait()
            wg, wu = bank[i], bank[unit_blocks + i]
            low_hidden, gate_grad, up_grad = ffn_middle(ffn_low[...], cot[...], wg, wu, wd[at])
            hidden[:, at] = low_hidden
            term = against_rows(gate_grad, wg) + against_rows(up_grad, wu)
            if i == 0:
                part[1, :rows] = term
            else:
                part[1, :rows] += term
        part[1, rows:] = jnp.zeros((8, width), F32)
        start(("part", 1))
        loads = load_attention()
        run("A4")
        sent(("part", 0))
        part[0, :rows] = rows_dot(hidden[...], wd[...]) + 0.5 * middle[...]
        run("A5")

        arrived(("part", 1))
        grad = part[1, :rows] + part_theirs[1, :rows]
        value = middle[...]
        factor = norm_factor(value)
        unit = value * factor
        total = cot[...].astype(F32) + norm_grad(grad, unit, factor, ffn_gain[...])
        middle_grad[...] = total
        branch_low = total.astype(BF16)
        branch[...] = branch_low.astype(F32)
        start("branch")
        gain_send[1:2, :] = jnp.sum(grad * unit, axis=0, keepdims=True)
        run("A6")
        for load_of in loads:
            load_of.wait()
        context_grad[...] = sum(
            against_rows(branch_low[:, i * block : (i + 1) * block], bank[at_o + i])
            for i in range(width // block)
        ).astype(BF16)
        q_total = jnp.zeros((1, head_width), F32)
        k_total = jnp.zeros((1, head_width), F32)
        for kv in range(sz.kv_heads):
            kv_at = slice(kv * head_width, (kv + 1) * head_width)
            keys, values = k_low[:, kv_at], v_low[:, kv_at]
            keys_grad = values_grad = 0.0
            for member in range(group):
                head = kv * group + member
                at = slice(head * head_width, (head + 1) * head_width)
                head_grad = context_grad[:, at]
                prob = probs_of(head)[...]
                prob_grad = against_rows(head_grad, values)
                values_grad += across_rows(prob.astype(BF16), head_grad)
                inner = jnp.sum(prob * prob_grad, axis=-1, keepdims=True)
                score_grad = (prob * (prob_grad - inner)).astype(BF16)
                queries_grad = rows_dot(score_grad, keys) * sz.scale
                keys_grad += across_rows(score_grad, q_low[:, at])
                head_low, head_total = turned_back(queries_grad, q_lin[:, at], query_gain)
                lows[0][:, at] = head_low.astype(F32)
                q_total += head_total
            head_low, head_total = turned_back(keys_grad * sz.scale, k_lin[:, kv_at], key_gain)
            k_total += head_total
            lows[1][:, kv_at] = head_low.astype(F32)
            at = k_cols + kv * head_width
            lows[1][:, at : at + head_width] = values_grad.astype(BF16).astype(F32)
        start(("low", 0), ("low", 1))
        run("A7")
        half_rows = pl.ds(pl.multiple_of(grad_base, 8), sz.grad_rows)
        arrived("ctx", "branch")
        for i in range(width // block):
            at = slice(i * block, (i + 1) * block)
            attn_grads[half_rows, at] = across_rows(
                context[:, own_half(q_cols // 2)], branch[:, at].astype(BF16)
            ) + across_rows(ctx_recv[...].astype(BF16), branch_recv[:, at].astype(BF16))
        arrived("attn", ("low", 0), ("low", 1))
        for k in range(2):
            for i in range(width // block):
                at = slice(i * block, (i + 1) * block)
                first = (k + 1) * width + i * block
                attn_grads[half_rows, first : first + block] = across_rows(
                    attn_low[:, own_half(width // 2)], lows[k][:, at].astype(BF16)
                ) + across_rows(attn_recv[...].astype(BF16), low_recvs[k][:, at].astype(BF16))
        for s in range(sz.streams):
            start(("su", s, 1), ("sd", s, 1))
        sent(("part", 1))
        part[1, :rows] = sum(
            against_rows(
                lows[i // q_blocks][:, i % q_blocks * block : (i % q_blocks + 1) * block].astype(BF16),
                bank[i],
            )
            for i in range(at_o)
        )
        part[1, rows:] = jnp.zeros((8, width), F32)
        part[1, rows : rows + 1, :head_width] = q_total
        part[1, rows : rows + 1, head_width : 2 * head_width] = k_total
        run("A8")
        sent("ctx", "attn", "branch", ("low", 0), ("low", 1))

    pl.run_scoped(
        first_phase,
        pltpu.VMEM((max(at_o + width // block, 2 * unit_blocks), width, block), BF16),
        pltpu.VMEM(w_down.shape, BF16),
        pltpu.VMEM((rows, q_cols), BF16),
        pltpu.VMEM((rows, k_cols), BF16),
        pltpu.VMEM((rows, k_cols), BF16),
        pltpu.VMEM((rows, q_cols), BF16),
        pltpu.VMEM((rows, width), BF16),
        pltpu.VMEM((rows, units), BF16),
        pltpu.VMEM((rows, q_cols), BF16),
        pltpu.VMEM((rows, width), BF16),
    )

    def second_phase(
        wg, wu, wd, staged, ffn_low, ffn_turned, cot_low
    ):
        scoped["staged"] = staged
        weight_loads = [
            pltpu.make_async_copy(src, dst, local_sems.at[i])
            for i, (src, dst) in enumerate(
                (
                    (w_gate.at[:, own_half(half_units)], wg),
                    (w_up.at[:, own_half(half_units)], wu),
                    (w_down.at[pl.ds(pl.multiple_of(core * half_units, 8), half_units)], wd),
                )
            )
        ]
        for load in weight_loads:
            load.start()

        for a in (COT, FFN):
            sent(("up", a, 1), ("down", a, 1), ("core", a, 0))
        arrived(("core", COT, 0), ("core", FFN, 0))
        for copy in stage_copies(0, True):
            copy.start()
        for load in weight_loads:
            load.wait()
        chunks = 3
        size = half_units // chunks
        def step(i, _):
            slot, j = i // chunks, i % chunks

            @pl.when(j == 0)
            def _():
                for copy in stage_copies(slot, False):
                    copy.wait()
                for lane in range(2):
                    here = pl.ds(lane * rows, rows)
                    low_block = staged[FFN, lane].astype(BF16)
                    ffn_low[here] = low_block
                    ffn_turned[:, lane * rows : (lane + 1) * rows] = low_block.T
                    cot_low[here] = staged[COT, lane].astype(BF16)

            def events(part_of_step):
                for when in PLAN:
                    if isinstance(when, tuple) and when[0] < chunks * slots and when[1] == part_of_step:

                        @pl.when(i == when[0])
                        def _():
                            run(when)

            events(0)
            at_units = pl.ds(pl.multiple_of(j * size, 128), size)
            hidden, gate_grad, up_grad = ffn_middle(
                ffn_low[...], cot_low[...], wg[:, at_units], wu[:, at_units], wd[at_units]
            )
            events(1)
            down = across_rows(hidden, cot_low[...])
            gate = rows_dot(ffn_turned[...], gate_grad)
            up = rows_dot(ffn_turned[...], up_grad)

            grad_units = core * half_units + j * size
            grad_cols = pl.ds(pl.multiple_of(grad_units, 128), size)

            @pl.when(slot == 0)
            def _():
                gate_grads[:, grad_cols] = gate
                up_grads[:, grad_cols] = up
                down_grads[grad_cols] = down

            @pl.when(slot > 0)
            def _():
                gate_grads[:, grad_cols] += gate
                up_grads[:, grad_cols] += up
                down_grads[grad_cols] += down

            events(2)
            return 0

        lax.fori_loop(0, chunks * slots, step, 0)
        for k in range(3):
            start(("out", k))
        run((chunks * slots, 0))
        for k in range(3):
            arrived(("out", k))

    pl.run_scoped(
        second_phase,
        pltpu.VMEM((width, half_units), BF16),
        pltpu.VMEM((width, half_units), BF16),
        pltpu.VMEM((half_units, width), BF16),
        pltpu.VMEM((2, 2, rows, width), F32),
        pltpu.VMEM((2 * rows, width), BF16),
        pltpu.VMEM((width, 2 * rows), BF16),
        pltpu.VMEM((2 * rows, width), BF16),
    )
    for s in range(sz.streams):
        for h in range(half + 1):
            arrived(("cu", s, h))
            if h:
                arrived(("cd", s, h))
    for name in book:
        if name not in waited:
            made(name).wait_send()


def results_kernel(
    sz,
    mixed, tokens_grad, gains, attn_grads, gate_grads, up_grads, down_grads,
    mixed_out, tokens_out, out_out, query_out, key_out, value_out, gate_out, up_out, down_out,
    attn_gain_out, ffn_gain_out, query_gain_out, key_gain_out,
    sems,
):
    moves = [(mixed, mixed_out), (tokens_grad, tokens_out)]
    moves += [(gate_grads, gate_out), (up_grads, up_out), (down_grads, down_out)]
    first = 0
    for dst in (out_out, query_out, key_out, value_out):
        moves.append((attn_grads.at[:, pl.ds(first, dst.shape[1])], dst))
        first += dst.shape[1]
    copies = [
        pltpu.make_async_copy(src, dst, sems.at[k]) for k, (src, dst) in enumerate(moves)
    ]
    for copy in copies:
        copy.start()
    attn_gain_out[...] = gains[0:1, :]
    ffn_gain_out[...] = gains[1:2, :]
    query_gain_out[...] = gains[2:3, : sz.head_width]
    key_gain_out[...] = gains[2:3, sz.head_width : 2 * sz.head_width]
    for copy in copies:
        copy.wait()


def over_groups(sz, dp_size, values):
    step = sz.group
    while step < dp_size:
        values = values + lax.ppermute(values, "dp", [(d, d ^ step) for d in range(dp_size)])
        step *= 2
    return values


def per_device(
    dp_size,
    tokens,
    segments,
    positions,
    attn_gain,
    w_query,
    key_weight,
    value_weight,
    query_gain,
    key_gain,
    w_out,
    ffn_gain,
    w_gate,
    w_up,
    w_down,
    cotangent,
):
    sz = Sizes(dp_size, tokens.shape, w_query.shape, key_weight.shape, query_gain.shape, w_gate.shape)
    rows, width, head_width, half = sz.rows, sz.width, sz.head_width, sz.half
    q_cols, k_cols = sz.q_cols, sz.k_cols
    lanes = np.arange(head_width) % (head_width // 2)
    inverse = (THETA ** (-2.0 * lanes / head_width)).astype(np.float32)[None]
    vmem = pl.BlockSpec(memory_space=pltpu.VMEM)
    anywhere = pl.BlockSpec(memory_space=pl.ANY)
    slots = 2 * half
    transfers = 256
    mixed, tokens_grad, gains, attn_grads, gate_grads, up_grads, down_grads, _, _ = pl.pallas_call(
        functools.partial(layer_kernel, sz),
        out_shape=[
            pltpu.VMEM((rows, width), BF16),
            pltpu.VMEM((rows, width), BF16),
            pltpu.VMEM((8, width), F32),
            pltpu.VMEM((width, sz.grad_cols), F32),
            pltpu.VMEM(w_gate.shape, F32),
            pltpu.VMEM(w_up.shape, F32),
            pltpu.VMEM(w_down.shape, F32),
            shaped(2, slots, rows, width),
            shaped(2, slots, rows, width),
        ],
        in_specs=[vmem] * 9 + [anywhere] * 7,
        out_specs=[vmem] * 7 + [anywhere] * 2,
        scratch_shapes=[
            pltpu.VMEM((2, rows + 8, width), F32),
            pltpu.VMEM((2, rows + 8, width), F32),
            pltpu.VMEM((rows, width), F32),
            pltpu.VMEM((half, sz.piece, sz.grad_cols), F32),
            pltpu.VMEM((half, sz.piece, sz.grad_cols), F32),
            pltpu.VMEM((8, width), F32),
            pltpu.VMEM((8, width), F32),
            pltpu.VMEM((sz.chips, 8, width), F32),
            pltpu.SemaphoreType.DMA((transfers,)),
            pltpu.SemaphoreType.DMA((transfers,)),
            pltpu.SemaphoreType.DMA((16,)),
        ],
        compiler_params=pltpu.CompilerParams(
            collective_id=0, has_side_effects=True, vmem_limit_bytes=VMEM_BYTES
        ),
    )(
        tokens, cotangent, segments, positions, jnp.asarray(inverse), attn_gain[None], query_gain[None], key_gain[None],
        ffn_gain[None], w_query, key_weight, value_weight, w_out, w_gate, w_up, w_down,
    )
    gains, attn_grads, gate_grads, up_grads, down_grads = [
        over_groups(sz, dp_size, v) for v in (gains, attn_grads, gate_grads, up_grads, down_grads)
    ]
    def in_vmem(values):
        return pltpu.with_memory_space_constraint(values, pltpu.VMEM)

    (
        mixed, tokens_grad, w_out_grad, w_query_grad, w_key_grad, w_value_grad,
        w_gate_grad, w_up_grad, w_down_grad,
        attn_gain_grad, ffn_gain_grad, query_gain_grad, key_gain_grad,
    ) = pl.pallas_call(
        functools.partial(results_kernel, sz),
        out_shape=[
            shaped(rows, width, kind=BF16),
            shaped(rows, width, kind=BF16),
            shaped(*w_out.shape),
            shaped(*w_query.shape),
            shaped(*key_weight.shape),
            shaped(*value_weight.shape),
            shaped(*w_gate.shape),
            shaped(*w_up.shape),
            shaped(*w_down.shape),
            shaped(1, width),
            shaped(1, width),
            shaped(1, head_width),
            shaped(1, head_width),
        ],
        in_specs=[anywhere, anywhere, vmem] + [anywhere] * 4,
        out_specs=[anywhere] * 9 + [vmem] * 4,
        scratch_shapes=[pltpu.SemaphoreType.DMA((9,))],
        compiler_params=pltpu.CompilerParams(vmem_limit_bytes=RESULTS_VMEM_BYTES),
    )(
        in_vmem(mixed), in_vmem(tokens_grad), gains, in_vmem(attn_grads),
        in_vmem(gate_grads), in_vmem(up_grads), in_vmem(down_grads),
    )
    return (
        mixed,
        tokens_grad,
        attn_gain_grad[0],
        w_query_grad,
        w_key_grad,
        w_value_grad,
        query_gain_grad[0],
        key_gain_grad[0],
        w_out_grad,
        ffn_gain_grad[0],
        w_gate_grad,
        w_up_grad,
        w_down_grad,
    )


def solution(mesh):
    def layer(*arrays):
        return per_device(mesh.shape["dp"], *arrays)

    return jax.shard_map(
        layer,
        mesh=mesh,
        in_specs=(
            P("dp", None),
            P("dp", None),
            P("dp", None),
            P(),
            P(None, "tensor"),
            P(None, "tensor"),
            P(None, "tensor"),
            P(),
            P(),
            P("tensor", None),
            P(),
            P(None, "tensor"),
            P(None, "tensor"),
            P("tensor", None),
            P("dp", None),
        ),
        out_specs=(
            P("dp", None),
            P("dp", None),
            P(),
            P(None, "tensor"),
            P(None, "tensor"),
            P(None, "tensor"),
            P(),
            P(),
            P("tensor", None),
            P(),
            P(None, "tensor"),
            P(None, "tensor"),
            P("tensor", None),
        ),
        check_vma=False,
    )
```

```python
import functools
import math

import jax
import jax.numpy as jnp
import numpy as np
from jax import lax
from jax.experimental import pallas as pl
from jax.experimental.pallas import tpu as pltpu
from jax.sharding import PartitionSpec as P

EPS = 1e-06
THETA = 1000000.0
F32 = jnp.float32
BF16 = jnp.bfloat16
MESH = pl.DeviceIdType.MESH
VMEM_BYTES = 32 * 2**20
RESULTS_VMEM_BYTES = 2**20
GROUP = 16
COT, FFN = 0, 1


PLAN = {
    "A2": [
        ("ring", COT, 1),
        ("start", "x", COT, 1),
    ],
    "A4": [
        ("ring", COT, 2),
    ],
    "A5": [
        ("x_done", COT, 1),
        ("ring", FFN, 1),
    ],
    "A6": [
        ("ring", COT, 3),
        ("start", "x", COT, 2),
        ("start", "x", COT, 3),
    ],
    "A8": [
        ("x_done", COT, 2),
        ("start", "x", COT, 4),
    ],
    (0, 0): [
        ("ring", FFN, 2),
        ("x_done", COT, 3),
        ("start", "x", FFN, 1),
    ],
    (1, 1): [
        ("x_done", COT, 4),
        ("start", "x", FFN, 2),
    ],
    (2, 0): [
        ("ring", COT, 4),
    ],
    (2, 2): [
        ("sum", 0, 1),
        ("sum", 1, 1),
        ("x_done", FFN, 1),
        ("start", "x", COT, 5),
        ("stage", 1),
    ],
    (4, 1): [
        ("ring", FFN, 3),
        ("x_done", FFN, 2),
        ("start", "x", COT, 6),
    ],
    (5, 1): [
        ("stage", 2),
    ],
    (6, 0): [
        ("x_done", COT, 5),
        ("start", "x", FFN, 3),
    ],
    (6, 1): [
        ("sum", 0, 2),
    ],
    (7, 1): [
        ("x_done", COT, 6),
        ("start", "x", FFN, 4),
    ],
    (8, 2): [
        ("sum", 1, 2),
        ("ring", FFN, 4),
        ("x_done", FFN, 3),
        ("start", "x", FFN, 5),
        ("stage", 3),
    ],
    (9, 1): [
        ("sum", 0, 3),
    ],
    (10, 1): [
        ("x_done", FFN, 4),
        ("start", "x", FFN, 6),
    ],
    (11, 1): [
        ("stage", 4),
    ],
    (12, 0): [
        ("sum", 1, 3),
    ],
    (13, 1): [
        ("x_done", FFN, 5),
        ("start", "x", COT, 7),
    ],
    (14, 0): [
        ("sum", 0, 4),
    ],
    (14, 1): [
        ("stage", 5),
    ],
    (16, 0): [
        ("sum", 1, 4),
        ("x_done", FFN, 6),
        ("start", "x", FFN, 7),
    ],
    (17, 0): [
        ("stage", 6),
    ],
    (17, 1): [
        ("x_done", COT, 7),
        ("start", "part", 2),
    ],
    (18, 0): [
        ("gather", 0, 1),
    ],
    (20, 1): [
        ("gather", 1, 1),
    ],
    (20, 2): [
        ("x_done", FFN, 7),
        ("start", "part", 3),
        ("stage", 7),
    ],
    (21, 0): [
        ("gather", 0, 2),
    ],
    (23, 1): [
        ("gather", 1, 2),
    ],
    (24, 0): [
        ("tokens",),
        ("gather", 0, 3),
        ("gather", 1, 3),
        ("gain", 0),
        ("gather", 0, 4),
        ("gather", 1, 4),
        ("gain", 1),
        ("gain", 2),
        ("gain", 3),
        ("mixed",),
        ("gain", 4),
    ],
}


def norm_factor(values):
    return lax.rsqrt(jnp.mean(values * values, axis=-1, keepdims=True) + EPS)


def norm_grad(grad_out, unit_rows, factor, scale_gain):
    scaled = grad_out * scale_gain
    return factor * (scaled - unit_rows * jnp.mean(scaled * unit_rows, axis=-1, keepdims=True))


def rows_dot(leading, trailing):
    return jnp.dot(leading, trailing, preferred_element_type=F32)


def across_rows(leading, trailing):
    return lax.dot_general(
        leading, trailing, (((0,), (0,)), ((), ())), preferred_element_type=F32
    )


def against_rows(leading, trailing):
    return lax.dot_general(
        leading, trailing, (((1,), (1,)), ((), ())), preferred_element_type=F32
    )


def ffn_middle(low_in, cot, wg, wu, wd):
    gate = rows_dot(low_in, wg)
    up = rows_dot(low_in, wu)
    sig = jax.nn.sigmoid(gate)
    silu = gate * sig
    hidden = (silu * up).astype(BF16)
    hidden_grad = against_rows(cot, wd)
    up_grad = (hidden_grad * silu).astype(BF16)
    gate_grad = (hidden_grad * up * sig * (1.0 + gate * (1.0 - sig))).astype(BF16)
    return hidden, gate_grad, up_grad


def shaped(*shape, kind=F32):
    return jax.ShapeDtypeStruct(shape, kind)


class Sizes:
    def __init__(self, dp_size, tokens, w_query, key_weight, query_gain, w_gate):
        self.rows, self.width = tokens
        self.head_width = query_gain[0]
        self.q_cols, self.k_cols = w_query[1], key_weight[1]
        self.heads, self.kv_heads = self.q_cols // self.head_width, self.k_cols // self.head_width
        self.units = w_gate[1]
        self.all_cols = self.q_cols + 2 * self.k_cols
        self.scale = 1.0 / math.sqrt(self.head_width)
        self.group = math.gcd(GROUP, dp_size)
        self.chips = self.group // 2
        self.half = self.chips // 2
        self.share = (self.width // 4, self.width // 2)
        self.grad_rows = self.width // 2
        self.grad_cols = self.width + self.all_cols
        self.piece = self.grad_rows // self.chips
        self.streams = 2


def layer_kernel(
    sz,
    tokens, cot, segments, positions, inverse, attn_gain, query_gain, key_gain, ffn_gain,
    w_query, key_weight, value_weight, w_out, w_gate, w_up, w_down,
    mixed, tokens_grad, gains, attn_grads, gate_grads, up_grads, down_grads,
    mine, theirs,
    part, part_theirs, middle_grad, sum_up, sum_down, gain_send, gain_recv, gain_slots,
    send_sems, recv_sems, local_sems,
):
    rows, width, head_width = sz.rows, sz.width, sz.head_width
    q_cols, k_cols, units = sz.q_cols, sz.k_cols, sz.units
    n, half, piece = sz.chips, sz.half, sz.piece
    half_units = units // 2
    mid = rows // 2

    device = lax.axis_index("dp")
    base = device // sz.group * sz.group
    core = device % 2
    chip = device % sz.group // 2
    line = chip % 2
    place = chip // 2 + line * (2 * half - 1 - 2 * (chip // 2))
    side = lax.axis_index("tensor")

    def device_at(position):
        position = position % n
        second = position // half
        return base + (2 * (position + second * (2 * half - 1 - 2 * position)) + second) * 2 + core

    forward = {"dp": device_at(place + 1)}
    backward = {"dp": device_at(place + n - 1)}
    sibling = {"dp": base + chip * 2 + 1 - core}
    across = {"tensor": 1 - side}

    barrier = pltpu.get_barrier_semaphore()
    for neighbour in (forward, backward, sibling, across):
        pl.semaphore_signal(barrier, inc=1, device_id=neighbour, device_id_type=MESH)
    pl.semaphore_wait(barrier, 4)

    book = {}
    waited = set()

    def remote(name, src, dst, target):
        book[name] = (len(book), src, dst, target)

    def made(name):
        index, src, dst, target = book[name]
        return pltpu.make_async_remote_copy(
            src_ref=src, dst_ref=dst, send_sem=send_sems.at[index], recv_sem=recv_sems.at[index],
            device_id=target, device_id_type=MESH,
        )

    def sent(*names):
        for name in names:
            made(name).wait_send()
            waited.add(name)

    def start(*names):
        for name in names:
            made(name).start()

    def arrived(*names):
        for name in names:
            made(name).wait_recv()

    def cols(first, count):
        return pl.ds(pl.multiple_of(first, 128), count)

    def piece_rows(index, first=0, count=piece, base_row=0):
        return pl.ds(pl.multiple_of(base_row + index % n * piece + first, 8), count)

    grad_base = core * sz.grad_rows
    slots = 2 * half
    up_slot = lambda h: 2 * h - 1
    down_slot = lambda h: 2 * h
    last = slots - 1
    up_place = lambda row, first, count: up_grads.at[pl.ds(row * rows, rows), pl.ds(first, count)]
    down_place = lambda row: down_grads.at[pl.ds(row * rows, rows)]
    half_width = width // 2
    gate_place = lambda row: gate_grads.at[pl.ds(row * rows, rows), pl.ds(units - width, width)]
    own = (gate_place(0), gate_place(1))
    for a, share in zip((COT, FFN), sz.share):
        window = cols(side * share, width - share)
        shared = cols(side * (width - share), share)
        for h in range(1, half):
            src = own[a] if h == 1 else mine.at[a, up_slot(h - 1)]
            remote(("up", a, h), src.at[:, window], mine.at[a, up_slot(h), :, window], forward)
            src = own[a] if h == 1 else mine.at[a, down_slot(h - 1)]
            remote(("down", a, h), src.at[:, window], mine.at[a, down_slot(h), :, window], backward)
        remote(
            ("up", a, half), mine.at[a, up_slot(half - 1), pl.ds(0, mid), window],
            mine.at[a, last, pl.ds(0, mid), window], forward,
        )
        remote(
            ("down", a, half), mine.at[a, down_slot(half - 1), pl.ds(mid, mid), window],
            mine.at[a, last, pl.ds(mid, mid), window], backward,
        )
        for s in range(1, slots):
            remote(("x", a, s), mine.at[a, s, :, shared], mine.at[a, s, :, shared], across)
        for s in range(slots):
            remote(("core", a, s), own[a] if s == 0 else mine.at[a, s], theirs.at[a, s], sibling)
    for k in range(4):
        remote(("part", k), part.at[(0, 1, 1, 0)[k]], part_theirs.at[k % 2], across)
    stream_cols = sz.grad_cols // sz.streams
    small = piece // 2
    for s in range(sz.streams):
        c = pl.ds(s * stream_cols, stream_cols)
        for h in range(1, half + 1):
            size, skip = (small, small) if h == 1 else (piece, 0)
            src = attn_grads.at[piece_rows(place + half, 0, small, grad_base), c]
            remote(
                ("su", s, h), src if h == 1 else sum_up.at[h - 2, :, c],
                sum_up.at[h - 1, pl.ds(0, size), c], forward,
            )
            src = attn_grads.at[piece_rows(place + half, small, small, grad_base), c]
            remote(
                ("sd", s, h), src if h == 1 else sum_down.at[h - 2, :, c],
                sum_down.at[h - 1, pl.ds(skip, size), c], backward,
            )
        for h in range(1, half + 1):
            size, skip = (small, small) if h == half else (piece, 0)
            going_up = attn_grads.at[piece_rows(place + n - h + 1, 0, size, grad_base), c]
            going_down = attn_grads.at[piece_rows(place + h - 1, skip, size, grad_base), c]
            remote(("gu", s, h), going_up, going_up, forward)
            remote(("gd", s, h), going_down, going_down, backward)
            got_up = attn_grads.at[piece_rows(place + n - h, 0, size, grad_base), c]
            got_down = attn_grads.at[piece_rows(place + h, skip, size, grad_base), c]
            remote(("cu", s, h), got_up, got_up, sibling)
            remote(("cd", s, h), got_down, got_down, sibling)
        own_piece = attn_grads.at[piece_rows(place, 0, piece, grad_base), c]
        remote(("cu", s, 0), own_piece, own_piece, sibling)
    remote("gains", gain_send, gain_recv, sibling)
    for h in range(1, half + 1):
        slot = gain_slots.at[(place + n - h + 1) % n]
        remote(("vu", h), slot, slot, forward)
        if h < half:
            slot = gain_slots.at[(place + h - 1) % n]
            remote(("vd", h), slot, slot, backward)

    def ring_step(a, h):
        arrived(("up", a, h), ("down", a, h))
        if h < half:
            start(("up", a, h + 1), ("down", a, h + 1))

    def x_start(a, s):
        start(("x", a, s))

    def x_done(a, s):
        arrived(("x", a, s))
        start(("core", a, s))


    def stream(s):
        return pl.ds(s * stream_cols, stream_cols)

    def sum_step(s, h):
        arrived(("su", s, h), ("sd", s, h))
        c = stream(s)
        up_rows = piece_rows(place + half - h, 0, piece, grad_base)
        down_rows = piece_rows(place + n - half + h, 0, piece, grad_base)
        if h == 1:
            sent(("su", s, 1), ("sd", s, 1))
            up, down = attn_grads[up_rows, c], attn_grads[down_rows, c]
            sum_up[0, :small, c] += up[:small]
            sum_up[0, small:, c] = up[small:]
            sum_down[0, :small, c] = down[:small]
            sum_down[0, small:, c] += down[small:]
        elif h < half:
            sum_up[h - 1, :, c] += attn_grads[up_rows, c]
            sum_down[h - 1, :, c] += attn_grads[down_rows, c]
        if h < half:
            start(("su", s, h + 1), ("sd", s, h + 1))
        else:
            own_rows = piece_rows(place, 0, piece, grad_base)
            attn_grads[own_rows, c] += sum_up[h - 1, :, c] + sum_down[h - 1, :, c]
            start(("gu", s, 1), ("gd", s, 1), ("cu", s, 0))

    def gather_step(s, h):
        arrived(("gu", s, h), ("gd", s, h))
        if h < half:
            start(("gu", s, h + 1), ("gd", s, h + 1))
        start(("cu", s, h), ("cd", s, h))

    def finish_tokens():
        arrived(("part", 2))
        grad = part[1, :rows] + part_theirs[0, :rows]
        value = tokens[...].astype(F32)
        factor = norm_factor(value)
        unit = value * factor
        tokens_grad[...] = (
            middle_grad[...] + norm_grad(grad, unit, factor, attn_gain[...])
        ).astype(BF16)
        gain_send[0:1, :] = jnp.sum(grad * unit, axis=0, keepdims=True)
        gain_send[2:, :] = part[1, rows : rows + 6] + part_theirs[0, rows : rows + 6]
        start("gains")

    def finish_mixed():
        arrived(("part", 3))
        mixed[...] = (part[0, :rows] + part_theirs[1, :rows]).astype(BF16)

    def gain_first():
        arrived("gains")
        gain_slots[place] = gain_send[...] + gain_recv[...]
        start(("vu", 1), ("vd", 1))

    def gain_step(h):
        arrived(("vu", h))
        if h < half:
            arrived(("vd", h))
            start(("vu", h + 1))
            if h + 1 < half:
                start(("vd", h + 1))
        else:
            total = gain_slots[0]
            for chip_at in range(1, n):
                total = total + gain_slots[chip_at]
            gains[...] = total

    def stage(slot):
        arrived(("core", COT, slot), ("core", FFN, slot))
        for copy in stage_copies(slot, False):
            copy.start()

    scoped = {}

    def stage_copies(slot, first):
        staged = scoped["staged"]
        copies = []
        for a in (COT, FFN):
            src = own[a] if first else mine.at[a, slot]
            copies.append(pltpu.make_async_copy(src, staged.at[a, 0], local_sems.at[9 + 2 * a]))
            copies.append(
                pltpu.make_async_copy(theirs.at[a, slot], staged.at[a, 1], local_sems.at[10 + 2 * a])
            )
        return copies

    def gain_event(h):
        if h == 0:
            gain_first()
        else:
            gain_step(h)

    actions = {
        "ring": ring_step,
        "start": lambda *name: start(name),
        "x_done": x_done,
        "sum": sum_step,
        "gather": gather_step,
        "stage": stage,
        "tokens": finish_tokens,
        "gain": gain_event,
        "mixed": finish_mixed,
    }

    def run(when):
        for event in PLAN.get(when, ()):
            actions[event[0]](*event[1:])

    group = q_cols // k_cols
    other_half = lambda count: cols((1 - core) * count, count)
    own_half = lambda count: cols(core * count, count)

    block = k_cols
    q_blocks, unit_blocks = q_cols // block, units // block
    at_k, at_v, at_o = q_blocks, q_blocks + 1, q_blocks + 2

    half_down = down_grads.at[pl.ds(pl.multiple_of(core * half_units, 8), half_units)]
    outs = (gate_grads.at[:, own_half(half_units)], up_grads.at[:, own_half(half_units)], half_down)
    for k, out in enumerate(outs):
        remote(("out", k), out, out, sibling)

    q_lin, k_lin = up_place(0, 0, q_cols), up_place(0, q_cols, k_cols)
    ctx_send, ctx_recv = up_place(1, 0, q_cols // 2), up_place(1, q_cols // 2, q_cols // 2)
    cosine, sine = up_place(1, q_cols, head_width), up_place(1, q_cols + head_width, head_width)
    attn_send, attn_recv = up_place(2, 0, half_width), up_place(2, half_width, half_width)
    mask = up_place(3, 0, rows)
    lows, low_recvs = (down_place(0), down_place(1)), (down_place(2), down_place(3))
    branch, branch_recv = down_place(4), down_place(5)
    deep = width // rows
    middle = gate_place(2)

    def probs_of(head):
        return gate_grads.at[pl.ds(head % deep * rows, rows), pl.ds(head // deep * rows, rows)]

    remote("ctx", ctx_send, ctx_recv, sibling)
    remote("attn", attn_send, attn_recv, sibling)
    remote("branch", branch, branch_recv, sibling)
    for k in range(2):
        remote(("low", k), lows[k], low_recvs[k], sibling)

    def first_phase(bank, wd, q_low, k_low, v_low, context, ffn_low, hidden, context_grad, attn_low):
        def load(src, dst, index):
            copy = pltpu.make_async_copy(src, dst, local_sems.at[index])
            copy.start()
            return copy

        def block_of(weights, index):
            return weights.at[:, pl.ds(index * block, block)]

        def load_attention():
            order = [(w_query, i) for i in range(q_blocks)] + [(key_weight, 0), (value_weight, 0)]
            order += [(w_out, i) for i in range(width // block)]
            return [load(block_of(w, i), bank.at[k], k) for k, (w, i) in enumerate(order)]

        def load_ffn():
            order = [(w, i) for w in (w_gate, w_up) for i in range(unit_blocks)]
            return [load(block_of(w, i), bank.at[k], k) for k, (w, i) in enumerate(order)]

        loads = load_attention()
        down_load = load(w_down, wd, 15)

        def head_norm(lin, gain):
            return lin * norm_factor(lin) * gain[...]

        def turned(lin, gain):
            normed = head_norm(lin, gain)
            swapped = pltpu.roll(normed, head_width // 2, 1)
            return (normed * cosine[...] + swapped * sine[...]).astype(BF16)

        def turned_back(grad, lin, gain):
            back = grad * cosine[...] - pltpu.roll(grad, head_width // 2, 1) * sine[...]
            factor = norm_factor(lin)
            unit = lin * factor
            return (
                norm_grad(back, unit, factor, gain[...]).astype(BF16),
                jnp.sum(back * unit, axis=0, keepdims=True),
            )

        own[COT][...] = cot[...].astype(F32)
        start(("up", COT, 1), ("down", COT, 1), ("core", COT, 0))

        resid = tokens[...].astype(F32)
        attn_in = (resid * norm_factor(resid) * attn_gain[...]).astype(BF16)
        attn_low[...] = attn_in
        attn_send[...] = attn_low[:, other_half(width // 2)].astype(F32)
        start("attn")

        def down_rows(row):
            return jnp.broadcast_to(row.astype(F32), (head_width, rows)).T

        segment_rows = jnp.concatenate([down_rows(segments[...])] * (rows // head_width), 1)
        same = segment_rows == jnp.broadcast_to(segments[...].astype(F32), (rows, rows))
        row_at = lax.broadcasted_iota(jnp.int32, (rows, rows), 0)
        column_at = lax.broadcasted_iota(jnp.int32, (rows, rows), 1)
        mask[...] = jnp.where(same & (row_at >= column_at), 1.0, 0.0)
        angles = down_rows(positions[...]) * inverse[...]
        lane = lax.broadcasted_iota(jnp.int32, (rows, head_width), 1)
        cosine[...] = jnp.cos(angles)
        sine[...] = jnp.where(lane < head_width // 2, -1.0, 1.0) * jnp.sin(angles)
        for i in range(q_blocks):
            loads[i].wait()
            q_lin[:, i * block : (i + 1) * block] = rows_dot(attn_in, bank[i])
        loads[at_k].wait()
        k_lin[...] = rows_dot(attn_in, bank[at_k])
        loads[at_v].wait()
        v_low[...] = rows_dot(attn_in, bank[at_v]).astype(BF16)
        run("A1")
        for kv in range(sz.kv_heads):
            kv_at = slice(kv * head_width, (kv + 1) * head_width)
            keys = turned(k_lin[:, kv_at], key_gain)
            k_low[:, kv_at] = keys
            values = v_low[:, kv_at]
            for member in range(group):
                head = kv * group + member
                at = slice(head * head_width, (head + 1) * head_width)
                queries = turned(q_lin[:, at], query_gain)
                q_low[:, at] = queries
                scores = jnp.where(mask[...] > 0, against_rows(queries, keys) * sz.scale, -1e30)
                raised = jnp.exp(scores - jnp.max(scores, axis=-1, keepdims=True))
                prob = raised / jnp.sum(raised, axis=-1, keepdims=True)
                probs_of(head)[...] = prob
                context[:, at] = rows_dot(prob.astype(BF16), values).astype(BF16)
        for i in range(width // block):
            loads[at_o + i].wait()
            part[0, :rows, i * block : (i + 1) * block] = rows_dot(context[...], bank[at_o + i])
        part[0, rows:] = jnp.zeros((8, width), F32)
        start(("part", 0))
        ctx_send[...] = context[:, other_half(q_cols // 2)].astype(F32)
        start("ctx")
        loads = load_ffn()
        run("A2")

        arrived(("part", 0))
        value = tokens[...].astype(F32) + (part[0, :rows] + part_theirs[0, :rows])
        middle[...] = value
        ffn_low[...] = (value * norm_factor(value) * ffn_gain[...]).astype(BF16)
        own[FFN][...] = ffn_low[...].astype(F32)
        start(("up", FFN, 1), ("down", FFN, 1), ("core", FFN, 0))
        run("A3")
        down_load.wait()
        for i in range(unit_blocks):
            at = slice(i * block, (i + 1) * block)
            loads[i].wait()
            loads[unit_blocks + i].wait()
            wg, wu = bank[i], bank[unit_blocks + i]
            low_hidden, gate_grad, up_grad = ffn_middle(ffn_low[...], cot[...], wg, wu, wd[at])
            hidden[:, at] = low_hidden
            term = against_rows(gate_grad, wg) + against_rows(up_grad, wu)
            if i == 0:
                part[1, :rows] = term
            else:
                part[1, :rows] += term
        part[1, rows:] = jnp.zeros((8, width), F32)
        start(("part", 1))
        loads = load_attention()
        run("A4")
        sent(("part", 0))
        part[0, :rows] = rows_dot(hidden[...], wd[...]) + 0.5 * middle[...]
        run("A5")

        arrived(("part", 1))
        grad = part[1, :rows] + part_theirs[1, :rows]
        value = middle[...]
        factor = norm_factor(value)
        unit = value * factor
        total = cot[...].astype(F32) + norm_grad(grad, unit, factor, ffn_gain[...])
        middle_grad[...] = total
        branch_low = total.astype(BF16)
        branch[...] = branch_low.astype(F32)
        start("branch")
        gain_send[1:2, :] = jnp.sum(grad * unit, axis=0, keepdims=True)
        run("A6")
        for load_of in loads:
            load_of.wait()
        context_grad[...] = sum(
            against_rows(branch_low[:, i * block : (i + 1) * block], bank[at_o + i])
            for i in range(width // block)
        ).astype(BF16)
        q_total = jnp.zeros((1, head_width), F32)
        k_total = jnp.zeros((1, head_width), F32)
        for kv in range(sz.kv_heads):
            kv_at = slice(kv * head_width, (kv + 1) * head_width)
            keys, values = k_low[:, kv_at], v_low[:, kv_at]
            keys_grad = values_grad = 0.0
            for member in range(group):
                head = kv * group + member
                at = slice(head * head_width, (head + 1) * head_width)
                head_grad = context_grad[:, at]
                prob = probs_of(head)[...]
                prob_grad = against_rows(head_grad, values)
                values_grad += across_rows(prob.astype(BF16), head_grad)
                inner = jnp.sum(prob * prob_grad, axis=-1, keepdims=True)
                score_grad = (prob * (prob_grad - inner)).astype(BF16)
                queries_grad = rows_dot(score_grad, keys) * sz.scale
                keys_grad += across_rows(score_grad, q_low[:, at])
                head_low, head_total = turned_back(queries_grad, q_lin[:, at], query_gain)
                lows[0][:, at] = head_low.astype(F32)
                q_total += head_total
            head_low, head_total = turned_back(keys_grad * sz.scale, k_lin[:, kv_at], key_gain)
            k_total += head_total
            lows[1][:, kv_at] = head_low.astype(F32)
            at = k_cols + kv * head_width
            lows[1][:, at : at + head_width] = values_grad.astype(BF16).astype(F32)
        start(("low", 0), ("low", 1))
        run("A7")
        half_rows = pl.ds(pl.multiple_of(grad_base, 8), sz.grad_rows)
        arrived("ctx", "branch")
        for i in range(width // block):
            at = slice(i * block, (i + 1) * block)
            attn_grads[half_rows, at] = across_rows(
                context[:, own_half(q_cols // 2)], branch[:, at].astype(BF16)
            ) + across_rows(ctx_recv[...].astype(BF16), branch_recv[:, at].astype(BF16))
        arrived("attn", ("low", 0), ("low", 1))
        for k in range(2):
            for i in range(width // block):
                at = slice(i * block, (i + 1) * block)
                first = (k + 1) * width + i * block
                attn_grads[half_rows, first : first + block] = across_rows(
                    attn_low[:, own_half(width // 2)], lows[k][:, at].astype(BF16)
                ) + across_rows(attn_recv[...].astype(BF16), low_recvs[k][:, at].astype(BF16))
        for s in range(sz.streams):
            start(("su", s, 1), ("sd", s, 1))
        sent(("part", 1))
        part[1, :rows] = sum(
            against_rows(
                lows[i // q_blocks][:, i % q_blocks * block : (i % q_blocks + 1) * block].astype(BF16),
                bank[i],
            )
            for i in range(at_o)
        )
        part[1, rows:] = jnp.zeros((8, width), F32)
        part[1, rows : rows + 1, :head_width] = q_total
        part[1, rows : rows + 1, head_width : 2 * head_width] = k_total
        run("A8")
        sent("ctx", "attn", "branch", ("low", 0), ("low", 1))

    pl.run_scoped(
        first_phase,
        pltpu.VMEM((max(at_o + width // block, 2 * unit_blocks), width, block), BF16),
        pltpu.VMEM(w_down.shape, BF16),
        pltpu.VMEM((rows, q_cols), BF16),
        pltpu.VMEM((rows, k_cols), BF16),
        pltpu.VMEM((rows, k_cols), BF16),
        pltpu.VMEM((rows, q_cols), BF16),
        pltpu.VMEM((rows, width), BF16),
        pltpu.VMEM((rows, units), BF16),
        pltpu.VMEM((rows, q_cols), BF16),
        pltpu.VMEM((rows, width), BF16),
    )

    def second_phase(
        wg, wu, wd, staged, ffn_low, ffn_turned, cot_low
    ):
        scoped["staged"] = staged
        weight_loads = [
            pltpu.make_async_copy(src, dst, local_sems.at[i])
            for i, (src, dst) in enumerate(
                (
                    (w_gate.at[:, own_half(half_units)], wg),
                    (w_up.at[:, own_half(half_units)], wu),
                    (w_down.at[pl.ds(pl.multiple_of(core * half_units, 8), half_units)], wd),
                )
            )
        ]
        for load in weight_loads:
            load.start()

        for a in (COT, FFN):
            sent(("up", a, 1), ("down", a, 1), ("core", a, 0))
        arrived(("core", COT, 0), ("core", FFN, 0))
        for copy in stage_copies(0, True):
            copy.start()
        for load in weight_loads:
            load.wait()
        chunks = 3
        size = half_units // chunks
        def step(i, _):
            slot, j = i // chunks, i % chunks

            @pl.when(j == 0)
            def _():
                for copy in stage_copies(slot, False):
                    copy.wait()
                for lane in range(2):
                    here = pl.ds(lane * rows, rows)
                    low_block = staged[FFN, lane].astype(BF16)
                    ffn_low[here] = low_block
                    ffn_turned[:, lane * rows : (lane + 1) * rows] = low_block.T
                    cot_low[here] = staged[COT, lane].astype(BF16)

            def events(part_of_step):
                for when in PLAN:
                    if isinstance(when, tuple) and when[0] < chunks * slots and when[1] == part_of_step:

                        @pl.when(i == when[0])
                        def _():
                            run(when)

            events(0)
            at_units = pl.ds(pl.multiple_of(j * size, 128), size)
            hidden, gate_grad, up_grad = ffn_middle(
                ffn_low[...], cot_low[...], wg[:, at_units], wu[:, at_units], wd[at_units]
            )
            events(1)
            down = across_rows(hidden, cot_low[...])
            gate = rows_dot(ffn_turned[...], gate_grad)
            up = rows_dot(ffn_turned[...], up_grad)

            grad_units = core * half_units + j * size
            grad_cols = pl.ds(pl.multiple_of(grad_units, 128), size)

            @pl.when(slot == 0)
            def _():
                gate_grads[:, grad_cols] = gate
                up_grads[:, grad_cols] = up
                down_grads[grad_cols] = down

            @pl.when(slot > 0)
            def _():
                gate_grads[:, grad_cols] += gate
                up_grads[:, grad_cols] += up
                down_grads[grad_cols] += down

            events(2)
            return 0

        lax.fori_loop(0, chunks * slots, step, 0)
        for k in range(3):
            start(("out", k))
        run((chunks * slots, 0))
        for k in range(3):
            arrived(("out", k))

    pl.run_scoped(
        second_phase,
        pltpu.VMEM((width, half_units), BF16),
        pltpu.VMEM((width, half_units), BF16),
        pltpu.VMEM((half_units, width), BF16),
        pltpu.VMEM((2, 2, rows, width), F32),
        pltpu.VMEM((2 * rows, width), BF16),
        pltpu.VMEM((width, 2 * rows), BF16),
        pltpu.VMEM((2 * rows, width), BF16),
    )
    for s in range(sz.streams):
        for h in range(half + 1):
            arrived(("cu", s, h))
            if h:
                arrived(("cd", s, h))
    for name in book:
        if name not in waited:
            made(name).wait_send()


def results_kernel(
    sz,
    mixed, tokens_grad, gains, attn_grads, gate_grads, up_grads, down_grads,
    mixed_out, tokens_out, out_out, query_out, key_out, value_out, gate_out, up_out, down_out,
    attn_gain_out, ffn_gain_out, query_gain_out, key_gain_out,
    sems,
):
    moves = [(mixed, mixed_out), (tokens_grad, tokens_out)]
    moves += [(gate_grads, gate_out), (up_grads, up_out), (down_grads, down_out)]
    first = 0
    for dst in (out_out, query_out, key_out, value_out):
        moves.append((attn_grads.at[:, pl.ds(first, dst.shape[1])], dst))
        first += dst.shape[1]
    copies = [
        pltpu.make_async_copy(src, dst, sems.at[k]) for k, (src, dst) in enumerate(moves)
    ]
    for copy in copies:
        copy.start()
    attn_gain_out[...] = gains[0:1, :]
    ffn_gain_out[...] = gains[1:2, :]
    query_gain_out[...] = gains[2:3, : sz.head_width]
    key_gain_out[...] = gains[2:3, sz.head_width : 2 * sz.head_width]
    for copy in copies:
        copy.wait()


def over_groups(sz, dp_size, values):
    step = sz.group
    while step < dp_size:
        values = values + lax.ppermute(values, "dp", [(d, d ^ step) for d in range(dp_size)])
        step *= 2
    return values


def per_device(
    dp_size,
    tokens,
    segments,
    positions,
    attn_gain,
    w_query,
    key_weight,
    value_weight,
    query_gain,
    key_gain,
    w_out,
    ffn_gain,
    w_gate,
    w_up,
    w_down,
    cotangent,
):
    sz = Sizes(dp_size, tokens.shape, w_query.shape, key_weight.shape, query_gain.shape, w_gate.shape)
    rows, width, head_width, half = sz.rows, sz.width, sz.head_width, sz.half
    q_cols, k_cols = sz.q_cols, sz.k_cols
    lanes = np.arange(head_width) % (head_width // 2)
    inverse = (THETA ** (-2.0 * lanes / head_width)).astype(np.float32)[None]
    vmem = pl.BlockSpec(memory_space=pltpu.VMEM)
    anywhere = pl.BlockSpec(memory_space=pl.ANY)
    slots = 2 * half
    transfers = 256
    mixed, tokens_grad, gains, attn_grads, gate_grads, up_grads, down_grads, _, _ = pl.pallas_call(
        functools.partial(layer_kernel, sz),
        out_shape=[
            pltpu.VMEM((rows, width), BF16),
            pltpu.VMEM((rows, width), BF16),
            pltpu.VMEM((8, width), F32),
            pltpu.VMEM((width, sz.grad_cols), F32),
            pltpu.VMEM(w_gate.shape, F32),
            pltpu.VMEM(w_up.shape, F32),
            pltpu.VMEM(w_down.shape, F32),
            shaped(2, slots, rows, width),
            shaped(2, slots, rows, width),
        ],
        in_specs=[vmem] * 9 + [anywhere] * 7,
        out_specs=[vmem] * 7 + [anywhere] * 2,
        scratch_shapes=[
            pltpu.VMEM((2, rows + 8, width), F32),
            pltpu.VMEM((2, rows + 8, width), F32),
            pltpu.VMEM((rows, width), F32),
            pltpu.VMEM((half, sz.piece, sz.grad_cols), F32),
            pltpu.VMEM((half, sz.piece, sz.grad_cols), F32),
            pltpu.VMEM((8, width), F32),
            pltpu.VMEM((8, width), F32),
            pltpu.VMEM((sz.chips, 8, width), F32),
            pltpu.SemaphoreType.DMA((transfers,)),
            pltpu.SemaphoreType.DMA((transfers,)),
            pltpu.SemaphoreType.DMA((16,)),
        ],
        compiler_params=pltpu.CompilerParams(
            collective_id=0, has_side_effects=True, vmem_limit_bytes=VMEM_BYTES
        ),
    )(
        tokens, cotangent, segments, positions, jnp.asarray(inverse), attn_gain[None], query_gain[None], key_gain[None],
        ffn_gain[None], w_query, key_weight, value_weight, w_out, w_gate, w_up, w_down,
    )
    gains, attn_grads, gate_grads, up_grads, down_grads = [
        over_groups(sz, dp_size, v) for v in (gains, attn_grads, gate_grads, up_grads, down_grads)
    ]
    def in_vmem(values):
        return pltpu.with_memory_space_constraint(values, pltpu.VMEM)

    (
        mixed, tokens_grad, w_out_grad, w_query_grad, w_key_grad, w_value_grad,
        w_gate_grad, w_up_grad, w_down_grad,
        attn_gain_grad, ffn_gain_grad, query_gain_grad, key_gain_grad,
    ) = pl.pallas_call(
        functools.partial(results_kernel, sz),
        out_shape=[
            shaped(rows, width, kind=BF16),
            shaped(rows, width, kind=BF16),
            shaped(*w_out.shape),
            shaped(*w_query.shape),
            shaped(*key_weight.shape),
            shaped(*value_weight.shape),
            shaped(*w_gate.shape),
            shaped(*w_up.shape),
            shaped(*w_down.shape),
            shaped(1, width),
            shaped(1, width),
            shaped(1, head_width),
            shaped(1, head_width),
        ],
        in_specs=[anywhere, anywhere, vmem] + [anywhere] * 4,
        out_specs=[anywhere] * 9 + [vmem] * 4,
        scratch_shapes=[pltpu.SemaphoreType.DMA((9,))],
        compiler_params=pltpu.CompilerParams(vmem_limit_bytes=RESULTS_VMEM_BYTES),
    )(
        in_vmem(mixed), in_vmem(tokens_grad), gains, in_vmem(attn_grads),
        in_vmem(gate_grads), in_vmem(up_grads), in_vmem(down_grads),
    )
    return (
        mixed,
        tokens_grad,
        attn_gain_grad[0],
        w_query_grad,
        w_key_grad,
        w_value_grad,
        query_gain_grad[0],
        key_gain_grad[0],
        w_out_grad,
        ffn_gain_grad[0],
        w_gate_grad,
        w_up_grad,
        w_down_grad,
    )


def solution(mesh):
    def layer(*arrays):
        return per_device(mesh.shape["dp"], *arrays)

    return jax.shard_map(
        layer,
        mesh=mesh,
        in_specs=(
            P("dp", None),
            P("dp", None),
            P("dp", None),
            P(),
            P(None, "tensor"),
            P(None, "tensor"),
            P(None, "tensor"),
            P(),
            P(),
            P("tensor", None),
            P(),
            P(None, "tensor"),
            P(None, "tensor"),
            P("tensor", None),
            P("dp", None),
        ),
        out_specs=(
            P("dp", None),
            P("dp", None),
            P(),
            P(None, "tensor"),
            P(None, "tensor"),
            P(None, "tensor"),
            P(),
            P(),
            P("tensor", None),
            P(),
            P(None, "tensor"),
            P(None, "tensor"),
            P("tensor", None),
        ),
        check_vma=False,
    )
```

```python
import functools
import math

import jax
import jax.numpy as jnp
import numpy as np
from jax import lax
from jax.experimental import pallas as pl
from jax.experimental.pallas import tpu as pltpu
from jax.sharding import PartitionSpec as P

EPS = 1e-06
THETA = 1000000.0
F32 = jnp.float32
BF16 = jnp.bfloat16
MESH = pl.DeviceIdType.MESH
VMEM_BYTES = 32 * 2**20
RESULTS_VMEM_BYTES = 2**20
GROUP = 16
COT, FFN = 0, 1


PLAN = {
    "A2": [
        ("ring", COT, 1),
    ],
    "A5": [
        ("start", "x", COT, 1),
        ("ring", COT, 2),
    ],
    "A7": [
        ("start", "x", COT, 2),
        ("start", "x", COT, 3),
        ("start", "x", COT, 4),
        ("ring", FFN, 1),
    ],
    "A10": [
        ("x_done", COT, 1),
        ("start", "x", FFN, 1),
    ],
    (0, 0): [
        ("ring", COT, 3),
        ("x_done", COT, 2),
        ("start", "x", FFN, 2),
    ],
    (0, 1): [
        ("x_done", COT, 3),
        ("start", "x", COT, 5),
    ],
    (2, 1): [
        ("ring", FFN, 2),
        ("x_done", COT, 4),
        ("start", "x", COT, 6),
    ],
    (2, 2): [
        ("sum", 0, 1),
        ("sum", 1, 1),
        ("x_done", FFN, 1),
        ("start", "x", FFN, 3),
        ("stage", 1),
    ],
    (3, 0): [
        ("ring", COT, 4),
    ],
    (4, 1): [
        ("x_done", FFN, 2),
        ("start", "x", FFN, 4),
    ],
    (5, 2): [
        ("stage", 2),
    ],
    (6, 0): [
        ("ring", FFN, 3),
        ("x_done", COT, 5),
        ("start", "x", FFN, 5),
    ],
    (6, 1): [
        ("x_done", COT, 6),
        ("start", "x", FFN, 6),
    ],
    (7, 1): [
        ("sum", 0, 2),
    ],
    (8, 2): [
        ("x_done", FFN, 3),
        ("start", "x", COT, 7),
        ("sum", 1, 2),
        ("stage", 3),
    ],
    (9, 0): [
        ("ring", FFN, 4),
    ],
    (10, 1): [
        ("x_done", FFN, 4),
        ("start", "x", FFN, 7),
    ],
    (11, 1): [
        ("sum", 0, 3),
        ("stage", 4),
    ],
    (13, 0): [
        ("sum", 1, 3),
        ("x_done", FFN, 5),
        ("start", "part", 2),
    ],
    (14, 1): [
        ("stage", 5),
    ],
    (15, 0): [
        ("sum", 0, 4),
    ],
    (15, 1): [
        ("x_done", FFN, 6),
        ("start", "part", 3),
    ],
    (17, 0): [
        ("x_done", COT, 7),
        ("stage", 6),
    ],
    (17, 1): [
        ("sum", 1, 4),
    ],
    (19, 1): [
        ("gather", 0, 1),
    ],
    (20, 0): [
        ("x_done", FFN, 7),
    ],
    (20, 2): [
        ("stage", 7),
    ],
    (21, 0): [
        ("gather", 1, 1),
    ],
    (23, 1): [
        ("gather", 0, 2),
    ],
    (24, 0): [
        ("gather", 1, 2),
        ("tokens",),
        ("gather", 0, 3),
        ("gain", 0),
        ("gather", 1, 3),
        ("gather", 0, 4),
        ("gain", 1),
        ("mixed",),
        ("gather", 1, 4),
        ("gain", 2),
        ("gain", 3),
        ("gain", 4),
    ],
}


def norm_factor(values):
    return lax.rsqrt(jnp.mean(values * values, axis=-1, keepdims=True) + EPS)


def norm_grad(grad_out, unit_rows, factor, scale_gain):
    scaled = grad_out * scale_gain
    return factor * (scaled - unit_rows * jnp.mean(scaled * unit_rows, axis=-1, keepdims=True))


def rows_dot(leading, trailing):
    return jnp.dot(leading, trailing, preferred_element_type=F32)


def across_rows(leading, trailing):
    return lax.dot_general(
        leading, trailing, (((0,), (0,)), ((), ())), preferred_element_type=F32
    )


def against_rows(leading, trailing):
    return lax.dot_general(
        leading, trailing, (((1,), (1,)), ((), ())), preferred_element_type=F32
    )


def ffn_middle(low_in, cot, wg, wu, wd):
    gate = rows_dot(low_in, wg)
    up = rows_dot(low_in, wu)
    sig = jax.nn.sigmoid(gate)
    silu = gate * sig
    hidden = (silu * up).astype(BF16)
    hidden_grad = against_rows(cot, wd)
    up_grad = (hidden_grad * silu).astype(BF16)
    gate_grad = (hidden_grad * up * sig * (1.0 + gate * (1.0 - sig))).astype(BF16)
    return hidden, gate_grad, up_grad


def shaped(*shape, kind=F32):
    return jax.ShapeDtypeStruct(shape, kind)


class Sizes:
    def __init__(self, dp_size, tokens, w_query, key_weight, query_gain, w_gate):
        self.rows, self.width = tokens
        self.head_width = query_gain[0]
        self.q_cols, self.k_cols = w_query[1], key_weight[1]
        self.heads, self.kv_heads = self.q_cols // self.head_width, self.k_cols // self.head_width
        self.units = w_gate[1]
        self.all_cols = self.q_cols + 2 * self.k_cols
        self.scale = 1.0 / math.sqrt(self.head_width)
        self.group = math.gcd(GROUP, dp_size)
        self.chips = self.group // 2
        self.half = self.chips // 2
        self.share = (self.width * 2 // 8, self.width * 4 // 8)
        self.grad_rows = self.width // 2
        self.grad_cols = self.width + self.all_cols
        self.piece = self.grad_rows // self.chips
        self.streams = 2


def layer_kernel(
    sz,
    tokens_in, cot_in, segments_in, positions_in, inverse_in, attn_gain_in, query_gain_in, key_gain_in,
    ffn_gain_in,
    w_query, key_weight, value_weight, w_out, w_gate, w_up, w_down,
    mixed, tokens_grad, attn_gain_grad, ffn_gain_grad, query_gain_grad, key_gain_grad,
    attn_grads, gate_grads, up_grads, down_grads,
    mine, theirs,
    tokens, cot, segments, positions, inverse, attn_gain, query_gain, key_gain, ffn_gain,
    part, part_theirs, middle_grad, sum_up, sum_down, gain_send, gain_recv, gain_slots,
    send_sems, recv_sems, local_sems,
):
    rows, width, head_width = sz.rows, sz.width, sz.head_width
    q_cols, k_cols, units = sz.q_cols, sz.k_cols, sz.units
    n, half, piece = sz.chips, sz.half, sz.piece
    half_units = units // 2
    mid = rows // 2

    device = lax.axis_index("dp")
    base = device // sz.group * sz.group
    core = device % 2
    chip = device % sz.group // 2
    line = chip % 2
    place = chip // 2 + line * (2 * half - 1 - 2 * (chip // 2))
    side = lax.axis_index("tensor")

    def device_at(position):
        position = position % n
        second = position // half
        return base + (2 * (position + second * (2 * half - 1 - 2 * position)) + second) * 2 + core

    forward = {"dp": device_at(place + 1)}
    backward = {"dp": device_at(place + n - 1)}
    sibling = {"dp": base + chip * 2 + 1 - core}
    across = {"tensor": 1 - side}

    barrier = pltpu.get_barrier_semaphore()
    for neighbour in (forward, backward, sibling, across):
        pl.semaphore_signal(barrier, inc=1, device_id=neighbour, device_id_type=MESH)
    small_loads = [
        pltpu.make_async_copy(src, dst, local_sems.at[16 + k])
        for k, (src, dst) in enumerate(
            (
                (cot_in, cot),
                (tokens_in, tokens),
                (attn_gain_in, attn_gain),
                (segments_in, segments),
                (positions_in, positions),
                (inverse_in, inverse),
                (query_gain_in, query_gain),
                (key_gain_in, key_gain),
                (ffn_gain_in, ffn_gain),
            )
        )
    ]
    for load in small_loads:
        load.start()

    book = {}
    waited = set()

    def remote(name, src, dst, target):
        book[name] = (len(book), src, dst, target)

    def made(name):
        index, src, dst, target = book[name]
        return pltpu.make_async_remote_copy(
            src_ref=src, dst_ref=dst, send_sem=send_sems.at[index], recv_sem=recv_sems.at[index],
            device_id=target, device_id_type=MESH,
        )

    def sent(*names):
        for name in names:
            made(name).wait_send()
            waited.add(name)

    def start(*names):
        for name in names:
            made(name).start()

    def arrived(*names):
        for name in names:
            made(name).wait_recv()

    def cols(first, count):
        return pl.ds(pl.multiple_of(first, 128), count)

    def piece_rows(index, first=0, count=piece, base_row=0):
        return pl.ds(pl.multiple_of(base_row + index % n * piece + first, 8), count)

    grad_base = core * sz.grad_rows
    slots = 2 * half
    up_slot = lambda h: 2 * h - 1
    down_slot = lambda h: 2 * h
    last = slots - 1
    up_place = lambda row, first, count: up_grads.at[pl.ds(row * rows, rows), pl.ds(first, count)]
    down_place = lambda row: down_grads.at[pl.ds(row * rows, rows)]
    half_width = width // 2
    gate_place = lambda row: gate_grads.at[pl.ds(row * rows, rows), pl.ds(units - width, width)]
    own = (gate_place(0), gate_place(1))
    for a, share in zip((COT, FFN), sz.share):
        window = cols(side * share, width - share)
        shared = cols(side * (width - share), share)
        for h in range(1, half):
            src = own[a] if h == 1 else mine.at[a, up_slot(h - 1)]
            remote(("up", a, h), src.at[:, window], mine.at[a, up_slot(h), :, window], forward)
            src = own[a] if h == 1 else mine.at[a, down_slot(h - 1)]
            remote(("down", a, h), src.at[:, window], mine.at[a, down_slot(h), :, window], backward)
        remote(
            ("up", a, half), mine.at[a, up_slot(half - 1), pl.ds(0, mid), window],
            mine.at[a, last, pl.ds(0, mid), window], forward,
        )
        remote(
            ("down", a, half), mine.at[a, down_slot(half - 1), pl.ds(mid, mid), window],
            mine.at[a, last, pl.ds(mid, mid), window], backward,
        )
        for s in range(1, slots):
            remote(("x", a, s), mine.at[a, s, :, shared], mine.at[a, s, :, shared], across)
        for s in range(slots):
            remote(("core", a, s), own[a] if s == 0 else mine.at[a, s], theirs.at[a, s], sibling)
    halves = (slice(0, mid), slice(mid, rows))
    for k in range(2):
        for index, at_rows in enumerate(halves):
            at_rows = pl.ds(at_rows.start, mid)
            remote(
                ("part", k, index), part.at[k, at_rows], part_theirs.at[k, at_rows], across
            )
        remote(("part", 2 + k), part.at[1 - k], part_theirs.at[k], across)
    stream_cols = sz.grad_cols // sz.streams
    small = piece // 2
    for s in range(sz.streams):
        c = pl.ds(s * stream_cols, stream_cols)
        for h in range(1, half + 1):
            size, skip = (small, small) if h == 1 else (piece, 0)
            src = attn_grads.at[piece_rows(place + half, 0, small, grad_base), c]
            remote(
                ("su", s, h), src if h == 1 else sum_up.at[h - 2, :, c],
                sum_up.at[h - 1, pl.ds(0, size), c], forward,
            )
            src = attn_grads.at[piece_rows(place + half, small, small, grad_base), c]
            remote(
                ("sd", s, h), src if h == 1 else sum_down.at[h - 2, :, c],
                sum_down.at[h - 1, pl.ds(skip, size), c], backward,
            )
        for h in range(1, half + 1):
            size, skip = (small, small) if h == half else (piece, 0)
            going_up = attn_grads.at[piece_rows(place + n - h + 1, 0, size, grad_base), c]
            going_down = attn_grads.at[piece_rows(place + h - 1, skip, size, grad_base), c]
            remote(("gu", s, h), going_up, going_up, forward)
            remote(("gd", s, h), going_down, going_down, backward)
            got_up = attn_grads.at[piece_rows(place + n - h, 0, size, grad_base), c]
            got_down = attn_grads.at[piece_rows(place + h, skip, size, grad_base), c]
            remote(("cu", s, h), got_up, got_up, sibling)
            remote(("cd", s, h), got_down, got_down, sibling)
        own_piece = attn_grads.at[piece_rows(place, 0, piece, grad_base), c]
        remote(("cu", s, 0), own_piece, own_piece, sibling)
    remote("gains", gain_send, gain_recv, sibling)
    for h in range(1, half + 1):
        slot = gain_slots.at[(place + n - h + 1) % n]
        remote(("vu", h), slot, slot, forward)
        if h < half:
            slot = gain_slots.at[(place + h - 1) % n]
            remote(("vd", h), slot, slot, backward)

    def ring_step(a, h):
        arrived(("up", a, h), ("down", a, h))
        if h < half:
            start(("up", a, h + 1), ("down", a, h + 1))

    def x_start(a, s):
        start(("x", a, s))

    def x_done(a, s):
        arrived(("x", a, s))
        start(("core", a, s))


    def stream(s):
        return pl.ds(s * stream_cols, stream_cols)

    def sum_step(s, h):
        arrived(("su", s, h), ("sd", s, h))
        c = stream(s)
        up_rows = piece_rows(place + half - h, 0, piece, grad_base)
        down_rows = piece_rows(place + n - half + h, 0, piece, grad_base)
        if h == 1:
            sent(("su", s, 1), ("sd", s, 1))
            up, down = attn_grads[up_rows, c], attn_grads[down_rows, c]
            sum_up[0, :small, c] += up[:small]
            sum_up[0, small:, c] = up[small:]
            sum_down[0, :small, c] = down[:small]
            sum_down[0, small:, c] += down[small:]
        elif h < half:
            sum_up[h - 1, :, c] += attn_grads[up_rows, c]
            sum_down[h - 1, :, c] += attn_grads[down_rows, c]
        if h < half:
            start(("su", s, h + 1), ("sd", s, h + 1))
        else:
            own_rows = piece_rows(place, 0, piece, grad_base)
            attn_grads[own_rows, c] += sum_up[h - 1, :, c] + sum_down[h - 1, :, c]
            start(("gu", s, 1), ("gd", s, 1), ("cu", s, 0))

    def gather_step(s, h):
        arrived(("gu", s, h), ("gd", s, h))
        if h < half:
            start(("gu", s, h + 1), ("gd", s, h + 1))
        start(("cu", s, h), ("cd", s, h))

    def finish_tokens():
        arrived(("part", 2))
        grad = part[1, :rows] + part_theirs[0, :rows]
        value = tokens[...].astype(F32)
        factor = norm_factor(value)
        unit = value * factor
        tokens_grad[...] = (
            middle_grad[...] + norm_grad(grad, unit, factor, attn_gain[...])
        ).astype(BF16)
        gain_send[0:1, :] = jnp.sum(grad * unit, axis=0, keepdims=True)
        gain_send[2:, :] = part[1, rows : rows + 6] + part_theirs[0, rows : rows + 6]
        start("gains")

    def finish_mixed():
        arrived(("part", 3))
        mixed[...] = (part[0, :rows] + part_theirs[1, :rows]).astype(BF16)

    def gain_first():
        arrived("gains")
        gain_slots[place] = gain_send[...] + gain_recv[...]
        start(("vu", 1), ("vd", 1))

    def gain_step(h):
        arrived(("vu", h))
        if h < half:
            arrived(("vd", h))
            start(("vu", h + 1))
            if h + 1 < half:
                start(("vd", h + 1))
        else:
            total = gain_slots[0]
            for chip_at in range(1, n):
                total = total + gain_slots[chip_at]
            attn_gain_grad[...] = total[0:1, :]
            ffn_gain_grad[...] = total[1:2, :]
            query_gain_grad[...] = total[2:3, :head_width]
            key_gain_grad[...] = total[2:3, head_width : 2 * head_width]

    def stage(slot):
        arrived(("core", COT, slot), ("core", FFN, slot))
        for copy in stage_copies(slot, False):
            copy.start()

    scoped = {}

    def stage_copies(slot, first):
        staged = scoped["staged"]
        copies = []
        for a in (COT, FFN):
            src = own[a] if first else mine.at[a, slot]
            copies.append(pltpu.make_async_copy(src, staged.at[a, 0], local_sems.at[9 + 2 * a]))
            copies.append(
                pltpu.make_async_copy(theirs.at[a, slot], staged.at[a, 1], local_sems.at[10 + 2 * a])
            )
        return copies

    def gain_event(h):
        if h == 0:
            gain_first()
        else:
            gain_step(h)

    actions = {
        "ring": ring_step,
        "start": lambda *name: start(name),
        "x_done": x_done,
        "sum": sum_step,
        "gather": gather_step,
        "stage": stage,
        "tokens": finish_tokens,
        "gain": gain_event,
        "mixed": finish_mixed,
    }

    def run(when):
        for event in PLAN.get(when, ()):
            actions[event[0]](*event[1:])

    group = q_cols // k_cols
    other_half = lambda count: cols((1 - core) * count, count)
    own_half = lambda count: cols(core * count, count)

    block = k_cols
    q_blocks, unit_blocks = q_cols // block, units // block
    at_k, at_v, at_o = q_blocks, q_blocks + 1, q_blocks + 2

    half_down = down_grads.at[pl.ds(pl.multiple_of(core * half_units, 8), half_units)]
    outs = (gate_grads.at[:, own_half(half_units)], up_grads.at[:, own_half(half_units)], half_down)
    for k, out in enumerate(outs):
        remote(("out", k), out, out, sibling)

    q_lin, k_lin = up_place(0, 0, q_cols), up_place(0, q_cols, k_cols)
    ctx_send, ctx_recv = up_place(1, 0, q_cols // 2), up_place(1, q_cols // 2, q_cols // 2)
    cosine, sine = up_place(1, q_cols, head_width), up_place(1, q_cols + head_width, head_width)
    attn_send, attn_recv = up_place(2, 0, half_width), up_place(2, half_width, half_width)
    mask = up_place(3, 0, rows)
    lows, low_recvs = (down_place(0), down_place(1)), (down_place(2), down_place(3))
    branch, branch_recv = down_place(4), down_place(5)
    deep = width // rows
    middle = gate_place(2)

    def probs_of(head):
        return gate_grads.at[pl.ds(head % deep * rows, rows), pl.ds(head // deep * rows, rows)]

    remote("ctx", ctx_send, ctx_recv, sibling)
    remote("attn", attn_send, attn_recv, sibling)
    remote("branch", branch, branch_recv, sibling)
    for k in range(2):
        remote(("low", k), lows[k], low_recvs[k], sibling)

    def first_phase(
        bank, wd, q_low, k_low, v_low, context, ffn_low, hidden, context_grad, attn_low, branch_low
    ):
        def load(src, dst, index):
            copy = pltpu.make_async_copy(src, dst, local_sems.at[index])
            copy.start()
            return copy

        def block_of(weights, index):
            return weights.at[:, pl.ds(index * block, block)]

        def load_attention():
            order = [(w_query, i) for i in range(q_blocks)] + [(key_weight, 0), (value_weight, 0)]
            order += [(w_out, i) for i in range(width // block)]
            return [load(block_of(w, i), bank.at[k], k) for k, (w, i) in enumerate(order)]

        def load_ffn():
            order = [(w, i) for w in (w_gate, w_up) for i in range(unit_blocks)]
            return [load(block_of(w, i), bank.at[k], k) for k, (w, i) in enumerate(order)]

        loads = load_attention()
        down_load = load(w_down, wd, 15)

        def head_norm(lin, gain):
            return lin * norm_factor(lin) * gain[...]

        def turned(lin, gain, at_rows):
            normed = head_norm(lin, gain)
            swapped = pltpu.roll(normed, head_width // 2, 1)
            return (normed * cosine[at_rows] + swapped * sine[at_rows]).astype(BF16)

        def turned_back(grad, lin, gain):
            back = grad * cosine[...] - pltpu.roll(grad, head_width // 2, 1) * sine[...]
            factor = norm_factor(lin)
            unit = lin * factor
            return (
                norm_grad(back, unit, factor, gain[...]).astype(BF16),
                jnp.sum(back * unit, axis=0, keepdims=True),
            )

        small_loads[0].wait()
        own[COT][...] = cot[...].astype(F32)
        pl.semaphore_wait(barrier, 4)
        start(("up", COT, 1), ("down", COT, 1), ("core", COT, 0))

        for small in small_loads[1:]:
            small.wait()
        resid = tokens[...].astype(F32)
        attn_in = (resid * norm_factor(resid) * attn_gain[...]).astype(BF16)
        attn_low[...] = attn_in
        attn_send[...] = attn_low[:, other_half(width // 2)].astype(F32)
        start("attn")

        def down_rows(row):
            return jnp.broadcast_to(row.astype(F32), (head_width, rows)).T

        segment_rows = jnp.concatenate([down_rows(segments[...])] * (rows // head_width), 1)
        same = segment_rows == jnp.broadcast_to(segments[...].astype(F32), (rows, rows))
        row_at = lax.broadcasted_iota(jnp.int32, (rows, rows), 0)
        column_at = lax.broadcasted_iota(jnp.int32, (rows, rows), 1)
        mask[...] = jnp.where(same & (row_at >= column_at), 1.0, 0.0)
        angles = down_rows(positions[...]) * inverse[...]
        lane = lax.broadcasted_iota(jnp.int32, (rows, head_width), 1)
        cosine[...] = jnp.cos(angles)
        sine[...] = jnp.where(lane < head_width // 2, -1.0, 1.0) * jnp.sin(angles)
        for i in range(q_blocks):
            loads[i].wait()
            q_lin[:, i * block : (i + 1) * block] = rows_dot(attn_in, bank[i])
        loads[at_k].wait()
        k_lin[...] = rows_dot(attn_in, bank[at_k])
        loads[at_v].wait()
        v_low[...] = rows_dot(attn_in, bank[at_v]).astype(BF16)
        run("A1")
        for kv in range(sz.kv_heads):
            kv_at = slice(kv * head_width, (kv + 1) * head_width)
            k_low[:, kv_at] = turned(k_lin[:, kv_at], key_gain, slice(0, rows))
        for index, at_rows in enumerate(halves):
            seen = at_rows.stop
            for head in range(sz.heads):
                at = slice(head * head_width, (head + 1) * head_width)
                kv_at = slice(head // group * head_width, (head // group + 1) * head_width)
                queries = turned(q_lin[at_rows, at], query_gain, at_rows)
                q_low[at_rows, at] = queries
                scores = against_rows(queries, k_low[:seen, kv_at]) * sz.scale
                scores = jnp.where(mask[at_rows, :seen] > 0, scores, -1e30)
                raised = jnp.exp(scores - jnp.max(scores, axis=-1, keepdims=True))
                prob = raised / jnp.sum(raised, axis=-1, keepdims=True)
                place_of = probs_of(head)
                place_of[at_rows, :seen] = prob
                if seen < rows:
                    place_of[at_rows, seen:] = jnp.zeros((mid, rows - seen), F32)
                context[at_rows, at] = rows_dot(prob.astype(BF16), v_low[:seen, kv_at]).astype(BF16)
            for i in range(width // block):
                if index == 0:
                    loads[at_o + i].wait()
                at = slice(i * block, (i + 1) * block)
                part[0, at_rows, at] = rows_dot(context[at_rows], bank[at_o + i])
            start(("part", 0, index))
        ctx_send[...] = context[:, other_half(q_cols // 2)].astype(F32)
        start("ctx")
        loads = load_ffn()
        for index, at_rows in enumerate(halves):
            run("A2" if index == 0 else "A3")
            arrived(("part", 0, index))
            value = tokens[at_rows].astype(F32) + (part[0, at_rows] + part_theirs[0, at_rows])
            middle[at_rows] = value
            low_rows = (value * norm_factor(value) * ffn_gain[...]).astype(BF16)
            ffn_low[at_rows] = low_rows
            own[FFN][at_rows] = low_rows.astype(F32)
            if index == 0:
                down_load.wait()
                for load_of in loads:
                    load_of.wait()
            else:
                start(("up", FFN, 1), ("down", FFN, 1), ("core", FFN, 0))
                run("A4")
            for i in range(unit_blocks):
                at = slice(i * block, (i + 1) * block)
                wg, wu = bank[i], bank[unit_blocks + i]
                low_hidden, gate_grad, up_grad = ffn_middle(low_rows, cot[at_rows], wg, wu, wd[at])
                hidden[at_rows, at] = low_hidden
                term = against_rows(gate_grad, wg) + against_rows(up_grad, wu)
                if i == 0:
                    part[1, at_rows] = term
                else:
                    part[1, at_rows] += term
            start(("part", 1, index))
        loads = load_attention()
        run("A5")
        sent(("part", 0, 0), ("part", 0, 1))
        part[0, :rows] = rows_dot(hidden[...], wd[...]) + 0.5 * middle[...]
        part[0, rows:] = jnp.zeros((8, width), F32)

        for index, at_rows in enumerate(halves):
            run("A6" if index == 0 else "A7")
            arrived(("part", 1, index))
            grad = part[1, at_rows] + part_theirs[1, at_rows]
            value = middle[at_rows]
            factor = norm_factor(value)
            unit = value * factor
            total = cot[at_rows].astype(F32) + norm_grad(grad, unit, factor, ffn_gain[...])
            middle_grad[at_rows] = total
            branch_low[at_rows] = total.astype(BF16)
            branch[at_rows] = total.astype(BF16).astype(F32)
            gain_term = jnp.sum(grad * unit, axis=0, keepdims=True)
            gain_send[1:2, :] = gain_term if index == 0 else gain_send[1:2, :] + gain_term
        start("branch")
        run("A8")
        for load_of in loads:
            load_of.wait()
        context_grad[...] = sum(
            against_rows(branch_low[:, i * block : (i + 1) * block], bank[at_o + i])
            for i in range(width // block)
        ).astype(BF16)
        q_total = jnp.zeros((1, head_width), F32)
        k_total = jnp.zeros((1, head_width), F32)
        for kv in range(sz.kv_heads):
            kv_at = slice(kv * head_width, (kv + 1) * head_width)
            keys, values = k_low[:, kv_at], v_low[:, kv_at]
            keys_grad = values_grad = 0.0
            for member in range(group):
                head = kv * group + member
                at = slice(head * head_width, (head + 1) * head_width)
                head_grad = context_grad[:, at]
                prob = probs_of(head)[...]
                prob_grad = against_rows(head_grad, values)
                values_grad += across_rows(prob.astype(BF16), head_grad)
                inner = jnp.sum(prob * prob_grad, axis=-1, keepdims=True)
                score_grad = (prob * (prob_grad - inner)).astype(BF16)
                queries_grad = rows_dot(score_grad, keys) * sz.scale
                keys_grad += across_rows(score_grad, q_low[:, at])
                head_low, head_total = turned_back(queries_grad, q_lin[:, at], query_gain)
                lows[0][:, at] = head_low.astype(F32)
                q_total += head_total
            head_low, head_total = turned_back(keys_grad * sz.scale, k_lin[:, kv_at], key_gain)
            k_total += head_total
            lows[1][:, kv_at] = head_low.astype(F32)
            at = k_cols + kv * head_width
            lows[1][:, at : at + head_width] = values_grad.astype(BF16).astype(F32)
        start(("low", 0), ("low", 1))
        run("A9")
        half_rows = pl.ds(pl.multiple_of(grad_base, 8), sz.grad_rows)
        arrived("ctx", "branch")
        for i in range(width // block):
            at = slice(i * block, (i + 1) * block)
            attn_grads[half_rows, at] = across_rows(
                context[:, own_half(q_cols // 2)], branch[:, at].astype(BF16)
            ) + across_rows(ctx_recv[...].astype(BF16), branch_recv[:, at].astype(BF16))
        arrived("attn", ("low", 0), ("low", 1))
        for k in range(2):
            for i in range(width // block):
                at = slice(i * block, (i + 1) * block)
                first = (k + 1) * width + i * block
                attn_grads[half_rows, first : first + block] = across_rows(
                    attn_low[:, own_half(width // 2)], lows[k][:, at].astype(BF16)
                ) + across_rows(attn_recv[...].astype(BF16), low_recvs[k][:, at].astype(BF16))
        for s in range(sz.streams):
            start(("su", s, 1), ("sd", s, 1))
        sent(("part", 1, 0), ("part", 1, 1))
        part[1, :rows] = sum(
            against_rows(
                lows[i // q_blocks][:, i % q_blocks * block : (i % q_blocks + 1) * block].astype(BF16),
                bank[i],
            )
            for i in range(at_o)
        )
        part[1, rows:] = jnp.zeros((8, width), F32)
        part[1, rows : rows + 1, :head_width] = q_total
        part[1, rows : rows + 1, head_width : 2 * head_width] = k_total
        run("A10")
        sent("ctx", "attn", "branch", ("low", 0), ("low", 1))

    pl.run_scoped(
        first_phase,
        pltpu.VMEM((max(at_o + width // block, 2 * unit_blocks), width, block), BF16),
        pltpu.VMEM(w_down.shape, BF16),
        pltpu.VMEM((rows, q_cols), BF16),
        pltpu.VMEM((rows, k_cols), BF16),
        pltpu.VMEM((rows, k_cols), BF16),
        pltpu.VMEM((rows, q_cols), BF16),
        pltpu.VMEM((rows, width), BF16),
        pltpu.VMEM((rows, units), BF16),
        pltpu.VMEM((rows, q_cols), BF16),
        pltpu.VMEM((rows, width), BF16),
        pltpu.VMEM((rows, width), BF16),
    )

    def second_phase(
        wg, wu, wd, staged, ffn_low, ffn_turned, cot_low
    ):
        scoped["staged"] = staged
        weight_loads = [
            pltpu.make_async_copy(src, dst, local_sems.at[i])
            for i, (src, dst) in enumerate(
                (
                    (w_gate.at[:, own_half(half_units)], wg),
                    (w_up.at[:, own_half(half_units)], wu),
                    (w_down.at[pl.ds(pl.multiple_of(core * half_units, 8), half_units)], wd),
                )
            )
        ]
        for load in weight_loads:
            load.start()

        for a in (COT, FFN):
            sent(("up", a, 1), ("down", a, 1), ("core", a, 0))
        arrived(("core", COT, 0), ("core", FFN, 0))
        for copy in stage_copies(0, True):
            copy.start()
        for load in weight_loads:
            load.wait()
        chunks = 3
        size = half_units // chunks
        def step(i, _):
            slot, j = i // chunks, i % chunks

            @pl.when(j == 0)
            def _():
                for copy in stage_copies(slot, False):
                    copy.wait()
                for lane in range(2):
                    here = pl.ds(lane * rows, rows)
                    low_block = staged[FFN, lane].astype(BF16)
                    ffn_low[here] = low_block
                    ffn_turned[:, lane * rows : (lane + 1) * rows] = low_block.T
                    cot_low[here] = staged[COT, lane].astype(BF16)

            def events(part_of_step):
                for when in PLAN:
                    if isinstance(when, tuple) and when[0] < chunks * slots and when[1] == part_of_step:

                        @pl.when(i == when[0])
                        def _():
                            run(when)

            events(0)
            at_units = pl.ds(pl.multiple_of(j * size, 128), size)
            hidden, gate_grad, up_grad = ffn_middle(
                ffn_low[...], cot_low[...], wg[:, at_units], wu[:, at_units], wd[at_units]
            )
            events(1)
            down = across_rows(hidden, cot_low[...])
            gate = rows_dot(ffn_turned[...], gate_grad)
            up = rows_dot(ffn_turned[...], up_grad)

            grad_units = core * half_units + j * size
            grad_cols = pl.ds(pl.multiple_of(grad_units, 128), size)

            @pl.when(slot == 0)
            def _():
                gate_grads[:, grad_cols] = gate
                up_grads[:, grad_cols] = up
                down_grads[grad_cols] = down

            @pl.when(slot > 0)
            def _():
                gate_grads[:, grad_cols] += gate
                up_grads[:, grad_cols] += up
                down_grads[grad_cols] += down

            events(2)
            return 0

        lax.fori_loop(0, chunks * slots, step, 0)
        for k in range(3):
            start(("out", k))
        run((chunks * slots, 0))
        for k in range(3):
            arrived(("out", k))

    pl.run_scoped(
        second_phase,
        pltpu.VMEM((width, half_units), BF16),
        pltpu.VMEM((width, half_units), BF16),
        pltpu.VMEM((half_units, width), BF16),
        pltpu.VMEM((2, 2, rows, width), F32),
        pltpu.VMEM((2 * rows, width), BF16),
        pltpu.VMEM((width, 2 * rows), BF16),
        pltpu.VMEM((2 * rows, width), BF16),
    )
    for s in range(sz.streams):
        for h in range(half + 1):
            arrived(("cu", s, h))
            if h:
                arrived(("cd", s, h))
    for name in book:
        if name not in waited:
            made(name).wait_send()


def results_kernel(*refs):
    count = 10
    held, places, sems = refs[:count], refs[count:-1], refs[-1]
    moves = list(zip(held[:-1], places))
    first = 0
    for dst in places[count - 1 :]:
        moves.append((held[-1].at[:, pl.ds(first, dst.shape[1])], dst))
        first += dst.shape[1]
    copies = [
        pltpu.make_async_copy(src, dst, sems.at[k]) for k, (src, dst) in enumerate(moves)
    ]
    for copy in copies:
        copy.start()
    for copy in copies:
        copy.wait()


def over_groups(sz, dp_size, values):
    step = sz.group
    while step < dp_size:
        values = values + lax.ppermute(values, "dp", [(d, d ^ step) for d in range(dp_size)])
        step *= 2
    return values


def per_device(
    dp_size,
    tokens,
    segments,
    positions,
    attn_gain,
    w_query,
    key_weight,
    value_weight,
    query_gain,
    key_gain,
    w_out,
    ffn_gain,
    w_gate,
    w_up,
    w_down,
    cotangent,
):
    sz = Sizes(dp_size, tokens.shape, w_query.shape, key_weight.shape, query_gain.shape, w_gate.shape)
    rows, width, head_width, half = sz.rows, sz.width, sz.head_width, sz.half
    q_cols, k_cols = sz.q_cols, sz.k_cols
    lanes = np.arange(head_width) % (head_width // 2)
    inverse = (THETA ** (-2.0 * lanes / head_width)).astype(np.float32)[None]
    vmem = pl.BlockSpec(memory_space=pltpu.VMEM)
    anywhere = pl.BlockSpec(memory_space=pl.ANY)
    slots = 2 * half
    transfers = 119
    mixed, tokens_grad, *others = pl.pallas_call(
        functools.partial(layer_kernel, sz),
        out_shape=[
            pltpu.VMEM((rows, width), BF16),
            pltpu.VMEM((rows, width), BF16),
            pltpu.VMEM((1, width), F32),
            pltpu.VMEM((1, width), F32),
            pltpu.VMEM((1, head_width), F32),
            pltpu.VMEM((1, head_width), F32),
            pltpu.VMEM((width, sz.grad_cols), F32),
            pltpu.VMEM(w_gate.shape, F32),
            pltpu.VMEM(w_up.shape, F32),
            pltpu.VMEM(w_down.shape, F32),
            shaped(2, slots, rows, width),
            shaped(2, slots, rows, width),
        ],
        in_specs=[anywhere] * 16,
        out_specs=[vmem] * 10 + [anywhere] * 2,
        scratch_shapes=[
            pltpu.VMEM((rows, width), BF16),
            pltpu.VMEM((rows, width), BF16),
            pltpu.VMEM((1, rows), jnp.int32),
            pltpu.VMEM((1, rows), jnp.int32),
            pltpu.VMEM((1, head_width), F32),
            pltpu.VMEM((1, width), F32),
            pltpu.VMEM((1, head_width), F32),
            pltpu.VMEM((1, head_width), F32),
            pltpu.VMEM((1, width), F32),
            pltpu.VMEM((2, rows + 8, width), F32),
            pltpu.VMEM((2, rows + 8, width), F32),
            pltpu.VMEM((rows, width), F32),
            pltpu.VMEM((half, sz.piece, sz.grad_cols), F32),
            pltpu.VMEM((half, sz.piece, sz.grad_cols), F32),
            pltpu.VMEM((8, width), F32),
            pltpu.VMEM((8, width), F32),
            pltpu.VMEM((sz.chips, 8, width), F32),
            pltpu.SemaphoreType.DMA((transfers,)),
            pltpu.SemaphoreType.DMA((transfers,)),
            pltpu.SemaphoreType.DMA((32,)),
        ],
        compiler_params=pltpu.CompilerParams(
            collective_id=0, has_side_effects=True, vmem_limit_bytes=VMEM_BYTES
        ),
    )(
        tokens, cotangent, segments, positions, jnp.asarray(inverse), attn_gain[None], query_gain[None], key_gain[None],
        ffn_gain[None], w_query, key_weight, value_weight, w_out, w_gate, w_up, w_down,
    )
    sums = [over_groups(sz, dp_size, values) for values in others[:-2]]
    attn_grads = sums.pop(4)
    results = [mixed, tokens_grad, *sums, attn_grads]
    places = [shaped(*v.shape, kind=v.dtype) for v in results[:-1]]
    places += [shaped(*v.shape) for v in (w_out, w_query, key_weight, value_weight)]
    (
        mixed, tokens_grad, attn_gain_grad, ffn_gain_grad, query_gain_grad, key_gain_grad,
        w_gate_grad, w_up_grad, w_down_grad, w_out_grad, w_query_grad, w_key_grad, w_value_grad,
    ) = pl.pallas_call(
        results_kernel,
        out_shape=places,
        in_specs=[anywhere] * len(results),
        out_specs=[anywhere] * len(places),
        scratch_shapes=[pltpu.SemaphoreType.DMA((len(places),))],
        compiler_params=pltpu.CompilerParams(vmem_limit_bytes=RESULTS_VMEM_BYTES),
    )(*[pltpu.with_memory_space_constraint(values, pltpu.VMEM) for values in results])
    return (
        mixed,
        tokens_grad,
        attn_gain_grad[0],
        w_query_grad,
        w_key_grad,
        w_value_grad,
        query_gain_grad[0],
        key_gain_grad[0],
        w_out_grad,
        ffn_gain_grad[0],
        w_gate_grad,
        w_up_grad,
        w_down_grad,
    )


def solution(mesh):
    def layer(*arrays):
        return per_device(mesh.shape["dp"], *arrays)

    return jax.shard_map(
        layer,
        mesh=mesh,
        in_specs=(
            P("dp", None),
            P("dp", None),
            P("dp", None),
            P(),
            P(None, "tensor"),
            P(None, "tensor"),
            P(None, "tensor"),
            P(),
            P(),
            P("tensor", None),
            P(),
            P(None, "tensor"),
            P(None, "tensor"),
            P("tensor", None),
            P("dp", None),
        ),
        out_specs=(
            P("dp", None),
            P("dp", None),
            P(),
            P(None, "tensor"),
            P(None, "tensor"),
            P(None, "tensor"),
            P(),
            P(),
            P("tensor", None),
            P(),
            P(None, "tensor"),
            P(None, "tensor"),
            P("tensor", None),
        ),
        check_vma=False,
    )
```

```python
import functools
import math

import jax
import jax.numpy as jnp
import numpy as np
from jax import lax
from jax.experimental import pallas as pl
from jax.experimental.pallas import tpu as pltpu
from jax.sharding import PartitionSpec as P

EPS = 1e-06
THETA = 1000000.0
F32 = jnp.float32
BF16 = jnp.bfloat16
MESH = pl.DeviceIdType.MESH
VMEM_BYTES = 32 * 2**20
RESULTS_VMEM_BYTES = 2**20
GROUP = 16
COT, FFN = 0, 1
SHARES = ((2, 2, 2, 3), (4, 4, 4, 4))


PLAN = {
    "A2": [
        ("ring", COT, 1),
    ],
    "A5": [
        ("start", "x", COT, 1),
        ("ring", COT, 2),
    ],
    "A7": [
        ("start", "x", COT, 2),
        ("start", "x", COT, 3),
        ("start", "x", COT, 4),
        ("ring", FFN, 1),
    ],
    "A10": [
        ("x_done", COT, 1),
        ("start", "x", FFN, 1),
        ("ring", COT, 3),
        ("x_done", COT, 2),
        ("start", "x", FFN, 2),
    ],
    (0, 1): [
        ("x_done", COT, 3),
        ("start", "x", COT, 5),
    ],
    (2, 0): [
        ("x_done", COT, 4),
        ("start", "x", COT, 6),
        ("ring", FFN, 2),
    ],
    (2, 1): [
        ("gain_sum",),
    ],
    (2, 2): [
        ("sum", 0, 1),
        ("gain", 0),
        ("sum", 1, 1),
        ("x_done", FFN, 1),
        ("start", "x", FFN, 3),
        ("stage", 1),
    ],
    (3, 0): [
        ("ring", COT, 4),
    ],
    (4, 1): [
        ("x_done", FFN, 2),
        ("start", "x", FFN, 4),
    ],
    (5, 1): [
        ("ring", FFN, 3),
        ("stage", 2),
    ],
    (6, 0): [
        ("x_done", COT, 5),
        ("start", "x", FFN, 5),
    ],
    (7, 0): [
        ("x_done", COT, 6),
        ("start", "x", FFN, 6),
    ],
    (7, 1): [
        ("sum", 0, 2),
        ("gain", 1),
    ],
    (8, 2): [
        ("sum", 1, 2),
        ("x_done", FFN, 3),
        ("start", "x", COT, 7),
        ("stage", 3),
    ],
    (9, 0): [
        ("ring", FFN, 4),
    ],
    (10, 1): [
        ("x_done", FFN, 4),
        ("start", "x", FFN, 7),
    ],
    (11, 0): [
        ("sum", 0, 3),
        ("gain", 2),
    ],
    (11, 1): [
        ("stage", 4),
    ],
    (13, 0): [
        ("sum", 1, 3),
        ("x_done", FFN, 5),
        ("start", "part", 2),
    ],
    (14, 1): [
        ("stage", 5),
    ],
    (15, 0): [
        ("sum", 0, 4),
        ("gain", 3),
    ],
    (15, 1): [
        ("x_done", FFN, 6),
        ("start", "part", 3),
    ],
    (17, 0): [
        ("stage", 6),
    ],
    (17, 1): [
        ("sum", 1, 4),
    ],
    (18, 0): [
        ("x_done", COT, 7),
    ],
    (19, 1): [
        ("gather", 0, 1),
        ("gain", 4),
    ],
    (20, 2): [
        ("x_done", FFN, 7),
        ("gather", 1, 1),
        ("stage", 7),
    ],
    (22, 0): [
        ("gather", 0, 2),
    ],
    (24, 0): [
        ("gather", 1, 2),
        ("tokens",),
        ("gather", 0, 3),
        ("gather", 1, 3),
        ("gather", 0, 4),
        ("mixed",),
        ("gather", 1, 4),
    ],
}


def norm_factor(values):
    return lax.rsqrt(jnp.mean(values * values, axis=-1, keepdims=True) + EPS)


def norm_grad(grad_out, unit_rows, factor, scale_gain):
    scaled = grad_out * scale_gain
    return factor * (scaled - unit_rows * jnp.mean(scaled * unit_rows, axis=-1, keepdims=True))


def rows_dot(leading, trailing):
    return jnp.dot(leading, trailing, preferred_element_type=F32)


def across_rows(leading, trailing):
    return lax.dot_general(
        leading, trailing, (((0,), (0,)), ((), ())), preferred_element_type=F32
    )


def against_rows(leading, trailing):
    return lax.dot_general(
        leading, trailing, (((1,), (1,)), ((), ())), preferred_element_type=F32
    )


def ffn_middle(low_in, cot, wg, wu, wd):
    gate = rows_dot(low_in, wg)
    up = rows_dot(low_in, wu)
    sig = jax.nn.sigmoid(gate)
    silu = gate * sig
    hidden = (silu * up).astype(BF16)
    hidden_grad = against_rows(cot, wd)
    up_grad = (hidden_grad * silu).astype(BF16)
    gate_grad = (hidden_grad * up * sig * (1.0 + gate * (1.0 - sig))).astype(BF16)
    return hidden, gate_grad, up_grad


def shaped(*shape, kind=F32):
    return jax.ShapeDtypeStruct(shape, kind)


class Sizes:
    def __init__(self, dp_size, tokens, w_query, key_weight, query_gain, w_gate):
        self.rows, self.width = tokens
        self.head_width = query_gain[0]
        self.q_cols, self.k_cols = w_query[1], key_weight[1]
        self.heads, self.kv_heads = self.q_cols // self.head_width, self.k_cols // self.head_width
        self.units = w_gate[1]
        self.all_cols = self.q_cols + 2 * self.k_cols
        self.scale = 1.0 / math.sqrt(self.head_width)
        self.group = math.gcd(GROUP, dp_size)
        self.chips = self.group // 2
        self.half = self.chips // 2
        self.share = tuple(tuple(self.width * part // 8 for part in parts) for parts in SHARES)
        self.grad_rows = self.width // 2
        self.grad_cols = self.width + self.all_cols
        self.piece = self.grad_rows // self.chips
        self.streams = 2


def layer_kernel(
    sz,
    tokens_in, cot_in, segments_in, positions_in, inverse_in, attn_gain_in, query_gain_in, key_gain_in,
    ffn_gain_in,
    w_query, key_weight, value_weight, w_out, w_gate, w_up, w_down,
    mixed, tokens_grad, attn_gain_grad, ffn_gain_grad, query_gain_grad, key_gain_grad,
    attn_grads, gate_grads, up_grads, down_grads,
    mine, theirs,
    tokens, cot, segments, positions, inverse, attn_gain, query_gain, key_gain, ffn_gain,
    part, part_theirs, middle_grad, sum_up, sum_down, gain_part, gain_theirs,
    gain_send, gain_recv, gain_slots,
    send_sems, recv_sems, local_sems,
):
    rows, width, head_width = sz.rows, sz.width, sz.head_width
    q_cols, k_cols, units = sz.q_cols, sz.k_cols, sz.units
    n, half, piece = sz.chips, sz.half, sz.piece
    half_units = units // 2
    mid = rows // 2

    device = lax.axis_index("dp")
    base = device // sz.group * sz.group
    core = device % 2
    chip = device % sz.group // 2
    line = chip % 2
    place = chip // 2 + line * (2 * half - 1 - 2 * (chip // 2))
    side = lax.axis_index("tensor")

    def device_at(position):
        position = position % n
        second = position // half
        return base + (2 * (position + second * (2 * half - 1 - 2 * position)) + second) * 2 + core

    forward = {"dp": device_at(place + 1)}
    backward = {"dp": device_at(place + n - 1)}
    sibling = {"dp": base + chip * 2 + 1 - core}
    across = {"tensor": 1 - side}

    barrier = pltpu.get_barrier_semaphore()
    for neighbour in (forward, backward, sibling, across):
        pl.semaphore_signal(barrier, inc=1, device_id=neighbour, device_id_type=MESH)
    small_loads = [
        pltpu.make_async_copy(src, dst, local_sems.at[16 + k])
        for k, (src, dst) in enumerate(
            (
                (cot_in, cot),
                (tokens_in, tokens),
                (attn_gain_in, attn_gain),
                (segments_in, segments),
                (positions_in, positions),
                (inverse_in, inverse),
                (query_gain_in, query_gain),
                (key_gain_in, key_gain),
                (ffn_gain_in, ffn_gain),
            )
        )
    ]
    for load in small_loads:
        load.start()

    book = {}
    waited = set()

    def remote(name, src, dst, target):
        book[name] = (len(book), src, dst, target)

    def made(name):
        index, src, dst, target = book[name]
        return pltpu.make_async_remote_copy(
            src_ref=src, dst_ref=dst, send_sem=send_sems.at[index], recv_sem=recv_sems.at[index],
            device_id=target, device_id_type=MESH,
        )

    def sent(*names):
        for name in names:
            made(name).wait_send()
            waited.add(name)

    def start(*names):
        for name in names:
            made(name).start()

    def arrived(*names):
        for name in names:
            made(name).wait_recv()

    def cols(first, count):
        return pl.ds(pl.multiple_of(first, 128), count)

    def piece_rows(index, first=0, count=piece, base_row=0):
        return pl.ds(pl.multiple_of(base_row + index % n * piece + first, 8), count)

    grad_base = core * sz.grad_rows
    slots = 2 * half
    up_slot = lambda h: 2 * h - 1
    down_slot = lambda h: 2 * h
    last = slots - 1
    up_place = lambda row, first, count: up_grads.at[pl.ds(row * rows, rows), pl.ds(first, count)]
    down_place = lambda row: down_grads.at[pl.ds(row * rows, rows)]
    half_width = width // 2
    gate_place = lambda row: gate_grads.at[pl.ds(row * rows, rows), pl.ds(units - width, width)]
    own = (gate_place(0), gate_place(1))
    for a in (COT, FFN):
        for h in range(1, half + 1):
            share = sz.share[a][h - 1]
            window = cols(side * share, width - share)
            shared = cols(side * (width - share), share)
            up = own[a] if h == 1 else mine.at[a, up_slot(h - 1)]
            down = own[a] if h == 1 else mine.at[a, down_slot(h - 1)]
            if h < half:
                remote(("up", a, h), up.at[:, window], mine.at[a, up_slot(h), :, window], forward)
                remote(
                    ("down", a, h), down.at[:, window], mine.at[a, down_slot(h), :, window], backward
                )
                of_distance = (up_slot(h), down_slot(h))
            else:
                first, second = pl.ds(0, mid), pl.ds(mid, mid)
                remote(("up", a, h), up.at[first, window], mine.at[a, last, first, window], forward)
                remote(
                    ("down", a, h), down.at[second, window], mine.at[a, last, second, window], backward
                )
                of_distance = (last,)
            for s in of_distance:
                remote(("x", a, s), mine.at[a, s, :, shared], mine.at[a, s, :, shared], across)
        for s in range(slots):
            remote(("core", a, s), own[a] if s == 0 else mine.at[a, s], theirs.at[a, s], sibling)
    halves = (slice(0, mid), slice(mid, rows))
    for k in range(2):
        for index, at_rows in enumerate(halves):
            at_rows = pl.ds(at_rows.start, mid)
            remote(
                ("part", k, index), part.at[k, at_rows], part_theirs.at[k, at_rows], across
            )
        remote(("part", 2 + k), part.at[1 - k], part_theirs.at[k], across)
    stream_cols = sz.grad_cols // sz.streams
    small = piece // 2
    for s in range(sz.streams):
        c = pl.ds(s * stream_cols, stream_cols)
        for h in range(1, half + 1):
            size, skip = (small, small) if h == 1 else (piece, 0)
            src = attn_grads.at[piece_rows(place + half, 0, small, grad_base), c]
            remote(
                ("su", s, h), src if h == 1 else sum_up.at[h - 2, :, c],
                sum_up.at[h - 1, pl.ds(0, size), c], forward,
            )
            src = attn_grads.at[piece_rows(place + half, small, small, grad_base), c]
            remote(
                ("sd", s, h), src if h == 1 else sum_down.at[h - 2, :, c],
                sum_down.at[h - 1, pl.ds(skip, size), c], backward,
            )
        for h in range(1, half + 1):
            size, skip = (small, small) if h == half else (piece, 0)
            going_up = attn_grads.at[piece_rows(place + n - h + 1, 0, size, grad_base), c]
            going_down = attn_grads.at[piece_rows(place + h - 1, skip, size, grad_base), c]
            remote(("gu", s, h), going_up, going_up, forward)
            remote(("gd", s, h), going_down, going_down, backward)
            got_up = attn_grads.at[piece_rows(place + n - h, 0, size, grad_base), c]
            got_down = attn_grads.at[piece_rows(place + h, skip, size, grad_base), c]
            remote(("cu", s, h), got_up, got_up, sibling)
            remote(("cd", s, h), got_down, got_down, sibling)
        own_piece = attn_grads.at[piece_rows(place, 0, piece, grad_base), c]
        remote(("cu", s, 0), own_piece, own_piece, sibling)
    remote("gain_parts", gain_part, gain_theirs, across)
    remote("gains", gain_send, gain_recv, sibling)
    for h in range(1, half + 1):
        slot = gain_slots.at[(place + n - h + 1) % n]
        remote(("vu", h), slot, slot, forward)
        if h < half:
            slot = gain_slots.at[(place + h - 1) % n]
            remote(("vd", h), slot, slot, backward)

    def ring_step(a, h):
        arrived(("up", a, h), ("down", a, h))
        if h < half:
            start(("up", a, h + 1), ("down", a, h + 1))

    def x_start(a, s):
        start(("x", a, s))

    def x_done(a, s):
        arrived(("x", a, s))
        start(("core", a, s))


    def stream(s):
        return pl.ds(s * stream_cols, stream_cols)

    def sum_step(s, h):
        arrived(("su", s, h), ("sd", s, h))
        c = stream(s)
        up_rows = piece_rows(place + half - h, 0, piece, grad_base)
        down_rows = piece_rows(place + n - half + h, 0, piece, grad_base)
        if h == 1:
            sent(("su", s, 1), ("sd", s, 1))
            up, down = attn_grads[up_rows, c], attn_grads[down_rows, c]
            sum_up[0, :small, c] += up[:small]
            sum_up[0, small:, c] = up[small:]
            sum_down[0, :small, c] = down[:small]
            sum_down[0, small:, c] += down[small:]
        elif h < half:
            sum_up[h - 1, :, c] += attn_grads[up_rows, c]
            sum_down[h - 1, :, c] += attn_grads[down_rows, c]
        if h < half:
            start(("su", s, h + 1), ("sd", s, h + 1))
        else:
            own_rows = piece_rows(place, 0, piece, grad_base)
            attn_grads[own_rows, c] += sum_up[h - 1, :, c] + sum_down[h - 1, :, c]
            start(("gu", s, 1), ("gd", s, 1), ("cu", s, 0))

    def gather_step(s, h):
        arrived(("gu", s, h), ("gd", s, h))
        if h < half:
            start(("gu", s, h + 1), ("gd", s, h + 1))
        start(("cu", s, h), ("cd", s, h))

    def finish_tokens():
        arrived(("part", 2))
        grad = part[1] + part_theirs[0]
        value = tokens[...].astype(F32)
        factor = norm_factor(value)
        unit = value * factor
        tokens_grad[...] = (
            middle_grad[...] + norm_grad(grad, unit, factor, attn_gain[...])
        ).astype(BF16)

    def finish_mixed():
        arrived(("part", 3))
        mixed[...] = (part[0] + part_theirs[1]).astype(BF16)

    def gain_sum():
        arrived("gain_parts")
        gain_send[...] = gain_part[...] + gain_theirs[...]
        start("gains")

    def gain_first():
        arrived("gains")
        gain_slots[place] = gain_send[...] + gain_recv[...]
        start(("vu", 1), ("vd", 1))

    def gain_step(h):
        arrived(("vu", h))
        if h < half:
            arrived(("vd", h))
            start(("vu", h + 1))
            if h + 1 < half:
                start(("vd", h + 1))
        else:
            total = gain_slots[0]
            for chip_at in range(1, n):
                total = total + gain_slots[chip_at]
            attn_gain_grad[...] = total[0:1, :]
            ffn_gain_grad[...] = total[1:2, :]
            query_gain_grad[...] = total[2:3, :head_width]
            key_gain_grad[...] = total[2:3, head_width : 2 * head_width]

    def stage(slot):
        arrived(("core", COT, slot), ("core", FFN, slot))
        for copy in stage_copies(slot, False):
            copy.start()

    scoped = {}

    def stage_copies(slot, first):
        staged = scoped["staged"]
        copies = []
        for a in (COT, FFN):
            src = own[a] if first else mine.at[a, slot]
            copies.append(pltpu.make_async_copy(src, staged.at[a, 0], local_sems.at[9 + 2 * a]))
            copies.append(
                pltpu.make_async_copy(theirs.at[a, slot], staged.at[a, 1], local_sems.at[10 + 2 * a])
            )
        return copies

    def gain_event(h):
        if h == 0:
            gain_first()
        else:
            gain_step(h)

    actions = {
        "ring": ring_step,
        "start": lambda *name: start(name),
        "x_done": x_done,
        "sum": sum_step,
        "gather": gather_step,
        "stage": stage,
        "gain_sum": gain_sum,
        "tokens": finish_tokens,
        "gain": gain_event,
        "mixed": finish_mixed,
    }

    def run(when):
        for event in PLAN.get(when, ()):
            actions[event[0]](*event[1:])

    group = q_cols // k_cols
    other_half = lambda count: cols((1 - core) * count, count)
    own_half = lambda count: cols(core * count, count)

    block = k_cols
    q_blocks, unit_blocks = q_cols // block, units // block
    at_k, at_v, at_o = q_blocks, q_blocks + 1, q_blocks + 2

    half_down = down_grads.at[pl.ds(pl.multiple_of(core * half_units, 8), half_units)]
    outs = (gate_grads.at[:, own_half(half_units)], up_grads.at[:, own_half(half_units)], half_down)
    for k, out in enumerate(outs):
        remote(("out", k), out, out, sibling)

    q_lin, k_lin = up_place(0, 0, q_cols), up_place(0, q_cols, k_cols)
    ctx_send, ctx_recv = up_place(1, 0, q_cols // 2), up_place(1, q_cols // 2, q_cols // 2)
    cosine, sine = up_place(1, q_cols, head_width), up_place(1, q_cols + head_width, head_width)
    attn_send, attn_recv = up_place(2, 0, half_width), up_place(2, half_width, half_width)
    mask = up_place(3, 0, rows)
    lows, low_recvs = (down_place(0), down_place(1)), (down_place(2), down_place(3))
    branch, branch_recv = down_place(4), down_place(5)
    deep = width // rows
    middle = gate_place(2)

    def probs_of(head):
        return gate_grads.at[pl.ds(head % deep * rows, rows), pl.ds(head // deep * rows, rows)]

    remote("ctx", ctx_send, ctx_recv, sibling)
    remote("attn", attn_send, attn_recv, sibling)
    remote("branch", branch, branch_recv, sibling)
    for k in range(2):
        remote(("low", k), lows[k], low_recvs[k], sibling)

    def first_phase(
        bank, wd, q_low, k_low, v_low, context, ffn_low, hidden, context_grad, attn_low, branch_low
    ):
        def load(src, dst, index):
            copy = pltpu.make_async_copy(src, dst, local_sems.at[index])
            copy.start()
            return copy

        def block_of(weights, index):
            return weights.at[:, pl.ds(index * block, block)]

        def load_attention():
            order = [(w_query, i) for i in range(q_blocks)] + [(key_weight, 0), (value_weight, 0)]
            order += [(w_out, i) for i in range(width // block)]
            return [load(block_of(w, i), bank.at[k], k) for k, (w, i) in enumerate(order)]

        def load_ffn():
            order = [(w, i) for w in (w_gate, w_up) for i in range(unit_blocks)]
            return [load(block_of(w, i), bank.at[k], k) for k, (w, i) in enumerate(order)]

        loads = load_attention()
        down_load = load(w_down, wd, 15)

        def head_norm(lin, gain):
            return lin * norm_factor(lin) * gain[...]

        def turned(lin, gain, at_rows):
            normed = head_norm(lin, gain)
            swapped = pltpu.roll(normed, head_width // 2, 1)
            return (normed * cosine[at_rows] + swapped * sine[at_rows]).astype(BF16)

        def turned_back(grad, lin, gain):
            back = grad * cosine[...] - pltpu.roll(grad, head_width // 2, 1) * sine[...]
            factor = norm_factor(lin)
            unit = lin * factor
            return (
                norm_grad(back, unit, factor, gain[...]).astype(BF16),
                jnp.sum(back * unit, axis=0, keepdims=True),
            )

        small_loads[0].wait()
        own[COT][...] = cot[...].astype(F32)
        pl.semaphore_wait(barrier, 4)
        start(("up", COT, 1), ("down", COT, 1), ("core", COT, 0))

        for small in small_loads[1:]:
            small.wait()
        resid = tokens[...].astype(F32)
        attn_in = (resid * norm_factor(resid) * attn_gain[...]).astype(BF16)
        attn_low[...] = attn_in
        attn_send[...] = attn_low[:, other_half(width // 2)].astype(F32)
        start("attn")

        def down_rows(row):
            return jnp.broadcast_to(row.astype(F32), (head_width, rows)).T

        segment_rows = jnp.concatenate([down_rows(segments[...])] * (rows // head_width), 1)
        same = segment_rows == jnp.broadcast_to(segments[...].astype(F32), (rows, rows))
        row_at = lax.broadcasted_iota(jnp.int32, (rows, rows), 0)
        column_at = lax.broadcasted_iota(jnp.int32, (rows, rows), 1)
        mask[...] = jnp.where(same & (row_at >= column_at), 1.0, 0.0)
        angles = down_rows(positions[...]) * inverse[...]
        lane = lax.broadcasted_iota(jnp.int32, (rows, head_width), 1)
        cosine[...] = jnp.cos(angles)
        sine[...] = jnp.where(lane < head_width // 2, -1.0, 1.0) * jnp.sin(angles)
        for i in range(q_blocks):
            loads[i].wait()
            q_lin[:, i * block : (i + 1) * block] = rows_dot(attn_in, bank[i])
        loads[at_k].wait()
        k_lin[...] = rows_dot(attn_in, bank[at_k])
        loads[at_v].wait()
        v_low[...] = rows_dot(attn_in, bank[at_v]).astype(BF16)
        run("A1")
        for kv in range(sz.kv_heads):
            kv_at = slice(kv * head_width, (kv + 1) * head_width)
            k_low[:, kv_at] = turned(k_lin[:, kv_at], key_gain, slice(0, rows))
        for index, at_rows in enumerate(halves):
            seen = at_rows.stop
            for head in range(sz.heads):
                at = slice(head * head_width, (head + 1) * head_width)
                kv_at = slice(head // group * head_width, (head // group + 1) * head_width)
                queries = turned(q_lin[at_rows, at], query_gain, at_rows)
                q_low[at_rows, at] = queries
                scores = against_rows(queries, k_low[:seen, kv_at]) * sz.scale
                scores = jnp.where(mask[at_rows, :seen] > 0, scores, -1e30)
                raised = jnp.exp(scores - jnp.max(scores, axis=-1, keepdims=True))
                prob = raised / jnp.sum(raised, axis=-1, keepdims=True)
                place_of = probs_of(head)
                place_of[at_rows, :seen] = prob
                if seen < rows:
                    place_of[at_rows, seen:] = jnp.zeros((mid, rows - seen), F32)
                context[at_rows, at] = rows_dot(prob.astype(BF16), v_low[:seen, kv_at]).astype(BF16)
            for i in range(width // block):
                if index == 0:
                    loads[at_o + i].wait()
                at = slice(i * block, (i + 1) * block)
                part[0, at_rows, at] = rows_dot(context[at_rows], bank[at_o + i])
            start(("part", 0, index))
        ctx_send[...] = context[:, other_half(q_cols // 2)].astype(F32)
        start("ctx")
        loads = load_ffn()
        for index, at_rows in enumerate(halves):
            run("A2" if index == 0 else "A3")
            arrived(("part", 0, index))
            value = tokens[at_rows].astype(F32) + (part[0, at_rows] + part_theirs[0, at_rows])
            middle[at_rows] = value
            low_rows = (value * norm_factor(value) * ffn_gain[...]).astype(BF16)
            ffn_low[at_rows] = low_rows
            own[FFN][at_rows] = low_rows.astype(F32)
            if index == 0:
                down_load.wait()
                for load_of in loads:
                    load_of.wait()
            else:
                start(("up", FFN, 1), ("down", FFN, 1), ("core", FFN, 0))
                run("A4")
            for i in range(unit_blocks):
                at = slice(i * block, (i + 1) * block)
                wg, wu = bank[i], bank[unit_blocks + i]
                low_hidden, gate_grad, up_grad = ffn_middle(low_rows, cot[at_rows], wg, wu, wd[at])
                hidden[at_rows, at] = low_hidden
                term = against_rows(gate_grad, wg) + against_rows(up_grad, wu)
                if i == 0:
                    part[1, at_rows] = term
                else:
                    part[1, at_rows] += term
            start(("part", 1, index))
        loads = load_attention()
        run("A5")
        sent(("part", 0, 0), ("part", 0, 1))
        part[0] = rows_dot(hidden[...], wd[...]) + 0.5 * middle[...]

        for index, at_rows in enumerate(halves):
            run("A6" if index == 0 else "A7")
            arrived(("part", 1, index))
            grad = part[1, at_rows] + part_theirs[1, at_rows]
            value = middle[at_rows]
            factor = norm_factor(value)
            unit = value * factor
            total = cot[at_rows].astype(F32) + norm_grad(grad, unit, factor, ffn_gain[...])
            middle_grad[at_rows] = total
            branch_low[at_rows] = total.astype(BF16)
            branch[at_rows] = total.astype(BF16).astype(F32)
            gain_term = jnp.sum(grad * unit, axis=0, keepdims=True)
            gain_part[1:2, :] = gain_term if index == 0 else 0.5 * (gain_part[1:2, :] + gain_term)
        start("branch")
        run("A8")
        for load_of in loads:
            load_of.wait()
        context_grad[...] = sum(
            against_rows(branch_low[:, i * block : (i + 1) * block], bank[at_o + i])
            for i in range(width // block)
        ).astype(BF16)
        q_total = jnp.zeros((1, head_width), F32)
        k_total = jnp.zeros((1, head_width), F32)
        for kv in range(sz.kv_heads):
            kv_at = slice(kv * head_width, (kv + 1) * head_width)
            keys, values = k_low[:, kv_at], v_low[:, kv_at]
            keys_grad = values_grad = 0.0
            for member in range(group):
                head = kv * group + member
                at = slice(head * head_width, (head + 1) * head_width)
                head_grad = context_grad[:, at]
                prob = probs_of(head)[...]
                prob_grad = against_rows(head_grad, values)
                values_grad += across_rows(prob.astype(BF16), head_grad)
                inner = jnp.sum(prob * prob_grad, axis=-1, keepdims=True)
                score_grad = (prob * (prob_grad - inner)).astype(BF16)
                queries_grad = rows_dot(score_grad, keys) * sz.scale
                keys_grad += across_rows(score_grad, q_low[:, at])
                head_low, head_total = turned_back(queries_grad, q_lin[:, at], query_gain)
                lows[0][:, at] = head_low.astype(F32)
                q_total += head_total
            head_low, head_total = turned_back(keys_grad * sz.scale, k_lin[:, kv_at], key_gain)
            k_total += head_total
            lows[1][:, kv_at] = head_low.astype(F32)
            at = k_cols + kv * head_width
            lows[1][:, at : at + head_width] = values_grad.astype(BF16).astype(F32)
        start(("low", 0), ("low", 1))
        run("A9")
        half_rows = pl.ds(pl.multiple_of(grad_base, 8), sz.grad_rows)
        arrived("ctx", "branch")
        for i in range(width // block):
            at = slice(i * block, (i + 1) * block)
            attn_grads[half_rows, at] = across_rows(
                context[:, own_half(q_cols // 2)], branch[:, at].astype(BF16)
            ) + across_rows(ctx_recv[...].astype(BF16), branch_recv[:, at].astype(BF16))
        arrived("attn", ("low", 0), ("low", 1))
        for k in range(2):
            for i in range(width // block):
                at = slice(i * block, (i + 1) * block)
                first = (k + 1) * width + i * block
                attn_grads[half_rows, first : first + block] = across_rows(
                    attn_low[:, own_half(width // 2)], lows[k][:, at].astype(BF16)
                ) + across_rows(attn_recv[...].astype(BF16), low_recvs[k][:, at].astype(BF16))
        for s in range(sz.streams):
            start(("su", s, 1), ("sd", s, 1))
        sent(("part", 1, 0), ("part", 1, 1))
        part[1] = sum(
            against_rows(
                lows[i // q_blocks][:, i % q_blocks * block : (i % q_blocks + 1) * block].astype(BF16),
                bank[i],
            )
            for i in range(at_o)
        )
        value = tokens[...].astype(F32)
        unit = value * norm_factor(value)
        gain_part[0:1, :] = jnp.sum(part[1] * unit, axis=0, keepdims=True)
        gain_part[2:, :] = jnp.zeros((6, width), F32)
        gain_part[2:3, :head_width] = q_total
        gain_part[2:3, head_width : 2 * head_width] = k_total
        start("gain_parts")
        run("A10")
        sent("ctx", "attn", "branch", ("low", 0), ("low", 1))

    pl.run_scoped(
        first_phase,
        pltpu.VMEM((max(at_o + width // block, 2 * unit_blocks), width, block), BF16),
        pltpu.VMEM(w_down.shape, BF16),
        pltpu.VMEM((rows, q_cols), BF16),
        pltpu.VMEM((rows, k_cols), BF16),
        pltpu.VMEM((rows, k_cols), BF16),
        pltpu.VMEM((rows, q_cols), BF16),
        pltpu.VMEM((rows, width), BF16),
        pltpu.VMEM((rows, units), BF16),
        pltpu.VMEM((rows, q_cols), BF16),
        pltpu.VMEM((rows, width), BF16),
        pltpu.VMEM((rows, width), BF16),
    )

    def second_phase(
        wg, wu, wd, staged, ffn_low, ffn_turned, cot_low
    ):
        scoped["staged"] = staged
        weight_loads = [
            pltpu.make_async_copy(src, dst, local_sems.at[i])
            for i, (src, dst) in enumerate(
                (
                    (w_gate.at[:, own_half(half_units)], wg),
                    (w_up.at[:, own_half(half_units)], wu),
                    (w_down.at[pl.ds(pl.multiple_of(core * half_units, 8), half_units)], wd),
                )
            )
        ]
        for load in weight_loads:
            load.start()

        for a in (COT, FFN):
            sent(("up", a, 1), ("down", a, 1), ("core", a, 0))
        arrived(("core", COT, 0), ("core", FFN, 0))
        for copy in stage_copies(0, True):
            copy.start()
        for load in weight_loads:
            load.wait()
        chunks = 3
        size = half_units // chunks
        def step(i, _):
            slot, j = i // chunks, i % chunks

            @pl.when(j == 0)
            def _():
                for copy in stage_copies(slot, False):
                    copy.wait()
                for lane in range(2):
                    here = pl.ds(lane * rows, rows)
                    low_block = staged[FFN, lane].astype(BF16)
                    ffn_low[here] = low_block
                    ffn_turned[:, lane * rows : (lane + 1) * rows] = low_block.T
                    cot_low[here] = staged[COT, lane].astype(BF16)

            def events(part_of_step):
                for when in PLAN:
                    if isinstance(when, tuple) and when[0] < chunks * slots and when[1] == part_of_step:

                        @pl.when(i == when[0])
                        def _():
                            run(when)

            events(0)
            at_units = pl.ds(pl.multiple_of(j * size, 128), size)
            hidden, gate_grad, up_grad = ffn_middle(
                ffn_low[...], cot_low[...], wg[:, at_units], wu[:, at_units], wd[at_units]
            )
            events(1)
            down = across_rows(hidden, cot_low[...])
            gate = rows_dot(ffn_turned[...], gate_grad)
            up = rows_dot(ffn_turned[...], up_grad)

            grad_units = core * half_units + j * size
            grad_cols = pl.ds(pl.multiple_of(grad_units, 128), size)

            @pl.when(slot == 0)
            def _():
                gate_grads[:, grad_cols] = gate
                up_grads[:, grad_cols] = up
                down_grads[grad_cols] = down

            @pl.when(slot > 0)
            def _():
                gate_grads[:, grad_cols] += gate
                up_grads[:, grad_cols] += up
                down_grads[grad_cols] += down

            events(2)
            return 0

        lax.fori_loop(0, chunks * slots, step, 0)
        for k in range(3):
            start(("out", k))
        run((chunks * slots, 0))
        for k in range(3):
            arrived(("out", k))

    pl.run_scoped(
        second_phase,
        pltpu.VMEM((width, half_units), BF16),
        pltpu.VMEM((width, half_units), BF16),
        pltpu.VMEM((half_units, width), BF16),
        pltpu.VMEM((2, 2, rows, width), F32),
        pltpu.VMEM((2 * rows, width), BF16),
        pltpu.VMEM((width, 2 * rows), BF16),
        pltpu.VMEM((2 * rows, width), BF16),
    )
    for s in range(sz.streams):
        for h in range(half + 1):
            arrived(("cu", s, h))
            if h:
                arrived(("cd", s, h))
    for name in book:
        if name not in waited:
            made(name).wait_send()


def results_kernel(*refs):
    count = 10
    held, places, sems = refs[:count], refs[count:-1], refs[-1]
    moves = list(zip(held[:-1], places))
    first = 0
    for dst in places[count - 1 :]:
        moves.append((held[-1].at[:, pl.ds(first, dst.shape[1])], dst))
        first += dst.shape[1]
    copies = [
        pltpu.make_async_copy(src, dst, sems.at[k]) for k, (src, dst) in enumerate(moves)
    ]
    for copy in copies:
        copy.start()
    for copy in copies:
        copy.wait()


def over_groups(sz, dp_size, values):
    step = sz.group
    while step < dp_size:
        values = values + lax.ppermute(values, "dp", [(d, d ^ step) for d in range(dp_size)])
        step *= 2
    return values


def per_device(
    dp_size,
    tokens,
    segments,
    positions,
    attn_gain,
    w_query,
    key_weight,
    value_weight,
    query_gain,
    key_gain,
    w_out,
    ffn_gain,
    w_gate,
    w_up,
    w_down,
    cotangent,
):
    sz = Sizes(dp_size, tokens.shape, w_query.shape, key_weight.shape, query_gain.shape, w_gate.shape)
    rows, width, head_width, half = sz.rows, sz.width, sz.head_width, sz.half
    q_cols, k_cols = sz.q_cols, sz.k_cols
    lanes = np.arange(head_width) % (head_width // 2)
    inverse = (THETA ** (-2.0 * lanes / head_width)).astype(np.float32)[None]
    vmem = pl.BlockSpec(memory_space=pltpu.VMEM)
    anywhere = pl.BlockSpec(memory_space=pl.ANY)
    slots = 2 * half
    transfers = 120
    mixed, tokens_grad, *others = pl.pallas_call(
        functools.partial(layer_kernel, sz),
        out_shape=[
            pltpu.VMEM((rows, width), BF16),
            pltpu.VMEM((rows, width), BF16),
            pltpu.VMEM((1, width), F32),
            pltpu.VMEM((1, width), F32),
            pltpu.VMEM((1, head_width), F32),
            pltpu.VMEM((1, head_width), F32),
            pltpu.VMEM((width, sz.grad_cols), F32),
            pltpu.VMEM(w_gate.shape, F32),
            pltpu.VMEM(w_up.shape, F32),
            pltpu.VMEM(w_down.shape, F32),
            shaped(2, slots, rows, width),
            shaped(2, slots, rows, width),
        ],
        in_specs=[anywhere] * 16,
        out_specs=[vmem] * 10 + [anywhere] * 2,
        scratch_shapes=[
            pltpu.VMEM((rows, width), BF16),
            pltpu.VMEM((rows, width), BF16),
            pltpu.VMEM((1, rows), jnp.int32),
            pltpu.VMEM((1, rows), jnp.int32),
            pltpu.VMEM((1, head_width), F32),
            pltpu.VMEM((1, width), F32),
            pltpu.VMEM((1, head_width), F32),
            pltpu.VMEM((1, head_width), F32),
            pltpu.VMEM((1, width), F32),
            pltpu.VMEM((2, rows, width), F32),
            pltpu.VMEM((2, rows, width), F32),
            pltpu.VMEM((rows, width), F32),
            pltpu.VMEM((half, sz.piece, sz.grad_cols), F32),
            pltpu.VMEM((half, sz.piece, sz.grad_cols), F32),
            pltpu.VMEM((8, width), F32),
            pltpu.VMEM((8, width), F32),
            pltpu.VMEM((8, width), F32),
            pltpu.VMEM((8, width), F32),
            pltpu.VMEM((sz.chips, 8, width), F32),
            pltpu.SemaphoreType.DMA((transfers,)),
            pltpu.SemaphoreType.DMA((transfers,)),
            pltpu.SemaphoreType.DMA((32,)),
        ],
        compiler_params=pltpu.CompilerParams(
            collective_id=0, has_side_effects=True, vmem_limit_bytes=VMEM_BYTES
        ),
    )(
        tokens, cotangent, segments, positions, jnp.asarray(inverse), attn_gain[None], query_gain[None], key_gain[None],
        ffn_gain[None], w_query, key_weight, value_weight, w_out, w_gate, w_up, w_down,
    )
    sums = [over_groups(sz, dp_size, values) for values in others[:-2]]
    attn_grads = sums.pop(4)
    results = [mixed, tokens_grad, *sums, attn_grads]
    places = [shaped(*v.shape, kind=v.dtype) for v in results[:-1]]
    places += [shaped(*v.shape) for v in (w_out, w_query, key_weight, value_weight)]
    (
        mixed, tokens_grad, attn_gain_grad, ffn_gain_grad, query_gain_grad, key_gain_grad,
        w_gate_grad, w_up_grad, w_down_grad, w_out_grad, w_query_grad, w_key_grad, w_value_grad,
    ) = pl.pallas_call(
        results_kernel,
        out_shape=places,
        in_specs=[anywhere] * len(results),
        out_specs=[anywhere] * len(places),
        scratch_shapes=[pltpu.SemaphoreType.DMA((len(places),))],
        compiler_params=pltpu.CompilerParams(vmem_limit_bytes=RESULTS_VMEM_BYTES),
    )(*[pltpu.with_memory_space_constraint(values, pltpu.VMEM) for values in results])
    return (
        mixed,
        tokens_grad,
        attn_gain_grad[0],
        w_query_grad,
        w_key_grad,
        w_value_grad,
        query_gain_grad[0],
        key_gain_grad[0],
        w_out_grad,
        ffn_gain_grad[0],
        w_gate_grad,
        w_up_grad,
        w_down_grad,
    )


def solution(mesh):
    def layer(*arrays):
        return per_device(mesh.shape["dp"], *arrays)

    return jax.shard_map(
        layer,
        mesh=mesh,
        in_specs=(
            P("dp", None),
            P("dp", None),
            P("dp", None),
            P(),
            P(None, "tensor"),
            P(None, "tensor"),
            P(None, "tensor"),
            P(),
            P(),
            P("tensor", None),
            P(),
            P(None, "tensor"),
            P(None, "tensor"),
            P("tensor", None),
            P("dp", None),
        ),
        out_specs=(
            P("dp", None),
            P("dp", None),
            P(),
            P(None, "tensor"),
            P(None, "tensor"),
            P(None, "tensor"),
            P(),
            P(),
            P("tensor", None),
            P(),
            P(None, "tensor"),
            P(None, "tensor"),
            P("tensor", None),
        ),
        check_vma=False,
    )
```

```python
import functools
import math

import jax
import jax.numpy as jnp
import numpy as np
from jax import lax
from jax.experimental import pallas as pl
from jax.experimental.pallas import tpu as pltpu
from jax.sharding import PartitionSpec as P

EPS = 1e-06
THETA = 1000000.0
F32 = jnp.float32
BF16 = jnp.bfloat16
MESH = pl.DeviceIdType.MESH
VMEM_BYTES = 32 * 2**20
RESULTS_VMEM_BYTES = 2**20
GROUP = 16
COT, FFN = 0, 1
SHARES = ((2, 2, 2, 3), (4, 4, 4, 4))


PLAN = {
    "A2": [
        ("ring_half", 0),
        ("ring_half", 1),
    ],
    "A5": [
        ("start", "x", COT, 1),
    ],
    "A6": [
        ("ring", COT, 2),
    ],
    "A7": [
        ("start", "x", COT, 2),
        ("start", "x", COT, 3),
        ("start", "x", COT, 4),
        ("ring", FFN, 1),
    ],
    "A10": [
        ("x_done", COT, 1),
        ("start", "x", FFN, 1),
        ("x_done", COT, 2),
        ("start", "x", FFN, 2),
    ],
    (0, 0): [
        ("ring", COT, 3),
    ],
    (0, 1): [
        ("x_done", COT, 3),
        ("start", "x", COT, 5),
    ],
    (2, 0): [
        ("x_done", COT, 4),
        ("start", "x", COT, 6),
    ],
    (2, 1): [
        ("ring", FFN, 2),
        ("gain_sum",),
    ],
    (2, 2): [
        ("sum", 0, 1),
        ("gain", 0),
        ("sum", 1, 1),
        ("x_done", FFN, 1),
        ("start", "x", FFN, 3),
        ("stage", 1),
    ],
    (3, 0): [
        ("ring", COT, 4),
    ],
    (4, 1): [
        ("x_done", FFN, 2),
        ("start", "x", FFN, 4),
    ],
    (5, 2): [
        ("stage", 2),
    ],
    (6, 0): [
        ("ring", FFN, 3),
        ("x_done", COT, 5),
        ("start", "x", FFN, 5),
    ],
    (6, 1): [
        ("x_done", COT, 6),
        ("start", "x", FFN, 6),
    ],
    (7, 0): [
        ("sum", 0, 2),
        ("gain", 1),
    ],
    (8, 2): [
        ("sum", 1, 2),
        ("x_done", FFN, 3),
        ("start", "x", COT, 7),
        ("stage", 3),
    ],
    (9, 0): [
        ("ring", FFN, 4),
    ],
    (10, 1): [
        ("x_done", FFN, 4),
        ("start", "x", FFN, 7),
    ],
    (11, 0): [
        ("sum", 0, 3),
        ("gain", 2),
    ],
    (11, 1): [
        ("stage", 4),
    ],
    (13, 0): [
        ("sum", 1, 3),
        ("x_done", FFN, 5),
        ("start", "part", 2),
    ],
    (14, 1): [
        ("stage", 5),
    ],
    (15, 0): [
        ("sum", 0, 4),
        ("gain", 3),
    ],
    (15, 1): [
        ("x_done", FFN, 6),
        ("start", "part", 3),
    ],
    (17, 0): [
        ("stage", 6),
    ],
    (17, 1): [
        ("sum", 1, 4),
    ],
    (18, 0): [
        ("x_done", COT, 7),
    ],
    (19, 1): [
        ("gather", 0, 1),
    ],
    (20, 0): [
        ("gain", 4),
    ],
    (20, 2): [
        ("x_done", FFN, 7),
        ("gather", 1, 1),
        ("stage", 7),
    ],
    (22, 0): [
        ("gather", 0, 2),
    ],
    (24, 0): [
        ("gather", 1, 2),
        ("tokens",),
        ("gather", 0, 3),
        ("gather", 1, 3),
        ("gather", 0, 4),
        ("mixed",),
        ("gather", 1, 4),
    ],
}


def norm_factor(values):
    return lax.rsqrt(jnp.mean(values * values, axis=-1, keepdims=True) + EPS)


def norm_grad(grad_out, unit_rows, factor, scale_gain):
    scaled = grad_out * scale_gain
    return factor * (scaled - unit_rows * jnp.mean(scaled * unit_rows, axis=-1, keepdims=True))


def rows_dot(leading, trailing):
    return jnp.dot(leading, trailing, preferred_element_type=F32)


def across_rows(leading, trailing):
    return lax.dot_general(
        leading, trailing, (((0,), (0,)), ((), ())), preferred_element_type=F32
    )


def against_rows(leading, trailing):
    return lax.dot_general(
        leading, trailing, (((1,), (1,)), ((), ())), preferred_element_type=F32
    )


def ffn_middle(low_in, cot, wg, wu, wd):
    gate = rows_dot(low_in, wg)
    up = rows_dot(low_in, wu)
    sig = jax.nn.sigmoid(gate)
    silu = gate * sig
    hidden = (silu * up).astype(BF16)
    hidden_grad = against_rows(cot, wd)
    up_grad = (hidden_grad * silu).astype(BF16)
    gate_grad = (hidden_grad * up * sig * (1.0 + gate * (1.0 - sig))).astype(BF16)
    return hidden, gate_grad, up_grad


def shaped(*shape, kind=F32):
    return jax.ShapeDtypeStruct(shape, kind)


class Sizes:
    def __init__(self, dp_size, tokens, w_query, key_weight, query_gain, w_gate):
        self.rows, self.width = tokens
        self.head_width = query_gain[0]
        self.q_cols, self.k_cols = w_query[1], key_weight[1]
        self.heads, self.kv_heads = self.q_cols // self.head_width, self.k_cols // self.head_width
        self.units = w_gate[1]
        self.all_cols = self.q_cols + 2 * self.k_cols
        self.scale = 1.0 / math.sqrt(self.head_width)
        self.group = math.gcd(GROUP, dp_size)
        self.chips = self.group // 2
        self.half = self.chips // 2
        self.share = tuple(tuple(self.width * part // 8 for part in parts) for parts in SHARES)
        self.grad_rows = self.width // 2
        self.grad_cols = self.width + self.all_cols
        self.piece = self.grad_rows // self.chips
        self.streams = 2


def layer_kernel(
    sz,
    tokens_in, cot_in, segments_in, positions_in, inverse_in, attn_gain_in, query_gain_in, key_gain_in,
    ffn_gain_in,
    w_query, key_weight, value_weight, w_out, w_gate, w_up, w_down,
    mixed, tokens_grad, attn_gain_grad, ffn_gain_grad, query_gain_grad, key_gain_grad,
    attn_grads, gate_grads, up_grads, down_grads,
    mine, theirs,
    tokens, cot, segments, positions, inverse, attn_gain, query_gain, key_gain, ffn_gain,
    part, part_theirs, middle_grad, sum_up, sum_down, gain_part, gain_theirs,
    gain_send, gain_recv, gain_slots,
    send_sems, recv_sems, local_sems,
):
    rows, width, head_width = sz.rows, sz.width, sz.head_width
    q_cols, k_cols, units = sz.q_cols, sz.k_cols, sz.units
    n, half, piece = sz.chips, sz.half, sz.piece
    half_units = units // 2
    mid = rows // 2

    device = lax.axis_index("dp")
    base = device // sz.group * sz.group
    core = device % 2
    chip = device % sz.group // 2
    line = chip % 2
    place = chip // 2 + line * (2 * half - 1 - 2 * (chip // 2))
    side = lax.axis_index("tensor")

    def device_at(position):
        position = position % n
        second = position // half
        return base + (2 * (position + second * (2 * half - 1 - 2 * position)) + second) * 2 + core

    forward = {"dp": device_at(place + 1)}
    backward = {"dp": device_at(place + n - 1)}
    sibling = {"dp": base + chip * 2 + 1 - core}
    across = {"tensor": 1 - side}

    barrier = pltpu.get_barrier_semaphore()
    for neighbour in (forward, backward, sibling, across):
        pl.semaphore_signal(barrier, inc=1, device_id=neighbour, device_id_type=MESH)
    small_loads = [
        pltpu.make_async_copy(src, dst, local_sems.at[16 + k])
        for k, (src, dst) in enumerate(
            (
                (cot_in, cot),
                (tokens_in, tokens),
                (attn_gain_in, attn_gain),
                (segments_in, segments),
                (positions_in, positions),
                (inverse_in, inverse),
                (query_gain_in, query_gain),
                (key_gain_in, key_gain),
                (ffn_gain_in, ffn_gain),
            )
        )
    ]
    for load in small_loads:
        load.start()

    book = {}
    waited = set()

    def remote(name, src, dst, target):
        book[name] = (len(book), src, dst, target)

    def made(name):
        index, src, dst, target = book[name]
        return pltpu.make_async_remote_copy(
            src_ref=src, dst_ref=dst, send_sem=send_sems.at[index], recv_sem=recv_sems.at[index],
            device_id=target, device_id_type=MESH,
        )

    def sent(*names):
        for name in names:
            made(name).wait_send()
            waited.add(name)

    def start(*names):
        for name in names:
            made(name).start()

    def arrived(*names):
        for name in names:
            made(name).wait_recv()

    def cols(first, count):
        return pl.ds(pl.multiple_of(first, 128), count)

    def piece_rows(index, first=0, count=piece, base_row=0):
        return pl.ds(pl.multiple_of(base_row + index % n * piece + first, 8), count)

    grad_base = core * sz.grad_rows
    slots = 2 * half
    up_slot = lambda h: 2 * h - 1
    down_slot = lambda h: 2 * h
    last = slots - 1
    up_place = lambda row, first, count: up_grads.at[pl.ds(row * rows, rows), pl.ds(first, count)]
    down_place = lambda row: down_grads.at[pl.ds(row * rows, rows)]
    half_width = width // 2
    gate_place = lambda row: gate_grads.at[pl.ds(row * rows, rows), pl.ds(units - width, width)]
    own = (gate_place(0), gate_place(1))
    in_halves = lambda a, h: a == COT and h <= 2

    def ring_names(a, h):
        count = 2 if in_halves(a, h) else 1
        return [(way, a, h, k) for k in range(count) for way in ("up", "down")]

    for a in (COT, FFN):
        for h in range(1, half + 1):
            share = sz.share[a][h - 1]
            window = cols(side * share, width - share)
            shared = cols(side * (width - share), share)
            up = own[a] if h == 1 else mine.at[a, up_slot(h - 1)]
            down = own[a] if h == 1 else mine.at[a, down_slot(h - 1)]
            first, second = pl.ds(0, mid), pl.ds(mid, mid)
            if h < half:
                for k, part_rows in enumerate((first, second) if in_halves(a, h) else (pl.ds(0, rows),)):
                    to_up = mine.at[a, up_slot(h), part_rows, window]
                    to_down = mine.at[a, down_slot(h), part_rows, window]
                    remote(("up", a, h, k), up.at[part_rows, window], to_up, forward)
                    remote(("down", a, h, k), down.at[part_rows, window], to_down, backward)
                of_distance = (up_slot(h), down_slot(h))
            else:
                remote(("up", a, h, 0), up.at[first, window], mine.at[a, last, first, window], forward)
                remote(
                    ("down", a, h, 0), down.at[second, window], mine.at[a, last, second, window], backward
                )
                of_distance = (last,)
            for s in of_distance:
                remote(("x", a, s), mine.at[a, s, :, shared], mine.at[a, s, :, shared], across)
        for s in range(slots):
            remote(("core", a, s), own[a] if s == 0 else mine.at[a, s], theirs.at[a, s], sibling)
    halves = (slice(0, mid), slice(mid, rows))
    for k in range(2):
        for index, at_rows in enumerate(halves):
            at_rows = pl.ds(at_rows.start, mid)
            remote(
                ("part", k, index), part.at[k, at_rows], part_theirs.at[k, at_rows], across
            )
        remote(("part", 2 + k), part.at[1 - k], part_theirs.at[k], across)
    stream_cols = sz.grad_cols // sz.streams
    small = piece // 2
    for s in range(sz.streams):
        c = pl.ds(s * stream_cols, stream_cols)
        for h in range(1, half + 1):
            size, skip = (small, small) if h == 1 else (piece, 0)
            src = attn_grads.at[piece_rows(place + half, 0, small, grad_base), c]
            remote(
                ("su", s, h), src if h == 1 else sum_up.at[h - 2, :, c],
                sum_up.at[h - 1, pl.ds(0, size), c], forward,
            )
            src = attn_grads.at[piece_rows(place + half, small, small, grad_base), c]
            remote(
                ("sd", s, h), src if h == 1 else sum_down.at[h - 2, :, c],
                sum_down.at[h - 1, pl.ds(skip, size), c], backward,
            )
        for h in range(1, half + 1):
            size, skip = (small, small) if h == half else (piece, 0)
            going_up = attn_grads.at[piece_rows(place + n - h + 1, 0, size, grad_base), c]
            going_down = attn_grads.at[piece_rows(place + h - 1, skip, size, grad_base), c]
            remote(("gu", s, h), going_up, going_up, forward)
            remote(("gd", s, h), going_down, going_down, backward)
            got_up = attn_grads.at[piece_rows(place + n - h, 0, size, grad_base), c]
            got_down = attn_grads.at[piece_rows(place + h, skip, size, grad_base), c]
            remote(("cu", s, h), got_up, got_up, sibling)
            remote(("cd", s, h), got_down, got_down, sibling)
        own_piece = attn_grads.at[piece_rows(place, 0, piece, grad_base), c]
        remote(("cu", s, 0), own_piece, own_piece, sibling)
    remote("gain_parts", gain_part, gain_theirs, across)
    remote("gains", gain_send, gain_recv, sibling)
    for h in range(1, half + 1):
        slot = gain_slots.at[(place + n - h + 1) % n]
        remote(("vu", h), slot, slot, forward)
        if h < half:
            slot = gain_slots.at[(place + h - 1) % n]
            remote(("vd", h), slot, slot, backward)

    def ring_step(a, h):
        arrived(*ring_names(a, h))
        if h < half:
            start(*ring_names(a, h + 1))

    def ring_half(k):
        arrived(("up", COT, 1, k), ("down", COT, 1, k))
        start(("up", COT, 2, k), ("down", COT, 2, k))

    def x_start(a, s):
        start(("x", a, s))

    def x_done(a, s):
        arrived(("x", a, s))
        start(("core", a, s))


    def stream(s):
        return pl.ds(s * stream_cols, stream_cols)

    def sum_step(s, h):
        arrived(("su", s, h), ("sd", s, h))
        c = stream(s)
        up_rows = piece_rows(place + half - h, 0, piece, grad_base)
        down_rows = piece_rows(place + n - half + h, 0, piece, grad_base)
        if h == 1:
            sent(("su", s, 1), ("sd", s, 1))
            up, down = attn_grads[up_rows, c], attn_grads[down_rows, c]
            sum_up[0, :small, c] += up[:small]
            sum_up[0, small:, c] = up[small:]
            sum_down[0, :small, c] = down[:small]
            sum_down[0, small:, c] += down[small:]
        elif h < half:
            sum_up[h - 1, :, c] += attn_grads[up_rows, c]
            sum_down[h - 1, :, c] += attn_grads[down_rows, c]
        if h < half:
            start(("su", s, h + 1), ("sd", s, h + 1))
        else:
            own_rows = piece_rows(place, 0, piece, grad_base)
            attn_grads[own_rows, c] += sum_up[h - 1, :, c] + sum_down[h - 1, :, c]
            start(("gu", s, 1), ("gd", s, 1), ("cu", s, 0))

    def gather_step(s, h):
        arrived(("gu", s, h), ("gd", s, h))
        if h < half:
            start(("gu", s, h + 1), ("gd", s, h + 1))
        start(("cu", s, h), ("cd", s, h))

    def finish_tokens():
        arrived(("part", 2))
        grad = part[1] + part_theirs[0]
        value = tokens[...].astype(F32)
        factor = norm_factor(value)
        unit = value * factor
        tokens_grad[...] = (
            middle_grad[...] + norm_grad(grad, unit, factor, attn_gain[...])
        ).astype(BF16)

    def finish_mixed():
        arrived(("part", 3))
        mixed[...] = (part[0] + part_theirs[1]).astype(BF16)

    def gain_sum():
        arrived("gain_parts")
        gain_send[...] = gain_part[...] + gain_theirs[...]
        start("gains")

    def gain_first():
        arrived("gains")
        gain_slots[place] = gain_send[...] + gain_recv[...]
        start(("vu", 1), ("vd", 1))

    def gain_step(h):
        arrived(("vu", h))
        if h < half:
            arrived(("vd", h))
            start(("vu", h + 1))
            if h + 1 < half:
                start(("vd", h + 1))
        else:
            total = gain_slots[0]
            for chip_at in range(1, n):
                total = total + gain_slots[chip_at]
            attn_gain_grad[...] = total[0:1, :]
            ffn_gain_grad[...] = total[1:2, :]
            query_gain_grad[...] = total[2:3, :head_width]
            key_gain_grad[...] = total[2:3, head_width : 2 * head_width]

    def stage(slot):
        arrived(("core", COT, slot), ("core", FFN, slot))
        for copy in stage_copies(slot, False):
            copy.start()

    scoped = {}

    def stage_copies(slot, first):
        staged = scoped["staged"]
        copies = []
        for a in (COT, FFN):
            src = own[a] if first else mine.at[a, slot]
            copies.append(pltpu.make_async_copy(src, staged.at[a, 0], local_sems.at[9 + 2 * a]))
            copies.append(
                pltpu.make_async_copy(theirs.at[a, slot], staged.at[a, 1], local_sems.at[10 + 2 * a])
            )
        return copies

    def gain_event(h):
        if h == 0:
            gain_first()
        else:
            gain_step(h)

    actions = {
        "ring": ring_step,
        "ring_half": ring_half,
        "start": lambda *name: start(name),
        "x_done": x_done,
        "sum": sum_step,
        "gather": gather_step,
        "stage": stage,
        "gain_sum": gain_sum,
        "tokens": finish_tokens,
        "gain": gain_event,
        "mixed": finish_mixed,
    }

    def run(when):
        for event in PLAN.get(when, ()):
            actions[event[0]](*event[1:])

    group = q_cols // k_cols
    other_half = lambda count: cols((1 - core) * count, count)
    own_half = lambda count: cols(core * count, count)

    block = k_cols
    q_blocks, unit_blocks = q_cols // block, units // block
    at_k, at_v, at_o = q_blocks, q_blocks + 1, q_blocks + 2

    half_down = down_grads.at[pl.ds(pl.multiple_of(core * half_units, 8), half_units)]
    outs = (gate_grads.at[:, own_half(half_units)], up_grads.at[:, own_half(half_units)], half_down)
    for k, out in enumerate(outs):
        remote(("out", k), out, out, sibling)

    q_lin, k_lin = up_place(0, 0, q_cols), up_place(0, q_cols, k_cols)
    ctx_send, ctx_recv = up_place(1, 0, q_cols // 2), up_place(1, q_cols // 2, q_cols // 2)
    cosine, sine = up_place(1, q_cols, head_width), up_place(1, q_cols + head_width, head_width)
    attn_send, attn_recv = up_place(2, 0, half_width), up_place(2, half_width, half_width)
    mask = up_place(3, 0, rows)
    lows, low_recvs = (down_place(0), down_place(1)), (down_place(2), down_place(3))
    branch, branch_recv = down_place(4), down_place(5)
    deep = width // rows
    middle = gate_place(2)

    def probs_of(head):
        return gate_grads.at[pl.ds(head % deep * rows, rows), pl.ds(head // deep * rows, rows)]

    remote("ctx", ctx_send, ctx_recv, sibling)
    remote("attn", attn_send, attn_recv, sibling)
    remote("branch", branch, branch_recv, sibling)
    for k in range(2):
        remote(("low", k), lows[k], low_recvs[k], sibling)

    def first_phase(
        bank, wd, q_low, k_low, v_low, context, ffn_low, hidden, context_grad, attn_low, branch_low
    ):
        def load(src, dst, index):
            copy = pltpu.make_async_copy(src, dst, local_sems.at[index])
            copy.start()
            return copy

        def block_of(weights, index):
            return weights.at[:, pl.ds(index * block, block)]

        def load_projections():
            order = [(w_query, i) for i in range(q_blocks)] + [(key_weight, 0), (value_weight, 0)]
            return [load(block_of(w, i), bank.at[k], k) for k, (w, i) in enumerate(order)]

        def load_out():
            count = width // block
            return [load(block_of(w_out, i), bank.at[at_o + i], at_o + i) for i in range(count)]

        def load_ffn():
            order = [(w, i) for w in (w_gate, w_up) for i in range(unit_blocks)]
            return [load(block_of(w, i), bank.at[k], k) for k, (w, i) in enumerate(order)]

        loads = load_projections()

        def head_norm(lin, gain):
            return lin * norm_factor(lin) * gain[...]

        def turned(lin, gain, at_rows):
            normed = head_norm(lin, gain)
            swapped = pltpu.roll(normed, head_width // 2, 1)
            return (normed * cosine[at_rows] + swapped * sine[at_rows]).astype(BF16)

        def turned_back(grad, lin, gain):
            back = grad * cosine[...] - pltpu.roll(grad, head_width // 2, 1) * sine[...]
            factor = norm_factor(lin)
            unit = lin * factor
            return (
                norm_grad(back, unit, factor, gain[...]).astype(BF16),
                jnp.sum(back * unit, axis=0, keepdims=True),
            )

        small_loads[0].wait()
        own[COT][...] = cot[...].astype(F32)
        pl.semaphore_wait(barrier, 4)
        start(*ring_names(COT, 1), ("core", COT, 0))

        for small in small_loads[1:]:
            small.wait()
        resid = tokens[...].astype(F32)
        attn_in = (resid * norm_factor(resid) * attn_gain[...]).astype(BF16)
        attn_low[...] = attn_in
        attn_send[...] = attn_low[:, other_half(width // 2)].astype(F32)
        start("attn")

        def down_rows(row):
            return jnp.broadcast_to(row.astype(F32), (head_width, rows)).T

        segment_rows = jnp.concatenate([down_rows(segments[...])] * (rows // head_width), 1)
        same = segment_rows == jnp.broadcast_to(segments[...].astype(F32), (rows, rows))
        row_at = lax.broadcasted_iota(jnp.int32, (rows, rows), 0)
        column_at = lax.broadcasted_iota(jnp.int32, (rows, rows), 1)
        mask[...] = jnp.where(same & (row_at >= column_at), 1.0, 0.0)
        angles = down_rows(positions[...]) * inverse[...]
        lane = lax.broadcasted_iota(jnp.int32, (rows, head_width), 1)
        cosine[...] = jnp.cos(angles)
        sine[...] = jnp.where(lane < head_width // 2, -1.0, 1.0) * jnp.sin(angles)
        for i in range(q_blocks):
            loads[i].wait()
            q_lin[:, i * block : (i + 1) * block] = rows_dot(attn_in, bank[i])
        loads[at_k].wait()
        k_lin[...] = rows_dot(attn_in, bank[at_k])
        loads[at_v].wait()
        v_low[...] = rows_dot(attn_in, bank[at_v]).astype(BF16)
        loads += load_out()
        run("A1")
        for kv in range(sz.kv_heads):
            kv_at = slice(kv * head_width, (kv + 1) * head_width)
            k_low[:, kv_at] = turned(k_lin[:, kv_at], key_gain, slice(0, rows))
        for index, at_rows in enumerate(halves):
            seen = at_rows.stop
            for head in range(sz.heads):
                at = slice(head * head_width, (head + 1) * head_width)
                kv_at = slice(head // group * head_width, (head // group + 1) * head_width)
                queries = turned(q_lin[at_rows, at], query_gain, at_rows)
                q_low[at_rows, at] = queries
                scores = against_rows(queries, k_low[:seen, kv_at]) * sz.scale
                scores = jnp.where(mask[at_rows, :seen] > 0, scores, -1e30)
                raised = jnp.exp(scores - jnp.max(scores, axis=-1, keepdims=True))
                prob = raised / jnp.sum(raised, axis=-1, keepdims=True)
                place_of = probs_of(head)
                place_of[at_rows, :seen] = prob
                if seen < rows:
                    place_of[at_rows, seen:] = jnp.zeros((mid, rows - seen), F32)
                context[at_rows, at] = rows_dot(prob.astype(BF16), v_low[:seen, kv_at]).astype(BF16)
            for i in range(width // block):
                if index == 0:
                    loads[at_o + i].wait()
                at = slice(i * block, (i + 1) * block)
                part[0, at_rows, at] = rows_dot(context[at_rows], bank[at_o + i])
            start(("part", 0, index))
        ctx_send[...] = context[:, other_half(q_cols // 2)].astype(F32)
        start("ctx")
        loads = load_ffn()
        down_load = load(w_down, wd, 15)
        for index, at_rows in enumerate(halves):
            run("A2" if index == 0 else "A3")
            arrived(("part", 0, index))
            value = tokens[at_rows].astype(F32) + (part[0, at_rows] + part_theirs[0, at_rows])
            middle[at_rows] = value
            low_rows = (value * norm_factor(value) * ffn_gain[...]).astype(BF16)
            ffn_low[at_rows] = low_rows
            own[FFN][at_rows] = low_rows.astype(F32)
            if index == 0:
                down_load.wait()
                for load_of in loads:
                    load_of.wait()
            else:
                start(*ring_names(FFN, 1), ("core", FFN, 0))
                run("A4")
            for i in range(unit_blocks):
                at = slice(i * block, (i + 1) * block)
                wg, wu = bank[i], bank[unit_blocks + i]
                low_hidden, gate_grad, up_grad = ffn_middle(low_rows, cot[at_rows], wg, wu, wd[at])
                hidden[at_rows, at] = low_hidden
                term = against_rows(gate_grad, wg) + against_rows(up_grad, wu)
                if i == 0:
                    part[1, at_rows] = term
                else:
                    part[1, at_rows] += term
            start(("part", 1, index))
        loads = load_projections() + load_out()
        run("A5")
        sent(("part", 0, 0), ("part", 0, 1))
        part[0] = rows_dot(hidden[...], wd[...]) + 0.5 * middle[...]

        for index, at_rows in enumerate(halves):
            run("A6" if index == 0 else "A7")
            arrived(("part", 1, index))
            grad = part[1, at_rows] + part_theirs[1, at_rows]
            value = middle[at_rows]
            factor = norm_factor(value)
            unit = value * factor
            total = cot[at_rows].astype(F32) + norm_grad(grad, unit, factor, ffn_gain[...])
            middle_grad[at_rows] = total
            branch_low[at_rows] = total.astype(BF16)
            branch[at_rows] = total.astype(BF16).astype(F32)
            gain_term = jnp.sum(grad * unit, axis=0, keepdims=True)
            gain_part[1:2, :] = gain_term if index == 0 else 0.5 * (gain_part[1:2, :] + gain_term)
        start("branch")
        run("A8")
        for load_of in loads:
            load_of.wait()
        context_grad[...] = sum(
            against_rows(branch_low[:, i * block : (i + 1) * block], bank[at_o + i])
            for i in range(width // block)
        ).astype(BF16)
        q_total = jnp.zeros((1, head_width), F32)
        k_total = jnp.zeros((1, head_width), F32)
        for kv in range(sz.kv_heads):
            kv_at = slice(kv * head_width, (kv + 1) * head_width)
            keys, values = k_low[:, kv_at], v_low[:, kv_at]
            keys_grad = values_grad = 0.0
            for member in range(group):
                head = kv * group + member
                at = slice(head * head_width, (head + 1) * head_width)
                head_grad = context_grad[:, at]
                prob = probs_of(head)[...]
                prob_grad = against_rows(head_grad, values)
                values_grad += across_rows(prob.astype(BF16), head_grad)
                inner = jnp.sum(prob * prob_grad, axis=-1, keepdims=True)
                score_grad = (prob * (prob_grad - inner)).astype(BF16)
                queries_grad = rows_dot(score_grad, keys) * sz.scale
                keys_grad += across_rows(score_grad, q_low[:, at])
                head_low, head_total = turned_back(queries_grad, q_lin[:, at], query_gain)
                lows[0][:, at] = head_low.astype(F32)
                q_total += head_total
            head_low, head_total = turned_back(keys_grad * sz.scale, k_lin[:, kv_at], key_gain)
            k_total += head_total
            lows[1][:, kv_at] = head_low.astype(F32)
            at = k_cols + kv * head_width
            lows[1][:, at : at + head_width] = values_grad.astype(BF16).astype(F32)
        start(("low", 0), ("low", 1))
        run("A9")
        half_rows = pl.ds(pl.multiple_of(grad_base, 8), sz.grad_rows)
        arrived("ctx", "branch")
        for i in range(width // block):
            at = slice(i * block, (i + 1) * block)
            attn_grads[half_rows, at] = across_rows(
                context[:, own_half(q_cols // 2)], branch[:, at].astype(BF16)
            ) + across_rows(ctx_recv[...].astype(BF16), branch_recv[:, at].astype(BF16))
        arrived("attn", ("low", 0), ("low", 1))
        for k in range(2):
            for i in range(width // block):
                at = slice(i * block, (i + 1) * block)
                first = (k + 1) * width + i * block
                attn_grads[half_rows, first : first + block] = across_rows(
                    attn_low[:, own_half(width // 2)], lows[k][:, at].astype(BF16)
                ) + across_rows(attn_recv[...].astype(BF16), low_recvs[k][:, at].astype(BF16))
        for s in range(sz.streams):
            start(("su", s, 1), ("sd", s, 1))
        sent(("part", 1, 0), ("part", 1, 1))
        part[1] = sum(
            against_rows(
                lows[i // q_blocks][:, i % q_blocks * block : (i % q_blocks + 1) * block].astype(BF16),
                bank[i],
            )
            for i in range(at_o)
        )
        value = tokens[...].astype(F32)
        unit = value * norm_factor(value)
        gain_part[0:1, :] = jnp.sum(part[1] * unit, axis=0, keepdims=True)
        gain_part[2:, :] = jnp.zeros((6, width), F32)
        gain_part[2:3, :head_width] = q_total
        gain_part[2:3, head_width : 2 * head_width] = k_total
        start("gain_parts")
        run("A10")
        sent("ctx", "attn", "branch", ("low", 0), ("low", 1))

    pl.run_scoped(
        first_phase,
        pltpu.VMEM((max(at_o + width // block, 2 * unit_blocks), width, block), BF16),
        pltpu.VMEM(w_down.shape, BF16),
        pltpu.VMEM((rows, q_cols), BF16),
        pltpu.VMEM((rows, k_cols), BF16),
        pltpu.VMEM((rows, k_cols), BF16),
        pltpu.VMEM((rows, q_cols), BF16),
        pltpu.VMEM((rows, width), BF16),
        pltpu.VMEM((rows, units), BF16),
        pltpu.VMEM((rows, q_cols), BF16),
        pltpu.VMEM((rows, width), BF16),
        pltpu.VMEM((rows, width), BF16),
    )

    def second_phase(
        wg, wu, wd, staged, ffn_low, ffn_turned, cot_low
    ):
        scoped["staged"] = staged
        weight_loads = [
            pltpu.make_async_copy(src, dst, local_sems.at[i])
            for i, (src, dst) in enumerate(
                (
                    (w_gate.at[:, own_half(half_units)], wg),
                    (w_up.at[:, own_half(half_units)], wu),
                    (w_down.at[pl.ds(pl.multiple_of(core * half_units, 8), half_units)], wd),
                )
            )
        ]
        for load in weight_loads:
            load.start()

        for a in (COT, FFN):
            sent(*ring_names(a, 1), ("core", a, 0))
        arrived(("core", COT, 0), ("core", FFN, 0))
        for copy in stage_copies(0, True):
            copy.start()
        for load in weight_loads:
            load.wait()
        chunks = 3
        size = half_units // chunks
        def step(i, _):
            slot, j = i // chunks, i % chunks

            @pl.when(j == 0)
            def _():
                for copy in stage_copies(slot, False):
                    copy.wait()
                for lane in range(2):
                    here = pl.ds(lane * rows, rows)
                    low_block = staged[FFN, lane].astype(BF16)
                    ffn_low[here] = low_block
                    ffn_turned[:, lane * rows : (lane + 1) * rows] = low_block.T
                    cot_low[here] = staged[COT, lane].astype(BF16)

            def events(part_of_step):
                for when in PLAN:
                    if isinstance(when, tuple) and when[0] < chunks * slots and when[1] == part_of_step:

                        @pl.when(i == when[0])
                        def _():
                            run(when)

            events(0)
            at_units = pl.ds(pl.multiple_of(j * size, 128), size)
            hidden, gate_grad, up_grad = ffn_middle(
                ffn_low[...], cot_low[...], wg[:, at_units], wu[:, at_units], wd[at_units]
            )
            events(1)
            down = across_rows(hidden, cot_low[...])
            gate = rows_dot(ffn_turned[...], gate_grad)
            up = rows_dot(ffn_turned[...], up_grad)

            grad_units = core * half_units + j * size
            grad_cols = pl.ds(pl.multiple_of(grad_units, 128), size)

            @pl.when(slot == 0)
            def _():
                gate_grads[:, grad_cols] = gate
                up_grads[:, grad_cols] = up
                down_grads[grad_cols] = down

            @pl.when(slot > 0)
            def _():
                gate_grads[:, grad_cols] += gate
                up_grads[:, grad_cols] += up
                down_grads[grad_cols] += down

            events(2)
            return 0

        lax.fori_loop(0, chunks * slots, step, 0)
        for k in range(3):
            start(("out", k))
        run((chunks * slots, 0))
        for k in range(3):
            arrived(("out", k))

    pl.run_scoped(
        second_phase,
        pltpu.VMEM((width, half_units), BF16),
        pltpu.VMEM((width, half_units), BF16),
        pltpu.VMEM((half_units, width), BF16),
        pltpu.VMEM((2, 2, rows, width), F32),
        pltpu.VMEM((2 * rows, width), BF16),
        pltpu.VMEM((width, 2 * rows), BF16),
        pltpu.VMEM((2 * rows, width), BF16),
    )
    for s in range(sz.streams):
        for h in range(half + 1):
            arrived(("cu", s, h))
            if h:
                arrived(("cd", s, h))
    for name in book:
        if name not in waited:
            made(name).wait_send()


def results_kernel(*refs):
    count = 10
    held, places, sems = refs[:count], refs[count:-1], refs[-1]
    moves = list(zip(held[:-1], places))
    first = 0
    for dst in places[count - 1 :]:
        moves.append((held[-1].at[:, pl.ds(first, dst.shape[1])], dst))
        first += dst.shape[1]
    copies = [
        pltpu.make_async_copy(src, dst, sems.at[k]) for k, (src, dst) in enumerate(moves)
    ]
    for copy in copies:
        copy.start()
    for copy in copies:
        copy.wait()


def over_groups(sz, dp_size, values):
    step = sz.group
    while step < dp_size:
        values = values + lax.ppermute(values, "dp", [(d, d ^ step) for d in range(dp_size)])
        step *= 2
    return values


def per_device(
    dp_size,
    tokens,
    segments,
    positions,
    attn_gain,
    w_query,
    key_weight,
    value_weight,
    query_gain,
    key_gain,
    w_out,
    ffn_gain,
    w_gate,
    w_up,
    w_down,
    cotangent,
):
    sz = Sizes(dp_size, tokens.shape, w_query.shape, key_weight.shape, query_gain.shape, w_gate.shape)
    rows, width, head_width, half = sz.rows, sz.width, sz.head_width, sz.half
    q_cols, k_cols = sz.q_cols, sz.k_cols
    lanes = np.arange(head_width) % (head_width // 2)
    inverse = (THETA ** (-2.0 * lanes / head_width)).astype(np.float32)[None]
    vmem = pl.BlockSpec(memory_space=pltpu.VMEM)
    anywhere = pl.BlockSpec(memory_space=pl.ANY)
    slots = 2 * half
    transfers = 124
    mixed, tokens_grad, *others = pl.pallas_call(
        functools.partial(layer_kernel, sz),
        out_shape=[
            pltpu.VMEM((rows, width), BF16),
            pltpu.VMEM((rows, width), BF16),
            pltpu.VMEM((1, width), F32),
            pltpu.VMEM((1, width), F32),
            pltpu.VMEM((1, head_width), F32),
            pltpu.VMEM((1, head_width), F32),
            pltpu.VMEM((width, sz.grad_cols), F32),
            pltpu.VMEM(w_gate.shape, F32),
            pltpu.VMEM(w_up.shape, F32),
            pltpu.VMEM(w_down.shape, F32),
            shaped(2, slots, rows, width),
            shaped(2, slots, rows, width),
        ],
        in_specs=[anywhere] * 16,
        out_specs=[vmem] * 10 + [anywhere] * 2,
        scratch_shapes=[
            pltpu.VMEM((rows, width), BF16),
            pltpu.VMEM((rows, width), BF16),
            pltpu.VMEM((1, rows), jnp.int32),
            pltpu.VMEM((1, rows), jnp.int32),
            pltpu.VMEM((1, head_width), F32),
            pltpu.VMEM((1, width), F32),
            pltpu.VMEM((1, head_width), F32),
            pltpu.VMEM((1, head_width), F32),
            pltpu.VMEM((1, width), F32),
            pltpu.VMEM((2, rows, width), F32),
            pltpu.VMEM((2, rows, width), F32),
            pltpu.VMEM((rows, width), F32),
            pltpu.VMEM((half, sz.piece, sz.grad_cols), F32),
            pltpu.VMEM((half, sz.piece, sz.grad_cols), F32),
            pltpu.VMEM((8, width), F32),
            pltpu.VMEM((8, width), F32),
            pltpu.VMEM((8, width), F32),
            pltpu.VMEM((8, width), F32),
            pltpu.VMEM((sz.chips, 8, width), F32),
            pltpu.SemaphoreType.DMA((transfers,)),
            pltpu.SemaphoreType.DMA((transfers,)),
            pltpu.SemaphoreType.DMA((32,)),
        ],
        compiler_params=pltpu.CompilerParams(
            collective_id=0, has_side_effects=True, vmem_limit_bytes=VMEM_BYTES
        ),
    )(
        tokens, cotangent, segments, positions, jnp.asarray(inverse), attn_gain[None], query_gain[None], key_gain[None],
        ffn_gain[None], w_query, key_weight, value_weight, w_out, w_gate, w_up, w_down,
    )
    sums = [over_groups(sz, dp_size, values) for values in others[:-2]]
    attn_grads = sums.pop(4)
    results = [mixed, tokens_grad, *sums, attn_grads]
    places = [shaped(*v.shape, kind=v.dtype) for v in results[:-1]]
    places += [shaped(*v.shape) for v in (w_out, w_query, key_weight, value_weight)]
    (
        mixed, tokens_grad, attn_gain_grad, ffn_gain_grad, query_gain_grad, key_gain_grad,
        w_gate_grad, w_up_grad, w_down_grad, w_out_grad, w_query_grad, w_key_grad, w_value_grad,
    ) = pl.pallas_call(
        results_kernel,
        out_shape=places,
        in_specs=[anywhere] * len(results),
        out_specs=[anywhere] * len(places),
        scratch_shapes=[pltpu.SemaphoreType.DMA((len(places),))],
        compiler_params=pltpu.CompilerParams(vmem_limit_bytes=RESULTS_VMEM_BYTES),
    )(*[pltpu.with_memory_space_constraint(values, pltpu.VMEM) for values in results])
    return (
        mixed,
        tokens_grad,
        attn_gain_grad[0],
        w_query_grad,
        w_key_grad,
        w_value_grad,
        query_gain_grad[0],
        key_gain_grad[0],
        w_out_grad,
        ffn_gain_grad[0],
        w_gate_grad,
        w_up_grad,
        w_down_grad,
    )


def solution(mesh):
    def layer(*arrays):
        return per_device(mesh.shape["dp"], *arrays)

    return jax.shard_map(
        layer,
        mesh=mesh,
        in_specs=(
            P("dp", None),
            P("dp", None),
            P("dp", None),
            P(),
            P(None, "tensor"),
            P(None, "tensor"),
            P(None, "tensor"),
            P(),
            P(),
            P("tensor", None),
            P(),
            P(None, "tensor"),
            P(None, "tensor"),
            P("tensor", None),
            P("dp", None),
        ),
        out_specs=(
            P("dp", None),
            P("dp", None),
            P(),
            P(None, "tensor"),
            P(None, "tensor"),
            P(None, "tensor"),
            P(),
            P(),
            P("tensor", None),
            P(),
            P(None, "tensor"),
            P(None, "tensor"),
            P("tensor", None),
        ),
        check_vma=False,
    )
```

```python
import functools
import math

import jax
import jax.numpy as jnp
import numpy as np
from jax import lax
from jax.experimental import pallas as pl
from jax.experimental.pallas import tpu as pltpu
from jax.sharding import PartitionSpec as P

EPS = 1e-06
THETA = 1000000.0
F32 = jnp.float32
BF16 = jnp.bfloat16
MESH = pl.DeviceIdType.MESH
VMEM_BYTES = 32 * 2**20
RESULTS_VMEM_BYTES = 2**20
GROUP = 16
COT, FFN = 0, 1
SHARES = ((2, 2, 2, 3), (4, 4, 4, 4))


PLAN = {
    "A2": [
        ("ring_half", 0),
        ("ring_half", 1),
    ],
    "A5": [
        ("start", "x", COT, 1),
    ],
    "A6": [
        ("ring", COT, 2),
    ],
    "A7": [
        ("start", "x", COT, 2),
        ("start", "x", COT, 3),
        ("start", "x", COT, 4),
        ("ring", FFN, 1),
    ],
    "A10": [
        ("x_done", COT, 1),
        ("start", "x", FFN, 1),
        ("x_done", COT, 2),
        ("start", "x", FFN, 2),
    ],
    (0, 0): [
        ("ring", COT, 3),
    ],
    (0, 1): [
        ("x_done", COT, 3),
        ("start", "x", COT, 5),
    ],
    (2, 0): [
        ("x_done", COT, 4),
        ("start", "x", COT, 6),
    ],
    (2, 1): [
        ("ring", FFN, 2),
        ("gain_sum",),
    ],
    (2, 2): [
        ("sum", 0, 1),
        ("gain", 0),
        ("sum", 1, 1),
        ("x_done", FFN, 1),
        ("start", "x", FFN, 3),
        ("stage", 1),
    ],
    (3, 0): [
        ("ring", COT, 4),
    ],
    (4, 1): [
        ("x_done", FFN, 2),
        ("start", "x", FFN, 4),
    ],
    (5, 2): [
        ("stage", 2),
    ],
    (6, 0): [
        ("ring", FFN, 3),
        ("x_done", COT, 5),
        ("start", "x", FFN, 5),
    ],
    (6, 1): [
        ("x_done", COT, 6),
        ("start", "x", FFN, 6),
    ],
    (7, 0): [
        ("sum", 0, 2),
        ("gain", 1),
    ],
    (8, 2): [
        ("sum", 1, 2),
        ("x_done", FFN, 3),
        ("start", "x", COT, 7),
        ("stage", 3),
    ],
    (9, 0): [
        ("ring", FFN, 4),
    ],
    (10, 1): [
        ("x_done", FFN, 4),
        ("start", "x", FFN, 7),
    ],
    (11, 0): [
        ("sum", 0, 3),
        ("gain", 2),
    ],
    (11, 1): [
        ("stage", 4),
    ],
    (13, 0): [
        ("sum", 1, 3),
        ("x_done", FFN, 5),
        ("start", "part", 2),
    ],
    (14, 1): [
        ("stage", 5),
    ],
    (15, 0): [
        ("sum", 0, 4),
        ("gain", 3),
    ],
    (15, 1): [
        ("x_done", FFN, 6),
        ("start", "part", 3),
    ],
    (17, 0): [
        ("stage", 6),
    ],
    (17, 1): [
        ("sum", 1, 4),
    ],
    (18, 0): [
        ("x_done", COT, 7),
    ],
    (19, 1): [
        ("gather", 0, 1),
    ],
    (20, 0): [
        ("gain", 4),
    ],
    (20, 2): [
        ("x_done", FFN, 7),
        ("gather", 1, 1),
        ("stage", 7),
    ],
    (22, 0): [
        ("gather", 0, 2),
    ],
    (24, 0): [
        ("gather", 1, 2),
        ("tokens",),
        ("gather", 0, 3),
        ("gather", 1, 3),
        ("gather", 0, 4),
        ("mixed",),
        ("gather", 1, 4),
    ],
}


def norm_factor(values):
    return lax.rsqrt(jnp.mean(values * values, axis=-1, keepdims=True) + EPS)


def norm_grad(grad_out, unit_rows, factor, scale_gain):
    scaled = grad_out * scale_gain
    return factor * (scaled - unit_rows * jnp.mean(scaled * unit_rows, axis=-1, keepdims=True))


def rows_dot(leading, trailing):
    return jnp.dot(leading, trailing, preferred_element_type=F32)


def across_rows(leading, trailing):
    return lax.dot_general(
        leading, trailing, (((0,), (0,)), ((), ())), preferred_element_type=F32
    )


def against_rows(leading, trailing):
    return lax.dot_general(
        leading, trailing, (((1,), (1,)), ((), ())), preferred_element_type=F32
    )


def ffn_middle(low_in, cot, wg, wu, wd):
    gate = rows_dot(low_in, wg)
    up = rows_dot(low_in, wu)
    sig = jax.nn.sigmoid(gate)
    silu = gate * sig
    hidden = (silu * up).astype(BF16)
    hidden_grad = against_rows(cot, wd)
    up_grad = (hidden_grad * silu).astype(BF16)
    gate_grad = (hidden_grad * up * sig * (1.0 + gate * (1.0 - sig))).astype(BF16)
    return hidden, gate_grad, up_grad


def shaped(*shape, kind=F32):
    return jax.ShapeDtypeStruct(shape, kind)


class Sizes:
    def __init__(self, dp_size, tokens, w_query, key_weight, query_gain, w_gate):
        self.rows, self.width = tokens
        self.head_width = query_gain[0]
        self.q_cols, self.k_cols = w_query[1], key_weight[1]
        self.heads, self.kv_heads = self.q_cols // self.head_width, self.k_cols // self.head_width
        self.units = w_gate[1]
        self.all_cols = self.q_cols + 2 * self.k_cols
        self.scale = 1.0 / math.sqrt(self.head_width)
        self.group = math.gcd(GROUP, dp_size)
        self.chips = self.group // 2
        self.half = self.chips // 2
        self.share = tuple(tuple(self.width * part // 8 for part in parts) for parts in SHARES)
        self.grad_rows = self.width // 2
        self.grad_cols = self.width + self.all_cols
        self.piece = self.grad_rows // self.chips
        self.streams = 2


def layer_kernel(
    sz,
    tokens_in, cot_in, segments_in, positions_in, inverse_in, attn_gain_in, query_gain_in, key_gain_in,
    ffn_gain_in,
    w_query, key_weight, value_weight, w_out, w_gate, w_up, w_down,
    mixed, tokens_grad, attn_gain_grad, ffn_gain_grad, query_gain_grad, key_gain_grad,
    attn_grads, gate_grads, up_grads, down_grads,
    mine, theirs,
    tokens, cot, segments, positions, inverse, attn_gain, query_gain, key_gain, ffn_gain,
    part, part_theirs, middle_grad, sum_up, sum_down, gain_part, gain_theirs,
    gain_send, gain_recv, gain_slots,
    send_sems, recv_sems, local_sems,
):
    rows, width, head_width = sz.rows, sz.width, sz.head_width
    q_cols, k_cols, units = sz.q_cols, sz.k_cols, sz.units
    n, half, piece = sz.chips, sz.half, sz.piece
    half_units = units // 2
    mid = rows // 2

    device = lax.axis_index("dp")
    base = device // sz.group * sz.group
    core = device % 2
    chip = device % sz.group // 2
    line = chip % 2
    place = chip // 2 + line * (2 * half - 1 - 2 * (chip // 2))
    side = lax.axis_index("tensor")

    def device_at(position):
        position = position % n
        second = position // half
        return base + (2 * (position + second * (2 * half - 1 - 2 * position)) + second) * 2 + core

    forward = {"dp": device_at(place + 1)}
    backward = {"dp": device_at(place + n - 1)}
    sibling = {"dp": base + chip * 2 + 1 - core}
    across = {"tensor": 1 - side}

    barrier = pltpu.get_barrier_semaphore()
    for neighbour in (forward, backward, sibling, across):
        pl.semaphore_signal(barrier, inc=1, device_id=neighbour, device_id_type=MESH)
    small_loads = [
        pltpu.make_async_copy(src, dst, local_sems.at[16 + k])
        for k, (src, dst) in enumerate(
            (
                (cot_in, cot),
                (tokens_in, tokens),
                (attn_gain_in, attn_gain),
                (segments_in, segments),
                (positions_in, positions),
                (inverse_in, inverse),
                (query_gain_in, query_gain),
                (key_gain_in, key_gain),
                (ffn_gain_in, ffn_gain),
            )
        )
    ]
    for load in small_loads:
        load.start()

    book = {}
    waited = set()

    send_of = {}
    before = {}

    def remote(name, src, dst, target, after=None):
        book[name] = (len(book), src, dst, target)
        if after is None:
            send_of[name] = len(set(send_of.values()))
        else:
            send_of[name], before[name] = send_of[after], after

    def made(name):
        index, src, dst, target = book[name]
        return pltpu.make_async_remote_copy(
            src_ref=src, dst_ref=dst, send_sem=send_sems.at[send_of[name]], recv_sem=recv_sems.at[index],
            device_id=target, device_id_type=MESH,
        )

    def sent(*names):
        for name in names:
            if name not in waited:
                made(name).wait_send()
                waited.add(name)

    def start(*names):
        for name in names:
            if name in before:
                sent(before[name])
            made(name).start()

    def arrived(*names):
        for name in names:
            made(name).wait_recv()

    def cols(first, count):
        return pl.ds(pl.multiple_of(first, 128), count)

    def piece_rows(index, first=0, count=piece, base_row=0):
        return pl.ds(pl.multiple_of(base_row + index % n * piece + first, 8), count)

    grad_base = core * sz.grad_rows
    slots = 2 * half
    up_slot = lambda h: 2 * h - 1
    down_slot = lambda h: 2 * h
    last = slots - 1
    up_place = lambda row, first, count: up_grads.at[pl.ds(row * rows, rows), pl.ds(first, count)]
    down_place = lambda row: down_grads.at[pl.ds(row * rows, rows)]
    half_width = width // 2
    gate_place = lambda row: gate_grads.at[pl.ds(row * rows, rows), pl.ds(units - width, width)]
    own = (gate_place(0), gate_place(1))
    in_halves = lambda a, h: a == COT and h <= 2

    def ring_names(a, h):
        count = 2 if in_halves(a, h) else 1
        return [(way, a, h, k) for k in range(count) for way in ("up", "down")]

    for a in (COT, FFN):
        for h in range(1, half + 1):
            share = sz.share[a][h - 1]
            window = cols(side * share, width - share)
            shared = cols(side * (width - share), share)
            up = own[a] if h == 1 else mine.at[a, up_slot(h - 1)]
            down = own[a] if h == 1 else mine.at[a, down_slot(h - 1)]
            first, second = pl.ds(0, mid), pl.ds(mid, mid)
            if h < half:
                for k, part_rows in enumerate((first, second) if in_halves(a, h) else (pl.ds(0, rows),)):
                    to_up = mine.at[a, up_slot(h), part_rows, window]
                    to_down = mine.at[a, down_slot(h), part_rows, window]
                    follows = None if h == 1 else h - 1
                    remote(
                        ("up", a, h, k), up.at[part_rows, window], to_up, forward,
                        follows and ("up", a, follows, k),
                    )
                    remote(
                        ("down", a, h, k), down.at[part_rows, window], to_down, backward,
                        follows and ("down", a, follows, k),
                    )
                of_distance = (up_slot(h), down_slot(h))
            else:
                remote(
                    ("up", a, h, 0), up.at[first, window], mine.at[a, last, first, window], forward,
                    ("up", a, h - 1, 0),
                )
                remote(
                    ("down", a, h, 0), down.at[second, window], mine.at[a, last, second, window],
                    backward, ("down", a, h - 1, 0),
                )
                of_distance = (last,)
            for s in of_distance:
                remote(("x", a, s), mine.at[a, s, :, shared], mine.at[a, s, :, shared], across)
        for s in range(slots):
            remote(("core", a, s), own[a] if s == 0 else mine.at[a, s], theirs.at[a, s], sibling)
    halves = (slice(0, mid), slice(mid, rows))
    for k in range(2):
        for index, at_rows in enumerate(halves):
            at_rows = pl.ds(at_rows.start, mid)
            remote(
                ("part", k, index), part.at[k, at_rows], part_theirs.at[k, at_rows], across
            )
        remote(("part", 2 + k), part.at[1 - k], part_theirs.at[k], across)
    stream_cols = sz.grad_cols // sz.streams
    small = piece // 2
    for s in range(sz.streams):
        c = pl.ds(s * stream_cols, stream_cols)
        for h in range(1, half + 1):
            size, skip = (small, small) if h == 1 else (piece, 0)
            src = attn_grads.at[piece_rows(place + half, 0, small, grad_base), c]
            remote(
                ("su", s, h), src if h == 1 else sum_up.at[h - 2, :, c],
                sum_up.at[h - 1, pl.ds(0, size), c], forward, None if h == 1 else ("su", s, h - 1),
            )
            src = attn_grads.at[piece_rows(place + half, small, small, grad_base), c]
            remote(
                ("sd", s, h), src if h == 1 else sum_down.at[h - 2, :, c],
                sum_down.at[h - 1, pl.ds(skip, size), c], backward, None if h == 1 else ("sd", s, h - 1),
            )
        own_piece = attn_grads.at[piece_rows(place, 0, piece, grad_base), c]
        remote(("cu", s, 0), own_piece, own_piece, sibling)
        for h in range(1, half + 1):
            size, skip = (small, small) if h == half else (piece, 0)
            going_up = attn_grads.at[piece_rows(place + n - h + 1, 0, size, grad_base), c]
            going_down = attn_grads.at[piece_rows(place + h - 1, skip, size, grad_base), c]
            follows = (("su", s, half), ("sd", s, half)) if h == 1 else (("gu", s, h - 1), ("gd", s, h - 1))
            remote(("gu", s, h), going_up, going_up, forward, follows[0])
            remote(("gd", s, h), going_down, going_down, backward, follows[1])
            got_up = attn_grads.at[piece_rows(place + n - h, 0, size, grad_base), c]
            got_down = attn_grads.at[piece_rows(place + h, skip, size, grad_base), c]
            remote(("cu", s, h), got_up, got_up, sibling, ("cu", s, h - 1))
            remote(("cd", s, h), got_down, got_down, sibling, None if h == 1 else ("cd", s, h - 1))
    remote("gain_parts", gain_part, gain_theirs, across)
    remote("gains", gain_send, gain_recv, sibling)
    for h in range(1, half + 1):
        slot = gain_slots.at[(place + n - h + 1) % n]
        remote(("vu", h), slot, slot, forward, None if h == 1 else ("vu", h - 1))
        if h < half:
            slot = gain_slots.at[(place + h - 1) % n]
            remote(("vd", h), slot, slot, backward, None if h == 1 else ("vd", h - 1))

    def ring_step(a, h):
        arrived(*ring_names(a, h))
        if h < half:
            start(*ring_names(a, h + 1))

    def ring_half(k):
        arrived(("up", COT, 1, k), ("down", COT, 1, k))
        start(("up", COT, 2, k), ("down", COT, 2, k))

    def x_start(a, s):
        start(("x", a, s))

    def x_done(a, s):
        arrived(("x", a, s))
        start(("core", a, s))


    def stream(s):
        return pl.ds(s * stream_cols, stream_cols)

    def sum_step(s, h):
        arrived(("su", s, h), ("sd", s, h))
        c = stream(s)
        up_rows = piece_rows(place + half - h, 0, piece, grad_base)
        down_rows = piece_rows(place + n - half + h, 0, piece, grad_base)
        if h == 1:
            sent(("su", s, 1), ("sd", s, 1))
            up, down = attn_grads[up_rows, c], attn_grads[down_rows, c]
            sum_up[0, :small, c] += up[:small]
            sum_up[0, small:, c] = up[small:]
            sum_down[0, :small, c] = down[:small]
            sum_down[0, small:, c] += down[small:]
        elif h < half:
            sum_up[h - 1, :, c] += attn_grads[up_rows, c]
            sum_down[h - 1, :, c] += attn_grads[down_rows, c]
        if h < half:
            start(("su", s, h + 1), ("sd", s, h + 1))
        else:
            own_rows = piece_rows(place, 0, piece, grad_base)
            attn_grads[own_rows, c] += sum_up[h - 1, :, c] + sum_down[h - 1, :, c]
            start(("gu", s, 1), ("gd", s, 1), ("cu", s, 0))

    def gather_step(s, h):
        arrived(("gu", s, h), ("gd", s, h))
        if h < half:
            start(("gu", s, h + 1), ("gd", s, h + 1))
        start(("cu", s, h), ("cd", s, h))

    def finish_tokens():
        arrived(("part", 2))
        grad = part[1] + part_theirs[0]
        value = tokens[...].astype(F32)
        factor = norm_factor(value)
        unit = value * factor
        tokens_grad[...] = (
            middle_grad[...] + norm_grad(grad, unit, factor, attn_gain[...])
        ).astype(BF16)

    def finish_mixed():
        arrived(("part", 3))
        mixed[...] = (part[0] + part_theirs[1]).astype(BF16)

    def gain_sum():
        arrived("gain_parts")
        gain_send[...] = gain_part[...] + gain_theirs[...]
        start("gains")

    def gain_first():
        arrived("gains")
        gain_slots[place] = gain_send[...] + gain_recv[...]
        start(("vu", 1), ("vd", 1))

    def gain_step(h):
        arrived(("vu", h))
        if h < half:
            arrived(("vd", h))
            start(("vu", h + 1))
            if h + 1 < half:
                start(("vd", h + 1))
        else:
            total = gain_slots[0]
            for chip_at in range(1, n):
                total = total + gain_slots[chip_at]
            attn_gain_grad[...] = total[0:1, :]
            ffn_gain_grad[...] = total[1:2, :]
            query_gain_grad[...] = total[2:3, :head_width]
            key_gain_grad[...] = total[2:3, head_width : 2 * head_width]

    def stage(slot):
        arrived(("core", COT, slot), ("core", FFN, slot))
        for copy in stage_copies(slot, False):
            copy.start()

    scoped = {}

    def stage_copies(slot, first):
        staged = scoped["staged"]
        copies = []
        for a in (COT, FFN):
            src = own[a] if first else mine.at[a, slot]
            copies.append(pltpu.make_async_copy(src, staged.at[a, 0], local_sems.at[9 + 2 * a]))
            copies.append(
                pltpu.make_async_copy(theirs.at[a, slot], staged.at[a, 1], local_sems.at[10 + 2 * a])
            )
        return copies

    def gain_event(h):
        if h == 0:
            gain_first()
        else:
            gain_step(h)

    actions = {
        "ring": ring_step,
        "ring_half": ring_half,
        "start": lambda *name: start(name),
        "x_done": x_done,
        "sum": sum_step,
        "gather": gather_step,
        "stage": stage,
        "gain_sum": gain_sum,
        "tokens": finish_tokens,
        "gain": gain_event,
        "mixed": finish_mixed,
    }

    def run(when):
        for event in PLAN.get(when, ()):
            actions[event[0]](*event[1:])

    group = q_cols // k_cols
    other_half = lambda count: cols((1 - core) * count, count)
    own_half = lambda count: cols(core * count, count)

    block = k_cols
    q_blocks, unit_blocks = q_cols // block, units // block
    at_k, at_v, at_o = q_blocks, q_blocks + 1, q_blocks + 2

    half_down = down_grads.at[pl.ds(pl.multiple_of(core * half_units, 8), half_units)]
    outs = (gate_grads.at[:, own_half(half_units)], up_grads.at[:, own_half(half_units)], half_down)
    for k, out in enumerate(outs):
        remote(("out", k), out, out, sibling)

    q_lin, k_lin = up_place(0, 0, q_cols), up_place(0, q_cols, k_cols)
    ctx_send, ctx_recv = up_place(1, 0, q_cols // 2), up_place(1, q_cols // 2, q_cols // 2)
    cosine, sine = up_place(1, q_cols, head_width), up_place(1, q_cols + head_width, head_width)
    attn_send, attn_recv = up_place(2, 0, half_width), up_place(2, half_width, half_width)
    mask = up_place(3, 0, rows)
    lows, low_recvs = (down_place(0), down_place(1)), (down_place(2), down_place(3))
    branch, branch_recv = down_place(4), down_place(5)
    deep = width // rows
    middle = gate_place(2)

    def probs_of(head):
        return gate_grads.at[pl.ds(head % deep * rows, rows), pl.ds(head // deep * rows, rows)]

    remote("ctx", ctx_send, ctx_recv, sibling)
    remote("attn", attn_send, attn_recv, sibling)
    remote("branch", branch, branch_recv, sibling)
    for k in range(2):
        remote(("low", k), lows[k], low_recvs[k], sibling)

    def first_phase(
        bank, wd, q_low, k_low, v_low, context, ffn_low, hidden, context_grad, attn_low, branch_low
    ):
        def load(src, dst, index):
            copy = pltpu.make_async_copy(src, dst, local_sems.at[index])
            copy.start()
            return copy

        def block_of(weights, index):
            return weights.at[:, pl.ds(index * block, block)]

        def load_projections():
            order = [(w_query, i) for i in range(q_blocks)] + [(key_weight, 0), (value_weight, 0)]
            return [load(block_of(w, i), bank.at[k], k) for k, (w, i) in enumerate(order)]

        def load_out():
            count = width // block
            return [load(block_of(w_out, i), bank.at[at_o + i], at_o + i) for i in range(count)]

        def load_ffn():
            order = [(w, i) for w in (w_gate, w_up) for i in range(unit_blocks)]
            return [load(block_of(w, i), bank.at[k], k) for k, (w, i) in enumerate(order)]

        loads = load_projections()

        def head_norm(lin, gain):
            return lin * norm_factor(lin) * gain[...]

        def turned(lin, gain, at_rows):
            normed = head_norm(lin, gain)
            swapped = pltpu.roll(normed, head_width // 2, 1)
            return (normed * cosine[at_rows] + swapped * sine[at_rows]).astype(BF16)

        def turned_back(grad, lin, gain):
            back = grad * cosine[...] - pltpu.roll(grad, head_width // 2, 1) * sine[...]
            factor = norm_factor(lin)
            unit = lin * factor
            return (
                norm_grad(back, unit, factor, gain[...]).astype(BF16),
                jnp.sum(back * unit, axis=0, keepdims=True),
            )

        small_loads[0].wait()
        own[COT][...] = cot[...].astype(F32)
        pl.semaphore_wait(barrier, 4)
        start(*ring_names(COT, 1), ("core", COT, 0))

        for small in small_loads[1:]:
            small.wait()
        resid = tokens[...].astype(F32)
        attn_in = (resid * norm_factor(resid) * attn_gain[...]).astype(BF16)
        attn_low[...] = attn_in
        attn_send[...] = attn_low[:, other_half(width // 2)].astype(F32)
        start("attn")

        def down_rows(row):
            return jnp.broadcast_to(row.astype(F32), (head_width, rows)).T

        segment_rows = jnp.concatenate([down_rows(segments[...])] * (rows // head_width), 1)
        same = segment_rows == jnp.broadcast_to(segments[...].astype(F32), (rows, rows))
        row_at = lax.broadcasted_iota(jnp.int32, (rows, rows), 0)
        column_at = lax.broadcasted_iota(jnp.int32, (rows, rows), 1)
        mask[...] = jnp.where(same & (row_at >= column_at), 1.0, 0.0)
        angles = down_rows(positions[...]) * inverse[...]
        lane = lax.broadcasted_iota(jnp.int32, (rows, head_width), 1)
        cosine[...] = jnp.cos(angles)
        sine[...] = jnp.where(lane < head_width // 2, -1.0, 1.0) * jnp.sin(angles)
        for i in range(q_blocks):
            loads[i].wait()
            q_lin[:, i * block : (i + 1) * block] = rows_dot(attn_in, bank[i])
        loads[at_k].wait()
        k_lin[...] = rows_dot(attn_in, bank[at_k])
        loads[at_v].wait()
        v_low[...] = rows_dot(attn_in, bank[at_v]).astype(BF16)
        loads += load_out()
        run("A1")
        for kv in range(sz.kv_heads):
            kv_at = slice(kv * head_width, (kv + 1) * head_width)
            k_low[:, kv_at] = turned(k_lin[:, kv_at], key_gain, slice(0, rows))
        for index, at_rows in enumerate(halves):
            seen = at_rows.stop
            for head in range(sz.heads):
                at = slice(head * head_width, (head + 1) * head_width)
                kv_at = slice(head // group * head_width, (head // group + 1) * head_width)
                queries = turned(q_lin[at_rows, at], query_gain, at_rows)
                q_low[at_rows, at] = queries
                scores = against_rows(queries, k_low[:seen, kv_at]) * sz.scale
                scores = jnp.where(mask[at_rows, :seen] > 0, scores, -1e30)
                raised = jnp.exp(scores - jnp.max(scores, axis=-1, keepdims=True))
                prob = raised / jnp.sum(raised, axis=-1, keepdims=True)
                place_of = probs_of(head)
                place_of[at_rows, :seen] = prob
                if seen < rows:
                    place_of[at_rows, seen:] = jnp.zeros((mid, rows - seen), F32)
                context[at_rows, at] = rows_dot(prob.astype(BF16), v_low[:seen, kv_at]).astype(BF16)
            for i in range(width // block):
                if index == 0:
                    loads[at_o + i].wait()
                at = slice(i * block, (i + 1) * block)
                part[0, at_rows, at] = rows_dot(context[at_rows], bank[at_o + i])
            start(("part", 0, index))
        ctx_send[...] = context[:, other_half(q_cols // 2)].astype(F32)
        start("ctx")
        loads = load_ffn()
        down_load = load(w_down, wd, 15)
        for index, at_rows in enumerate(halves):
            run("A2" if index == 0 else "A3")
            arrived(("part", 0, index))
            value = tokens[at_rows].astype(F32) + (part[0, at_rows] + part_theirs[0, at_rows])
            middle[at_rows] = value
            low_rows = (value * norm_factor(value) * ffn_gain[...]).astype(BF16)
            ffn_low[at_rows] = low_rows
            own[FFN][at_rows] = low_rows.astype(F32)
            if index == 0:
                down_load.wait()
                for load_of in loads:
                    load_of.wait()
            else:
                start(*ring_names(FFN, 1), ("core", FFN, 0))
                run("A4")
            for i in range(unit_blocks):
                at = slice(i * block, (i + 1) * block)
                wg, wu = bank[i], bank[unit_blocks + i]
                low_hidden, gate_grad, up_grad = ffn_middle(low_rows, cot[at_rows], wg, wu, wd[at])
                hidden[at_rows, at] = low_hidden
                term = against_rows(gate_grad, wg) + against_rows(up_grad, wu)
                if i == 0:
                    part[1, at_rows] = term
                else:
                    part[1, at_rows] += term
            start(("part", 1, index))
        loads = load_projections() + load_out()
        run("A5")
        sent(("part", 0, 0), ("part", 0, 1))
        part[0] = rows_dot(hidden[...], wd[...]) + 0.5 * middle[...]

        for index, at_rows in enumerate(halves):
            run("A6" if index == 0 else "A7")
            arrived(("part", 1, index))
            grad = part[1, at_rows] + part_theirs[1, at_rows]
            value = middle[at_rows]
            factor = norm_factor(value)
            unit = value * factor
            total = cot[at_rows].astype(F32) + norm_grad(grad, unit, factor, ffn_gain[...])
            middle_grad[at_rows] = total
            branch_low[at_rows] = total.astype(BF16)
            branch[at_rows] = total.astype(BF16).astype(F32)
            gain_term = jnp.sum(grad * unit, axis=0, keepdims=True)
            gain_part[1:2, :] = gain_term if index == 0 else 0.5 * (gain_part[1:2, :] + gain_term)
        start("branch")
        run("A8")
        for load_of in loads:
            load_of.wait()
        context_grad[...] = sum(
            against_rows(branch_low[:, i * block : (i + 1) * block], bank[at_o + i])
            for i in range(width // block)
        ).astype(BF16)
        q_total = jnp.zeros((1, head_width), F32)
        k_total = jnp.zeros((1, head_width), F32)
        for kv in range(sz.kv_heads):
            kv_at = slice(kv * head_width, (kv + 1) * head_width)
            keys, values = k_low[:, kv_at], v_low[:, kv_at]
            keys_grad = values_grad = 0.0
            for member in range(group):
                head = kv * group + member
                at = slice(head * head_width, (head + 1) * head_width)
                head_grad = context_grad[:, at]
                prob = probs_of(head)[...]
                prob_grad = against_rows(head_grad, values)
                values_grad += across_rows(prob.astype(BF16), head_grad)
                inner = jnp.sum(prob * prob_grad, axis=-1, keepdims=True)
                score_grad = (prob * (prob_grad - inner)).astype(BF16)
                queries_grad = rows_dot(score_grad, keys) * sz.scale
                keys_grad += across_rows(score_grad, q_low[:, at])
                head_low, head_total = turned_back(queries_grad, q_lin[:, at], query_gain)
                lows[0][:, at] = head_low.astype(F32)
                q_total += head_total
            head_low, head_total = turned_back(keys_grad * sz.scale, k_lin[:, kv_at], key_gain)
            k_total += head_total
            lows[1][:, kv_at] = head_low.astype(F32)
            at = k_cols + kv * head_width
            lows[1][:, at : at + head_width] = values_grad.astype(BF16).astype(F32)
        start(("low", 0), ("low", 1))
        run("A9")
        half_rows = pl.ds(pl.multiple_of(grad_base, 8), sz.grad_rows)
        arrived("ctx", "branch")
        for i in range(width // block):
            at = slice(i * block, (i + 1) * block)
            attn_grads[half_rows, at] = across_rows(
                context[:, own_half(q_cols // 2)], branch[:, at].astype(BF16)
            ) + across_rows(ctx_recv[...].astype(BF16), branch_recv[:, at].astype(BF16))
        arrived("attn", ("low", 0), ("low", 1))
        for k in range(2):
            for i in range(width // block):
                at = slice(i * block, (i + 1) * block)
                first = (k + 1) * width + i * block
                attn_grads[half_rows, first : first + block] = across_rows(
                    attn_low[:, own_half(width // 2)], lows[k][:, at].astype(BF16)
                ) + across_rows(attn_recv[...].astype(BF16), low_recvs[k][:, at].astype(BF16))
        for s in range(sz.streams):
            start(("su", s, 1), ("sd", s, 1))
        sent(("part", 1, 0), ("part", 1, 1))
        part[1] = sum(
            against_rows(
                lows[i // q_blocks][:, i % q_blocks * block : (i % q_blocks + 1) * block].astype(BF16),
                bank[i],
            )
            for i in range(at_o)
        )
        value = tokens[...].astype(F32)
        unit = value * norm_factor(value)
        gain_part[0:1, :] = jnp.sum(part[1] * unit, axis=0, keepdims=True)
        gain_part[2:, :] = jnp.zeros((6, width), F32)
        gain_part[2:3, :head_width] = q_total
        gain_part[2:3, head_width : 2 * head_width] = k_total
        start("gain_parts")
        run("A10")
        sent("ctx", "attn", "branch", ("low", 0), ("low", 1))

    pl.run_scoped(
        first_phase,
        pltpu.VMEM((max(at_o + width // block, 2 * unit_blocks), width, block), BF16),
        pltpu.VMEM(w_down.shape, BF16),
        pltpu.VMEM((rows, q_cols), BF16),
        pltpu.VMEM((rows, k_cols), BF16),
        pltpu.VMEM((rows, k_cols), BF16),
        pltpu.VMEM((rows, q_cols), BF16),
        pltpu.VMEM((rows, width), BF16),
        pltpu.VMEM((rows, units), BF16),
        pltpu.VMEM((rows, q_cols), BF16),
        pltpu.VMEM((rows, width), BF16),
        pltpu.VMEM((rows, width), BF16),
    )

    def second_phase(
        wg, wu, wd, staged, ffn_low, ffn_turned, cot_low
    ):
        scoped["staged"] = staged
        weight_loads = [
            pltpu.make_async_copy(src, dst, local_sems.at[i])
            for i, (src, dst) in enumerate(
                (
                    (w_gate.at[:, own_half(half_units)], wg),
                    (w_up.at[:, own_half(half_units)], wu),
                    (w_down.at[pl.ds(pl.multiple_of(core * half_units, 8), half_units)], wd),
                )
            )
        ]
        for load in weight_loads:
            load.start()

        for a in (COT, FFN):
            sent(*ring_names(a, 1), ("core", a, 0))
        arrived(("core", COT, 0), ("core", FFN, 0))
        for copy in stage_copies(0, True):
            copy.start()
        for load in weight_loads:
            load.wait()
        chunks = 3
        size = half_units // chunks
        def step(i, _):
            slot, j = i // chunks, i % chunks

            @pl.when(j == 0)
            def _():
                for copy in stage_copies(slot, False):
                    copy.wait()
                for lane in range(2):
                    here = pl.ds(lane * rows, rows)
                    low_block = staged[FFN, lane].astype(BF16)
                    ffn_low[here] = low_block
                    ffn_turned[:, lane * rows : (lane + 1) * rows] = low_block.T
                    cot_low[here] = staged[COT, lane].astype(BF16)

            def events(part_of_step):
                for when in PLAN:
                    if isinstance(when, tuple) and when[0] < chunks * slots and when[1] == part_of_step:

                        @pl.when(i == when[0])
                        def _():
                            run(when)

            events(0)
            at_units = pl.ds(pl.multiple_of(j * size, 128), size)
            hidden, gate_grad, up_grad = ffn_middle(
                ffn_low[...], cot_low[...], wg[:, at_units], wu[:, at_units], wd[at_units]
            )
            events(1)
            down = across_rows(hidden, cot_low[...])
            gate = rows_dot(ffn_turned[...], gate_grad)
            up = rows_dot(ffn_turned[...], up_grad)

            grad_units = core * half_units + j * size
            grad_cols = pl.ds(pl.multiple_of(grad_units, 128), size)

            @pl.when(slot == 0)
            def _():
                gate_grads[:, grad_cols] = gate
                up_grads[:, grad_cols] = up
                down_grads[grad_cols] = down

            @pl.when(slot > 0)
            def _():
                gate_grads[:, grad_cols] += gate
                up_grads[:, grad_cols] += up
                down_grads[grad_cols] += down

            events(2)
            return 0

        lax.fori_loop(0, chunks * slots, step, 0)
        for k in range(3):
            start(("out", k))
        run((chunks * slots, 0))
        for k in range(3):
            arrived(("out", k))

    pl.run_scoped(
        second_phase,
        pltpu.VMEM((width, half_units), BF16),
        pltpu.VMEM((width, half_units), BF16),
        pltpu.VMEM((half_units, width), BF16),
        pltpu.VMEM((2, 2, rows, width), F32),
        pltpu.VMEM((2 * rows, width), BF16),
        pltpu.VMEM((width, 2 * rows), BF16),
        pltpu.VMEM((2 * rows, width), BF16),
    )
    for s in range(sz.streams):
        for h in range(half + 1):
            arrived(("cu", s, h))
            if h:
                arrived(("cd", s, h))
    for name in book:
        if name not in waited:
            made(name).wait_send()


def results_kernel(*refs):
    count = 10
    held, places, sems = refs[:count], refs[count:-1], refs[-1]
    moves = list(zip(held[:-1], places))
    first = 0
    for dst in places[count - 1 :]:
        moves.append((held[-1].at[:, pl.ds(first, dst.shape[1])], dst))
        first += dst.shape[1]
    copies = [
        pltpu.make_async_copy(src, dst, sems.at[k]) for k, (src, dst) in enumerate(moves)
    ]
    for copy in copies:
        copy.start()
    for copy in copies:
        copy.wait()


def over_groups(sz, dp_size, values):
    step = sz.group
    while step < dp_size:
        values = values + lax.ppermute(values, "dp", [(d, d ^ step) for d in range(dp_size)])
        step *= 2
    return values


def per_device(
    dp_size,
    tokens,
    segments,
    positions,
    attn_gain,
    w_query,
    key_weight,
    value_weight,
    query_gain,
    key_gain,
    w_out,
    ffn_gain,
    w_gate,
    w_up,
    w_down,
    cotangent,
):
    sz = Sizes(dp_size, tokens.shape, w_query.shape, key_weight.shape, query_gain.shape, w_gate.shape)
    rows, width, head_width, half = sz.rows, sz.width, sz.head_width, sz.half
    q_cols, k_cols = sz.q_cols, sz.k_cols
    lanes = np.arange(head_width) % (head_width // 2)
    inverse = (THETA ** (-2.0 * lanes / head_width)).astype(np.float32)[None]
    vmem = pl.BlockSpec(memory_space=pltpu.VMEM)
    anywhere = pl.BlockSpec(memory_space=pl.ANY)
    slots = 2 * half
    transfers, sends = 123, 62
    mixed, tokens_grad, *others = pl.pallas_call(
        functools.partial(layer_kernel, sz),
        out_shape=[
            pltpu.VMEM((rows, width), BF16),
            pltpu.VMEM((rows, width), BF16),
            pltpu.VMEM((1, width), F32),
            pltpu.VMEM((1, width), F32),
            pltpu.VMEM((1, head_width), F32),
            pltpu.VMEM((1, head_width), F32),
            pltpu.VMEM((width, sz.grad_cols), F32),
            pltpu.VMEM(w_gate.shape, F32),
            pltpu.VMEM(w_up.shape, F32),
            pltpu.VMEM(w_down.shape, F32),
            shaped(2, slots, rows, width),
            shaped(2, slots, rows, width),
        ],
        in_specs=[anywhere] * 16,
        out_specs=[vmem] * 10 + [anywhere] * 2,
        scratch_shapes=[
            pltpu.VMEM((rows, width), BF16),
            pltpu.VMEM((rows, width), BF16),
            pltpu.VMEM((1, rows), jnp.int32),
            pltpu.VMEM((1, rows), jnp.int32),
            pltpu.VMEM((1, head_width), F32),
            pltpu.VMEM((1, width), F32),
            pltpu.VMEM((1, head_width), F32),
            pltpu.VMEM((1, head_width), F32),
            pltpu.VMEM((1, width), F32),
            pltpu.VMEM((2, rows, width), F32),
            pltpu.VMEM((2, rows, width), F32),
            pltpu.VMEM((rows, width), F32),
            pltpu.VMEM((half, sz.piece, sz.grad_cols), F32),
            pltpu.VMEM((half, sz.piece, sz.grad_cols), F32),
            pltpu.VMEM((8, width), F32),
            pltpu.VMEM((8, width), F32),
            pltpu.VMEM((8, width), F32),
            pltpu.VMEM((8, width), F32),
            pltpu.VMEM((sz.chips, 8, width), F32),
            pltpu.SemaphoreType.DMA((sends,)),
            pltpu.SemaphoreType.DMA((transfers,)),
            pltpu.SemaphoreType.DMA((25,)),
        ],
        compiler_params=pltpu.CompilerParams(
            collective_id=0, has_side_effects=True, vmem_limit_bytes=VMEM_BYTES
        ),
    )(
        tokens, cotangent, segments, positions, jnp.asarray(inverse), attn_gain[None], query_gain[None], key_gain[None],
        ffn_gain[None], w_query, key_weight, value_weight, w_out, w_gate, w_up, w_down,
    )
    sums = [over_groups(sz, dp_size, values) for values in others[:-2]]
    attn_grads = sums.pop(4)
    results = [mixed, tokens_grad, *sums, attn_grads]
    places = [shaped(*v.shape, kind=v.dtype) for v in results[:-1]]
    places += [shaped(*v.shape) for v in (w_out, w_query, key_weight, value_weight)]
    (
        mixed, tokens_grad, attn_gain_grad, ffn_gain_grad, query_gain_grad, key_gain_grad,
        w_gate_grad, w_up_grad, w_down_grad, w_out_grad, w_query_grad, w_key_grad, w_value_grad,
    ) = pl.pallas_call(
        results_kernel,
        out_shape=places,
        in_specs=[anywhere] * len(results),
        out_specs=[anywhere] * len(places),
        scratch_shapes=[pltpu.SemaphoreType.DMA((len(places),))],
        compiler_params=pltpu.CompilerParams(vmem_limit_bytes=RESULTS_VMEM_BYTES),
    )(*[pltpu.with_memory_space_constraint(values, pltpu.VMEM) for values in results])
    return (
        mixed,
        tokens_grad,
        attn_gain_grad[0],
        w_query_grad,
        w_key_grad,
        w_value_grad,
        query_gain_grad[0],
        key_gain_grad[0],
        w_out_grad,
        ffn_gain_grad[0],
        w_gate_grad,
        w_up_grad,
        w_down_grad,
    )


def solution(mesh):
    def layer(*arrays):
        return per_device(mesh.shape["dp"], *arrays)

    return jax.shard_map(
        layer,
        mesh=mesh,
        in_specs=(
            P("dp", None),
            P("dp", None),
            P("dp", None),
            P(),
            P(None, "tensor"),
            P(None, "tensor"),
            P(None, "tensor"),
            P(),
            P(),
            P("tensor", None),
            P(),
            P(None, "tensor"),
            P(None, "tensor"),
            P("tensor", None),
            P("dp", None),
        ),
        out_specs=(
            P("dp", None),
            P("dp", None),
            P(),
            P(None, "tensor"),
            P(None, "tensor"),
            P(None, "tensor"),
            P(),
            P(),
            P("tensor", None),
            P(),
            P(None, "tensor"),
            P(None, "tensor"),
            P("tensor", None),
        ),
        check_vma=False,
    )
```

```python
import functools
import math

import jax
import jax.numpy as jnp
import numpy as np
from jax import lax
from jax.experimental import pallas as pl
from jax.experimental.pallas import tpu as pltpu
from jax.sharding import PartitionSpec as P

EPS = 1e-06
THETA = 1000000.0
F32 = jnp.float32
BF16 = jnp.bfloat16
MESH = pl.DeviceIdType.MESH
VMEM_BYTES = 32 * 2**20
RESULTS_VMEM_BYTES = 2**20
GROUP = 16
COT, FFN = 0, 1
SHARES = ((2, 2, 2, 3), (4, 4, 4, 4))


PLAN = {
    "A2": [
        ("ring_half", 0),
        ("ring_half", 1),
    ],
    "A5": [
        ("start", "x", COT, 1),
    ],
    "A6": [
        ("ring", COT, 2),
    ],
    "A7": [
        ("start", "x", COT, 2),
        ("start", "x", COT, 3),
        ("start", "x", COT, 4),
        ("ring", FFN, 1),
    ],
    "A10": [
        ("x_done", COT, 1),
        ("start", "x", FFN, 1),
        ("x_done", COT, 2),
        ("start", "x", FFN, 2),
    ],
    (0, 0): [
        ("ring", COT, 3),
    ],
    (0, 1): [
        ("x_done", COT, 3),
        ("start", "x", COT, 5),
    ],
    (2, 0): [
        ("x_done", COT, 4),
        ("start", "x", COT, 6),
    ],
    (2, 1): [
        ("ring", FFN, 2),
        ("gain_sum",),
    ],
    (2, 2): [
        ("sum", 0, 1),
        ("gain", 0),
        ("sum", 1, 1),
        ("x_done", FFN, 1),
        ("start", "x", FFN, 3),
        ("stage", 1),
    ],
    (3, 0): [
        ("ring", COT, 4),
    ],
    (4, 1): [
        ("x_done", FFN, 2),
        ("start", "x", FFN, 4),
    ],
    (5, 2): [
        ("stage", 2),
    ],
    (6, 0): [
        ("ring", FFN, 3),
        ("x_done", COT, 5),
        ("start", "x", FFN, 5),
    ],
    (6, 1): [
        ("x_done", COT, 6),
        ("start", "x", FFN, 6),
    ],
    (7, 0): [
        ("sum", 0, 2),
        ("gain", 1),
    ],
    (8, 2): [
        ("sum", 1, 2),
        ("x_done", FFN, 3),
        ("start", "x", COT, 7),
        ("stage", 3),
    ],
    (9, 0): [
        ("ring", FFN, 4),
    ],
    (10, 1): [
        ("x_done", FFN, 4),
        ("start", "x", FFN, 7),
    ],
    (11, 0): [
        ("sum", 0, 3),
        ("gain", 2),
    ],
    (11, 1): [
        ("stage", 4),
    ],
    (13, 0): [
        ("sum", 1, 3),
        ("x_done", FFN, 5),
        ("start", "part", 2),
    ],
    (14, 1): [
        ("stage", 5),
    ],
    (15, 0): [
        ("sum", 0, 4),
        ("gain", 3),
    ],
    (15, 1): [
        ("x_done", FFN, 6),
        ("start", "part", 3),
    ],
    (17, 0): [
        ("stage", 6),
    ],
    (17, 1): [
        ("sum", 1, 4),
    ],
    (18, 0): [
        ("x_done", COT, 7),
    ],
    (19, 1): [
        ("gather", 0, 1),
    ],
    (20, 0): [
        ("gain", 4),
    ],
    (20, 2): [
        ("x_done", FFN, 7),
        ("gather", 1, 1),
        ("stage", 7),
    ],
    (22, 0): [
        ("gather", 0, 2),
    ],
    (24, 0): [
        ("gather", 1, 2),
        ("tokens",),
        ("gather", 0, 3),
        ("gather", 1, 3),
        ("gather", 0, 4),
        ("mixed",),
        ("gather", 1, 4),
    ],
}


def norm_factor(values):
    return lax.rsqrt(jnp.mean(values * values, axis=-1, keepdims=True) + EPS)


def norm_grad(grad_out, unit_rows, factor, scale_gain):
    scaled = grad_out * scale_gain
    return factor * (scaled - unit_rows * jnp.mean(scaled * unit_rows, axis=-1, keepdims=True))


def rows_dot(leading, trailing):
    return jnp.dot(leading, trailing, preferred_element_type=F32)


def across_rows(leading, trailing):
    return lax.dot_general(
        leading, trailing, (((0,), (0,)), ((), ())), preferred_element_type=F32
    )


def against_rows(leading, trailing):
    return lax.dot_general(
        leading, trailing, (((1,), (1,)), ((), ())), preferred_element_type=F32
    )


def ffn_middle(low_in, cot, wg, wu, wd):
    gate = rows_dot(low_in, wg)
    up = rows_dot(low_in, wu)
    sig = jax.nn.sigmoid(gate)
    silu = gate * sig
    hidden = (silu * up).astype(BF16)
    hidden_grad = against_rows(cot, wd)
    up_grad = (hidden_grad * silu).astype(BF16)
    gate_grad = (hidden_grad * up * sig * (1.0 + gate * (1.0 - sig))).astype(BF16)
    return hidden, gate_grad, up_grad


def shaped(*shape, kind=F32):
    return jax.ShapeDtypeStruct(shape, kind)


class Sizes:
    def __init__(self, dp_size, tokens, w_query, key_weight, query_gain, w_gate):
        self.rows, self.width = tokens
        self.head_width = query_gain[0]
        self.q_cols, self.k_cols = w_query[1], key_weight[1]
        self.heads, self.kv_heads = self.q_cols // self.head_width, self.k_cols // self.head_width
        self.units = w_gate[1]
        self.all_cols = self.q_cols + 2 * self.k_cols
        self.scale = 1.0 / math.sqrt(self.head_width)
        self.group = math.gcd(GROUP, dp_size)
        self.chips = self.group // 2
        self.half = self.chips // 2
        self.share = tuple(tuple(self.width * part // 8 for part in parts) for parts in SHARES)
        self.grad_rows = self.width // 2
        self.grad_cols = self.width + self.all_cols
        self.piece = self.grad_rows // self.chips
        self.streams = 2


def layer_kernel(
    sz,
    tokens_in, cot_in, segments_in, positions_in, inverse_in, attn_gain_in, query_gain_in, key_gain_in,
    ffn_gain_in,
    w_query, key_weight, value_weight, w_out, w_gate, w_up, w_down,
    mixed, tokens_grad, attn_gain_grad, ffn_gain_grad, query_gain_grad, key_gain_grad,
    attn_grads, gate_grads, up_grads, down_grads,
    mine, theirs,
    tokens, cot, segments, positions, inverse, attn_gain, query_gain, key_gain, ffn_gain,
    part, part_theirs, middle_grad, sum_up, sum_down, gain_part, gain_theirs,
    gain_send, gain_recv, gain_slots,
    send_sems, recv_sems, local_sems,
):
    rows, width, head_width = sz.rows, sz.width, sz.head_width
    q_cols, k_cols, units = sz.q_cols, sz.k_cols, sz.units
    n, half, piece = sz.chips, sz.half, sz.piece
    half_units = units // 2
    mid = rows // 2

    device = lax.axis_index("dp")
    base = device // sz.group * sz.group
    core = device % 2
    chip = device % sz.group // 2
    line = chip % 2
    place = chip // 2 + line * (2 * half - 1 - 2 * (chip // 2))
    side = lax.axis_index("tensor")

    def device_at(position):
        position = position % n
        second = position // half
        return base + (2 * (position + second * (2 * half - 1 - 2 * position)) + second) * 2 + core

    forward = {"dp": device_at(place + 1)}
    backward = {"dp": device_at(place + n - 1)}
    sibling = {"dp": base + chip * 2 + 1 - core}
    across = {"tensor": 1 - side}

    barrier = pltpu.get_barrier_semaphore()
    for neighbour in (forward, backward, sibling, across):
        pl.semaphore_signal(barrier, inc=1, device_id=neighbour, device_id_type=MESH)
    small_loads = [
        pltpu.make_async_copy(src, dst, local_sems.at[16 + k])
        for k, (src, dst) in enumerate(
            (
                (cot_in, cot),
                (tokens_in, tokens),
                (attn_gain_in, attn_gain),
                (segments_in, segments),
                (positions_in, positions),
                (inverse_in, inverse),
                (query_gain_in, query_gain),
                (key_gain_in, key_gain),
                (ffn_gain_in, ffn_gain),
            )
        )
    ]
    for load in small_loads:
        load.start()

    book = {}
    waited = set()

    send_of = {}
    before = {}

    def remote(name, src, dst, target, after=None):
        book[name] = (len(book), src, dst, target)
        if after is None:
            send_of[name] = len(set(send_of.values()))
        else:
            send_of[name], before[name] = send_of[after], after

    def made(name):
        index, src, dst, target = book[name]
        return pltpu.make_async_remote_copy(
            src_ref=src, dst_ref=dst, send_sem=send_sems.at[send_of[name]], recv_sem=recv_sems.at[index],
            device_id=target, device_id_type=MESH,
        )

    def sent(*names):
        for name in names:
            if name not in waited:
                made(name).wait_send()
                waited.add(name)

    def start(*names):
        for name in names:
            if name in before:
                sent(before[name])
            made(name).start()

    def arrived(*names):
        for name in names:
            made(name).wait_recv()

    def cols(first, count):
        return pl.ds(pl.multiple_of(first, 128), count)

    def piece_rows(index, first=0, count=piece, base_row=0):
        return pl.ds(pl.multiple_of(base_row + index % n * piece + first, 8), count)

    grad_base = core * sz.grad_rows
    slots = 2 * half
    up_slot = lambda h: 2 * h - 1
    down_slot = lambda h: 2 * h
    last = slots - 1
    up_place = lambda row, first, count: up_grads.at[pl.ds(row * rows, rows), pl.ds(first, count)]
    down_place = lambda row: down_grads.at[pl.ds(row * rows, rows)]
    half_width = width // 2
    gate_place = lambda row: gate_grads.at[pl.ds(row * rows, rows), pl.ds(units - width, width)]
    own = (gate_place(0), gate_place(1))
    in_halves = lambda a, h: a == COT and h <= 2

    def ring_names(a, h):
        count = 2 if in_halves(a, h) else 1
        return [(way, a, h, k) for k in range(count) for way in ("up", "down")]

    phase = sorted((when for when in PLAN if isinstance(when, str)), key=lambda when: int(when[1:]))
    steps = sorted(when for when in PLAN if isinstance(when, tuple))
    passed = [e[1:] for when in (*phase, *steps) for e in PLAN[when] if e[0] == "x_done"]
    follows_block = dict(zip(passed[2:], passed))

    for a in (COT, FFN):
        for h in range(1, half + 1):
            share = sz.share[a][h - 1]
            window = cols(side * share, width - share)
            shared = cols(side * (width - share), share)
            up = own[a] if h == 1 else mine.at[a, up_slot(h - 1)]
            down = own[a] if h == 1 else mine.at[a, down_slot(h - 1)]
            first, second = pl.ds(0, mid), pl.ds(mid, mid)
            if h < half:
                for k, part_rows in enumerate((first, second) if in_halves(a, h) else (pl.ds(0, rows),)):
                    to_up = mine.at[a, up_slot(h), part_rows, window]
                    to_down = mine.at[a, down_slot(h), part_rows, window]
                    follows = None if h == 1 else h - 1
                    remote(
                        ("up", a, h, k), up.at[part_rows, window], to_up, forward,
                        follows and ("up", a, follows, k),
                    )
                    remote(
                        ("down", a, h, k), down.at[part_rows, window], to_down, backward,
                        follows and ("down", a, follows, k),
                    )
                of_distance = (up_slot(h), down_slot(h))
            else:
                remote(
                    ("up", a, h, 0), up.at[first, window], mine.at[a, last, first, window], forward,
                    ("up", a, h - 1, 0),
                )
                remote(
                    ("down", a, h, 0), down.at[second, window], mine.at[a, last, second, window],
                    backward, ("down", a, h - 1, 0),
                )
                of_distance = (last,)
            for s in of_distance:
                remote(("x", a, s), mine.at[a, s, :, shared], mine.at[a, s, :, shared], across)
    for a, s in [(COT, 0), (FFN, 0), *passed]:
        last_but_one = follows_block.get((a, s))
        remote(
            ("core", a, s), own[a] if s == 0 else mine.at[a, s], theirs.at[a, s], sibling,
            last_but_one and ("core", *last_but_one),
        )
    halves = (slice(0, mid), slice(mid, rows))
    for k in range(2):
        for index, at_rows in enumerate(halves):
            at_rows = pl.ds(at_rows.start, mid)
            remote(
                ("part", k, index), part.at[k, at_rows], part_theirs.at[k, at_rows], across
            )
        remote(("part", 2 + k), part.at[1 - k], part_theirs.at[k], across)
    stream_cols = sz.grad_cols // sz.streams
    small = piece // 2
    for s in range(sz.streams):
        c = pl.ds(s * stream_cols, stream_cols)
        for h in range(1, half + 1):
            size, skip = (small, small) if h == 1 else (piece, 0)
            src = attn_grads.at[piece_rows(place + half, 0, small, grad_base), c]
            remote(
                ("su", s, h), src if h == 1 else sum_up.at[h - 2, :, c],
                sum_up.at[h - 1, pl.ds(0, size), c], forward, None if h == 1 else ("su", s, h - 1),
            )
            src = attn_grads.at[piece_rows(place + half, small, small, grad_base), c]
            remote(
                ("sd", s, h), src if h == 1 else sum_down.at[h - 2, :, c],
                sum_down.at[h - 1, pl.ds(skip, size), c], backward, None if h == 1 else ("sd", s, h - 1),
            )
        own_piece = attn_grads.at[piece_rows(place, 0, piece, grad_base), c]
        remote(("cu", s, 0), own_piece, own_piece, sibling)
        for h in range(1, half + 1):
            size, skip = (small, small) if h == half else (piece, 0)
            going_up = attn_grads.at[piece_rows(place + n - h + 1, 0, size, grad_base), c]
            going_down = attn_grads.at[piece_rows(place + h - 1, skip, size, grad_base), c]
            follows = (("su", s, half), ("sd", s, half)) if h == 1 else (("gu", s, h - 1), ("gd", s, h - 1))
            remote(("gu", s, h), going_up, going_up, forward, follows[0])
            remote(("gd", s, h), going_down, going_down, backward, follows[1])
            got_up = attn_grads.at[piece_rows(place + n - h, 0, size, grad_base), c]
            got_down = attn_grads.at[piece_rows(place + h, skip, size, grad_base), c]
            remote(("cu", s, h), got_up, got_up, sibling, ("cu", s, h - 1))
            remote(("cd", s, h), got_down, got_down, sibling, None if h == 1 else ("cd", s, h - 1))
    remote("gain_parts", gain_part, gain_theirs, across)
    remote("gains", gain_send, gain_recv, sibling)
    for h in range(1, half + 1):
        slot = gain_slots.at[(place + n - h + 1) % n]
        remote(("vu", h), slot, slot, forward, None if h == 1 else ("vu", h - 1))
        if h < half:
            slot = gain_slots.at[(place + h - 1) % n]
            remote(("vd", h), slot, slot, backward, None if h == 1 else ("vd", h - 1))

    def ring_step(a, h):
        arrived(*ring_names(a, h))
        if h < half:
            start(*ring_names(a, h + 1))

    def ring_half(k):
        arrived(("up", COT, 1, k), ("down", COT, 1, k))
        start(("up", COT, 2, k), ("down", COT, 2, k))

    def x_start(a, s):
        start(("x", a, s))

    def x_done(a, s):
        arrived(("x", a, s))
        start(("core", a, s))


    def stream(s):
        return pl.ds(s * stream_cols, stream_cols)

    def sum_step(s, h):
        arrived(("su", s, h), ("sd", s, h))
        c = stream(s)
        up_rows = piece_rows(place + half - h, 0, piece, grad_base)
        down_rows = piece_rows(place + n - half + h, 0, piece, grad_base)
        if h == 1:
            sent(("su", s, 1), ("sd", s, 1))
            up, down = attn_grads[up_rows, c], attn_grads[down_rows, c]
            sum_up[0, :small, c] += up[:small]
            sum_up[0, small:, c] = up[small:]
            sum_down[0, :small, c] = down[:small]
            sum_down[0, small:, c] += down[small:]
        elif h < half:
            sum_up[h - 1, :, c] += attn_grads[up_rows, c]
            sum_down[h - 1, :, c] += attn_grads[down_rows, c]
        if h < half:
            start(("su", s, h + 1), ("sd", s, h + 1))
        else:
            own_rows = piece_rows(place, 0, piece, grad_base)
            attn_grads[own_rows, c] += sum_up[h - 1, :, c] + sum_down[h - 1, :, c]
            start(("gu", s, 1), ("gd", s, 1), ("cu", s, 0))

    def gather_step(s, h):
        arrived(("gu", s, h), ("gd", s, h))
        if h < half:
            start(("gu", s, h + 1), ("gd", s, h + 1))
        start(("cu", s, h), ("cd", s, h))

    def finish_tokens():
        arrived(("part", 2))
        grad = part[1] + part_theirs[0]
        value = tokens[...].astype(F32)
        factor = norm_factor(value)
        unit = value * factor
        tokens_grad[...] = (
            middle_grad[...] + norm_grad(grad, unit, factor, attn_gain[...])
        ).astype(BF16)

    def finish_mixed():
        arrived(("part", 3))
        mixed[...] = (part[0] + part_theirs[1]).astype(BF16)

    def gain_sum():
        arrived("gain_parts")
        gain_send[...] = gain_part[...] + gain_theirs[...]
        start("gains")

    def gain_first():
        arrived("gains")
        gain_slots[place] = gain_send[...] + gain_recv[...]
        start(("vu", 1), ("vd", 1))

    def gain_step(h):
        arrived(("vu", h))
        if h < half:
            arrived(("vd", h))
            start(("vu", h + 1))
            if h + 1 < half:
                start(("vd", h + 1))
        else:
            total = gain_slots[0]
            for chip_at in range(1, n):
                total = total + gain_slots[chip_at]
            attn_gain_grad[...] = total[0:1, :]
            ffn_gain_grad[...] = total[1:2, :]
            query_gain_grad[...] = total[2:3, :head_width]
            key_gain_grad[...] = total[2:3, head_width : 2 * head_width]

    def stage(slot):
        arrived(("core", COT, slot), ("core", FFN, slot))
        for copy in stage_copies(slot, False):
            copy.start()

    scoped = {}

    def stage_copies(slot, first):
        staged = scoped["staged"]
        copies = []
        for a in (COT, FFN):
            src = own[a] if first else mine.at[a, slot]
            copies.append(pltpu.make_async_copy(src, staged.at[a, 0], local_sems.at[9 + 2 * a]))
            copies.append(
                pltpu.make_async_copy(theirs.at[a, slot], staged.at[a, 1], local_sems.at[10 + 2 * a])
            )
        return copies

    def gain_event(h):
        if h == 0:
            gain_first()
        else:
            gain_step(h)

    actions = {
        "ring": ring_step,
        "ring_half": ring_half,
        "start": lambda *name: start(name),
        "x_done": x_done,
        "sum": sum_step,
        "gather": gather_step,
        "stage": stage,
        "gain_sum": gain_sum,
        "tokens": finish_tokens,
        "gain": gain_event,
        "mixed": finish_mixed,
    }

    def run(when):
        for event in PLAN.get(when, ()):
            actions[event[0]](*event[1:])

    group = q_cols // k_cols
    other_half = lambda count: cols((1 - core) * count, count)
    own_half = lambda count: cols(core * count, count)

    block = k_cols
    q_blocks, unit_blocks = q_cols // block, units // block
    at_k, at_v, at_o = q_blocks, q_blocks + 1, q_blocks + 2

    half_down = down_grads.at[pl.ds(pl.multiple_of(core * half_units, 8), half_units)]
    outs = (gate_grads.at[:, own_half(half_units)], up_grads.at[:, own_half(half_units)], half_down)
    for k, out in enumerate(outs):
        remote(("out", k), out, out, sibling)

    q_lin, k_lin = up_place(0, 0, q_cols), up_place(0, q_cols, k_cols)
    ctx_send, ctx_recv = up_place(1, 0, q_cols // 2), up_place(1, q_cols // 2, q_cols // 2)
    cosine, sine = up_place(1, q_cols, head_width), up_place(1, q_cols + head_width, head_width)
    attn_send, attn_recv = up_place(2, 0, half_width), up_place(2, half_width, half_width)
    mask = up_place(3, 0, rows)
    lows, low_recvs = (down_place(0), down_place(1)), (down_place(2), down_place(3))
    branch, branch_recv = down_place(4), down_place(5)
    deep = width // rows
    middle = gate_place(2)

    def probs_of(head):
        return gate_grads.at[pl.ds(head % deep * rows, rows), pl.ds(head // deep * rows, rows)]

    remote("ctx", ctx_send, ctx_recv, sibling)
    remote("attn", attn_send, attn_recv, sibling)
    remote("branch", branch, branch_recv, sibling)
    for k in range(2):
        remote(("low", k), lows[k], low_recvs[k], sibling)

    def first_phase(
        bank, wd, q_low, k_low, v_low, context, ffn_low, hidden, context_grad, attn_low, branch_low
    ):
        def load(src, dst, index):
            copy = pltpu.make_async_copy(src, dst, local_sems.at[index])
            copy.start()
            return copy

        def block_of(weights, index):
            return weights.at[:, pl.ds(index * block, block)]

        def load_projections():
            order = [(w_query, i) for i in range(q_blocks)] + [(key_weight, 0), (value_weight, 0)]
            return [load(block_of(w, i), bank.at[k], k) for k, (w, i) in enumerate(order)]

        def load_out():
            count = width // block
            return [load(block_of(w_out, i), bank.at[at_o + i], at_o + i) for i in range(count)]

        def load_ffn():
            order = [(w, i) for w in (w_gate, w_up) for i in range(unit_blocks)]
            return [load(block_of(w, i), bank.at[k], k) for k, (w, i) in enumerate(order)]

        loads = load_projections()

        def head_norm(lin, gain):
            return lin * norm_factor(lin) * gain[...]

        def turned(lin, gain, at_rows):
            normed = head_norm(lin, gain)
            swapped = pltpu.roll(normed, head_width // 2, 1)
            return (normed * cosine[at_rows] + swapped * sine[at_rows]).astype(BF16)

        def turned_back(grad, lin, gain):
            back = grad * cosine[...] - pltpu.roll(grad, head_width // 2, 1) * sine[...]
            factor = norm_factor(lin)
            unit = lin * factor
            return (
                norm_grad(back, unit, factor, gain[...]).astype(BF16),
                jnp.sum(back * unit, axis=0, keepdims=True),
            )

        small_loads[0].wait()
        own[COT][...] = cot[...].astype(F32)
        pl.semaphore_wait(barrier, 4)
        start(*ring_names(COT, 1), ("core", COT, 0))

        for small in small_loads[1:]:
            small.wait()
        resid = tokens[...].astype(F32)
        attn_in = (resid * norm_factor(resid) * attn_gain[...]).astype(BF16)
        attn_low[...] = attn_in
        attn_send[...] = attn_low[:, other_half(width // 2)].astype(F32)
        start("attn")

        def down_rows(row):
            return jnp.broadcast_to(row.astype(F32), (head_width, rows)).T

        segment_rows = jnp.concatenate([down_rows(segments[...])] * (rows // head_width), 1)
        same = segment_rows == jnp.broadcast_to(segments[...].astype(F32), (rows, rows))
        row_at = lax.broadcasted_iota(jnp.int32, (rows, rows), 0)
        column_at = lax.broadcasted_iota(jnp.int32, (rows, rows), 1)
        mask[...] = jnp.where(same & (row_at >= column_at), 1.0, 0.0)
        angles = down_rows(positions[...]) * inverse[...]
        lane = lax.broadcasted_iota(jnp.int32, (rows, head_width), 1)
        cosine[...] = jnp.cos(angles)
        sine[...] = jnp.where(lane < head_width // 2, -1.0, 1.0) * jnp.sin(angles)
        for i in range(q_blocks):
            loads[i].wait()
            q_lin[:, i * block : (i + 1) * block] = rows_dot(attn_in, bank[i])
        loads[at_k].wait()
        k_lin[...] = rows_dot(attn_in, bank[at_k])
        loads[at_v].wait()
        v_low[...] = rows_dot(attn_in, bank[at_v]).astype(BF16)
        loads += load_out()
        run("A1")
        for kv in range(sz.kv_heads):
            kv_at = slice(kv * head_width, (kv + 1) * head_width)
            k_low[:, kv_at] = turned(k_lin[:, kv_at], key_gain, slice(0, rows))
        for index, at_rows in enumerate(halves):
            seen = at_rows.stop
            for head in range(sz.heads):
                at = slice(head * head_width, (head + 1) * head_width)
                kv_at = slice(head // group * head_width, (head // group + 1) * head_width)
                queries = turned(q_lin[at_rows, at], query_gain, at_rows)
                q_low[at_rows, at] = queries
                scores = against_rows(queries, k_low[:seen, kv_at]) * sz.scale
                scores = jnp.where(mask[at_rows, :seen] > 0, scores, -1e30)
                raised = jnp.exp(scores - jnp.max(scores, axis=-1, keepdims=True))
                prob = raised / jnp.sum(raised, axis=-1, keepdims=True)
                place_of = probs_of(head)
                place_of[at_rows, :seen] = prob
                if seen < rows:
                    place_of[at_rows, seen:] = jnp.zeros((mid, rows - seen), F32)
                context[at_rows, at] = rows_dot(prob.astype(BF16), v_low[:seen, kv_at]).astype(BF16)
            for i in range(width // block):
                if index == 0:
                    loads[at_o + i].wait()
                at = slice(i * block, (i + 1) * block)
                part[0, at_rows, at] = rows_dot(context[at_rows], bank[at_o + i])
            start(("part", 0, index))
        ctx_send[...] = context[:, other_half(q_cols // 2)].astype(F32)
        start("ctx")
        loads = load_ffn()
        down_load = load(w_down, wd, 15)
        for index, at_rows in enumerate(halves):
            run("A2" if index == 0 else "A3")
            arrived(("part", 0, index))
            value = tokens[at_rows].astype(F32) + (part[0, at_rows] + part_theirs[0, at_rows])
            middle[at_rows] = value
            low_rows = (value * norm_factor(value) * ffn_gain[...]).astype(BF16)
            ffn_low[at_rows] = low_rows
            own[FFN][at_rows] = low_rows.astype(F32)
            if index == 0:
                down_load.wait()
                for load_of in loads:
                    load_of.wait()
            else:
                start(*ring_names(FFN, 1), ("core", FFN, 0))
                run("A4")
            for i in range(unit_blocks):
                at = slice(i * block, (i + 1) * block)
                wg, wu = bank[i], bank[unit_blocks + i]
                low_hidden, gate_grad, up_grad = ffn_middle(low_rows, cot[at_rows], wg, wu, wd[at])
                hidden[at_rows, at] = low_hidden
                term = against_rows(gate_grad, wg) + against_rows(up_grad, wu)
                if i == 0:
                    part[1, at_rows] = term
                else:
                    part[1, at_rows] += term
            start(("part", 1, index))
        loads = load_projections() + load_out()
        run("A5")
        sent(("part", 0, 0), ("part", 0, 1))
        part[0] = rows_dot(hidden[...], wd[...]) + 0.5 * middle[...]

        for index, at_rows in enumerate(halves):
            run("A6" if index == 0 else "A7")
            arrived(("part", 1, index))
            grad = part[1, at_rows] + part_theirs[1, at_rows]
            value = middle[at_rows]
            factor = norm_factor(value)
            unit = value * factor
            total = cot[at_rows].astype(F32) + norm_grad(grad, unit, factor, ffn_gain[...])
            middle_grad[at_rows] = total
            branch_low[at_rows] = total.astype(BF16)
            branch[at_rows] = total.astype(BF16).astype(F32)
            gain_term = jnp.sum(grad * unit, axis=0, keepdims=True)
            gain_part[1:2, :] = gain_term if index == 0 else 0.5 * (gain_part[1:2, :] + gain_term)
        start("branch")
        run("A8")
        for load_of in loads:
            load_of.wait()
        context_grad[...] = sum(
            against_rows(branch_low[:, i * block : (i + 1) * block], bank[at_o + i])
            for i in range(width // block)
        ).astype(BF16)
        q_total = jnp.zeros((1, head_width), F32)
        k_total = jnp.zeros((1, head_width), F32)
        for kv in range(sz.kv_heads):
            kv_at = slice(kv * head_width, (kv + 1) * head_width)
            keys, values = k_low[:, kv_at], v_low[:, kv_at]
            keys_grad = values_grad = 0.0
            for member in range(group):
                head = kv * group + member
                at = slice(head * head_width, (head + 1) * head_width)
                head_grad = context_grad[:, at]
                prob = probs_of(head)[...]
                prob_grad = against_rows(head_grad, values)
                values_grad += across_rows(prob.astype(BF16), head_grad)
                inner = jnp.sum(prob * prob_grad, axis=-1, keepdims=True)
                score_grad = (prob * (prob_grad - inner)).astype(BF16)
                queries_grad = rows_dot(score_grad, keys) * sz.scale
                keys_grad += across_rows(score_grad, q_low[:, at])
                head_low, head_total = turned_back(queries_grad, q_lin[:, at], query_gain)
                lows[0][:, at] = head_low.astype(F32)
                q_total += head_total
            head_low, head_total = turned_back(keys_grad * sz.scale, k_lin[:, kv_at], key_gain)
            k_total += head_total
            lows[1][:, kv_at] = head_low.astype(F32)
            at = k_cols + kv * head_width
            lows[1][:, at : at + head_width] = values_grad.astype(BF16).astype(F32)
        start(("low", 0), ("low", 1))
        run("A9")
        half_rows = pl.ds(pl.multiple_of(grad_base, 8), sz.grad_rows)
        arrived("ctx", "branch")
        for i in range(width // block):
            at = slice(i * block, (i + 1) * block)
            attn_grads[half_rows, at] = across_rows(
                context[:, own_half(q_cols // 2)], branch[:, at].astype(BF16)
            ) + across_rows(ctx_recv[...].astype(BF16), branch_recv[:, at].astype(BF16))
        arrived("attn", ("low", 0), ("low", 1))
        for k in range(2):
            for i in range(width // block):
                at = slice(i * block, (i + 1) * block)
                first = (k + 1) * width + i * block
                attn_grads[half_rows, first : first + block] = across_rows(
                    attn_low[:, own_half(width // 2)], lows[k][:, at].astype(BF16)
                ) + across_rows(attn_recv[...].astype(BF16), low_recvs[k][:, at].astype(BF16))
        for s in range(sz.streams):
            start(("su", s, 1), ("sd", s, 1))
        sent(("part", 1, 0), ("part", 1, 1))
        part[1] = sum(
            against_rows(
                lows[i // q_blocks][:, i % q_blocks * block : (i % q_blocks + 1) * block].astype(BF16),
                bank[i],
            )
            for i in range(at_o)
        )
        value = tokens[...].astype(F32)
        unit = value * norm_factor(value)
        gain_part[0:1, :] = jnp.sum(part[1] * unit, axis=0, keepdims=True)
        gain_part[2:, :] = jnp.zeros((6, width), F32)
        gain_part[2:3, :head_width] = q_total
        gain_part[2:3, head_width : 2 * head_width] = k_total
        start("gain_parts")
        run("A10")
        sent("ctx", "attn", "branch", ("low", 0), ("low", 1))

    pl.run_scoped(
        first_phase,
        pltpu.VMEM((max(at_o + width // block, 2 * unit_blocks), width, block), BF16),
        pltpu.VMEM(w_down.shape, BF16),
        pltpu.VMEM((rows, q_cols), BF16),
        pltpu.VMEM((rows, k_cols), BF16),
        pltpu.VMEM((rows, k_cols), BF16),
        pltpu.VMEM((rows, q_cols), BF16),
        pltpu.VMEM((rows, width), BF16),
        pltpu.VMEM((rows, units), BF16),
        pltpu.VMEM((rows, q_cols), BF16),
        pltpu.VMEM((rows, width), BF16),
        pltpu.VMEM((rows, width), BF16),
    )

    def second_phase(
        wg, wu, wd, staged, ffn_low, ffn_turned, cot_low
    ):
        scoped["staged"] = staged
        weight_loads = [
            pltpu.make_async_copy(src, dst, local_sems.at[i])
            for i, (src, dst) in enumerate(
                (
                    (w_gate.at[:, own_half(half_units)], wg),
                    (w_up.at[:, own_half(half_units)], wu),
                    (w_down.at[pl.ds(pl.multiple_of(core * half_units, 8), half_units)], wd),
                )
            )
        ]
        for load in weight_loads:
            load.start()

        for a in (COT, FFN):
            sent(*ring_names(a, 1), ("core", a, 0))
        arrived(("core", COT, 0), ("core", FFN, 0))
        for copy in stage_copies(0, True):
            copy.start()
        for load in weight_loads:
            load.wait()
        chunks = 3
        size = half_units // chunks
        def step(i, _):
            slot, j = i // chunks, i % chunks

            @pl.when(j == 0)
            def _():
                for copy in stage_copies(slot, False):
                    copy.wait()
                for lane in range(2):
                    here = pl.ds(lane * rows, rows)
                    low_block = staged[FFN, lane].astype(BF16)
                    ffn_low[here] = low_block
                    ffn_turned[:, lane * rows : (lane + 1) * rows] = low_block.T
                    cot_low[here] = staged[COT, lane].astype(BF16)

            def events(part_of_step):
                for when in PLAN:
                    if isinstance(when, tuple) and when[0] < chunks * slots and when[1] == part_of_step:

                        @pl.when(i == when[0])
                        def _():
                            run(when)

            events(0)
            at_units = pl.ds(pl.multiple_of(j * size, 128), size)
            hidden, gate_grad, up_grad = ffn_middle(
                ffn_low[...], cot_low[...], wg[:, at_units], wu[:, at_units], wd[at_units]
            )
            events(1)
            down = across_rows(hidden, cot_low[...])
            gate = rows_dot(ffn_turned[...], gate_grad)
            up = rows_dot(ffn_turned[...], up_grad)

            grad_units = core * half_units + j * size
            grad_cols = pl.ds(pl.multiple_of(grad_units, 128), size)

            @pl.when(slot == 0)
            def _():
                gate_grads[:, grad_cols] = gate
                up_grads[:, grad_cols] = up
                down_grads[grad_cols] = down

            @pl.when(slot > 0)
            def _():
                gate_grads[:, grad_cols] += gate
                up_grads[:, grad_cols] += up
                down_grads[grad_cols] += down

            events(2)
            return 0

        lax.fori_loop(0, chunks * slots, step, 0)
        for k in range(3):
            start(("out", k))
        run((chunks * slots, 0))
        for k in range(3):
            arrived(("out", k))

    pl.run_scoped(
        second_phase,
        pltpu.VMEM((width, half_units), BF16),
        pltpu.VMEM((width, half_units), BF16),
        pltpu.VMEM((half_units, width), BF16),
        pltpu.VMEM((2, 2, rows, width), F32),
        pltpu.VMEM((2 * rows, width), BF16),
        pltpu.VMEM((width, 2 * rows), BF16),
        pltpu.VMEM((2 * rows, width), BF16),
    )
    for s in range(sz.streams):
        for h in range(half + 1):
            arrived(("cu", s, h))
            if h:
                arrived(("cd", s, h))
    for name in book:
        if name not in waited:
            made(name).wait_send()


def results_kernel(*refs):
    count = 10
    held, places, sems = refs[:count], refs[count:-1], refs[-1]
    moves = list(zip(held[:-1], places))
    first = 0
    for dst in places[count - 1 :]:
        moves.append((held[-1].at[:, pl.ds(first, dst.shape[1])], dst))
        first += dst.shape[1]
    copies = [
        pltpu.make_async_copy(src, dst, sems.at[k]) for k, (src, dst) in enumerate(moves)
    ]
    for copy in copies:
        copy.start()
    for copy in copies:
        copy.wait()


def over_groups(sz, dp_size, values):
    step = sz.group
    while step < dp_size:
        values = values + lax.ppermute(values, "dp", [(d, d ^ step) for d in range(dp_size)])
        step *= 2
    return values


def per_device(
    dp_size,
    tokens,
    segments,
    positions,
    attn_gain,
    w_query,
    key_weight,
    value_weight,
    query_gain,
    key_gain,
    w_out,
    ffn_gain,
    w_gate,
    w_up,
    w_down,
    cotangent,
):
    sz = Sizes(dp_size, tokens.shape, w_query.shape, key_weight.shape, query_gain.shape, w_gate.shape)
    rows, width, head_width, half = sz.rows, sz.width, sz.head_width, sz.half
    q_cols, k_cols = sz.q_cols, sz.k_cols
    lanes = np.arange(head_width) % (head_width // 2)
    inverse = (THETA ** (-2.0 * lanes / head_width)).astype(np.float32)[None]
    vmem = pl.BlockSpec(memory_space=pltpu.VMEM)
    anywhere = pl.BlockSpec(memory_space=pl.ANY)
    slots = 2 * half
    transfers, sends = 123, 50
    mixed, tokens_grad, *others = pl.pallas_call(
        functools.partial(layer_kernel, sz),
        out_shape=[
            pltpu.VMEM((rows, width), BF16),
            pltpu.VMEM((rows, width), BF16),
            pltpu.VMEM((1, width), F32),
            pltpu.VMEM((1, width), F32),
            pltpu.VMEM((1, head_width), F32),
            pltpu.VMEM((1, head_width), F32),
            pltpu.VMEM((width, sz.grad_cols), F32),
            pltpu.VMEM(w_gate.shape, F32),
            pltpu.VMEM(w_up.shape, F32),
            pltpu.VMEM(w_down.shape, F32),
            shaped(2, slots, rows, width),
            shaped(2, slots, rows, width),
        ],
        in_specs=[anywhere] * 16,
        out_specs=[vmem] * 10 + [anywhere] * 2,
        scratch_shapes=[
            pltpu.VMEM((rows, width), BF16),
            pltpu.VMEM((rows, width), BF16),
            pltpu.VMEM((1, rows), jnp.int32),
            pltpu.VMEM((1, rows), jnp.int32),
            pltpu.VMEM((1, head_width), F32),
            pltpu.VMEM((1, width), F32),
            pltpu.VMEM((1, head_width), F32),
            pltpu.VMEM((1, head_width), F32),
            pltpu.VMEM((1, width), F32),
            pltpu.VMEM((2, rows, width), F32),
            pltpu.VMEM((2, rows, width), F32),
            pltpu.VMEM((rows, width), F32),
            pltpu.VMEM((half, sz.piece, sz.grad_cols), F32),
            pltpu.VMEM((half, sz.piece, sz.grad_cols), F32),
            pltpu.VMEM((8, width), F32),
            pltpu.VMEM((8, width), F32),
            pltpu.VMEM((8, width), F32),
            pltpu.VMEM((8, width), F32),
            pltpu.VMEM((sz.chips, 8, width), F32),
            pltpu.SemaphoreType.DMA((sends,)),
            pltpu.SemaphoreType.DMA((transfers,)),
            pltpu.SemaphoreType.DMA((25,)),
        ],
        compiler_params=pltpu.CompilerParams(
            collective_id=0, has_side_effects=True, vmem_limit_bytes=VMEM_BYTES
        ),
    )(
        tokens, cotangent, segments, positions, jnp.asarray(inverse), attn_gain[None], query_gain[None], key_gain[None],
        ffn_gain[None], w_query, key_weight, value_weight, w_out, w_gate, w_up, w_down,
    )
    sums = [over_groups(sz, dp_size, values) for values in others[:-2]]
    attn_grads = sums.pop(4)
    results = [mixed, tokens_grad, *sums, attn_grads]
    places = [shaped(*v.shape, kind=v.dtype) for v in results[:-1]]
    places += [shaped(*v.shape) for v in (w_out, w_query, key_weight, value_weight)]
    (
        mixed, tokens_grad, attn_gain_grad, ffn_gain_grad, query_gain_grad, key_gain_grad,
        w_gate_grad, w_up_grad, w_down_grad, w_out_grad, w_query_grad, w_key_grad, w_value_grad,
    ) = pl.pallas_call(
        results_kernel,
        out_shape=places,
        in_specs=[anywhere] * len(results),
        out_specs=[anywhere] * len(places),
        scratch_shapes=[pltpu.SemaphoreType.DMA((len(places),))],
        compiler_params=pltpu.CompilerParams(vmem_limit_bytes=RESULTS_VMEM_BYTES),
    )(*[pltpu.with_memory_space_constraint(values, pltpu.VMEM) for values in results])
    return (
        mixed,
        tokens_grad,
        attn_gain_grad[0],
        w_query_grad,
        w_key_grad,
        w_value_grad,
        query_gain_grad[0],
        key_gain_grad[0],
        w_out_grad,
        ffn_gain_grad[0],
        w_gate_grad,
        w_up_grad,
        w_down_grad,
    )


def solution(mesh):
    def layer(*arrays):
        return per_device(mesh.shape["dp"], *arrays)

    return jax.shard_map(
        layer,
        mesh=mesh,
        in_specs=(
            P("dp", None),
            P("dp", None),
            P("dp", None),
            P(),
            P(None, "tensor"),
            P(None, "tensor"),
            P(None, "tensor"),
            P(),
            P(),
            P("tensor", None),
            P(),
            P(None, "tensor"),
            P(None, "tensor"),
            P("tensor", None),
            P("dp", None),
        ),
        out_specs=(
            P("dp", None),
            P("dp", None),
            P(),
            P(None, "tensor"),
            P(None, "tensor"),
            P(None, "tensor"),
            P(),
            P(),
            P("tensor", None),
            P(),
            P(None, "tensor"),
            P(None, "tensor"),
            P("tensor", None),
        ),
        check_vma=False,
    )
```
